32 devices in a mesh: ctx: 8 (over y, x, core), fsdp: 4 (over z).
Axes of the slice: x: 2, y: 2, z: 4, core: 2. Of those that a mesh axis runs over, the one named last changes fastest.
Arguments:
- layer_input: bfloat16 [4, 2048, 576], P('fsdp', 'ctx'), may hold values from -6 to 6
- slot_table: int32 [8], replicated, may hold values from 0 to 7, each once
- seq_ids: int32 [4, 2048], P('fsdp'), may hold values from 0 to 3, as said below
- w_query: bfloat16 [576, 576], P('fsdp'), may hold values from -0.5 to 0.5
- w_key: bfloat16 [576, 192], P('fsdp'), may hold values from -0.25 to 0.25
- w_value: bfloat16 [576, 192], P('fsdp'), may hold values from -0.25 to 0.25
- w_out: bfloat16 [576, 576], P('fsdp'), may hold values from -3 to 3
- w_gate: bfloat16 [576, 1536], P('fsdp'), may hold values from -0.25 to 0.25
- w_up: bfloat16 [576, 1536], P('fsdp'), may hold values from -0.25 to 0.25
- w_down: bfloat16 [1536, 576], P('fsdp'), may hold values from -0.15625 to 0.15625
- attn_gain: bfloat16 [576], P('fsdp'), may hold values from 0.5 to 1.5
- ffn_gain: bfloat16 [576], P('fsdp'), may hold values from 0.5 to 1.5
- cotangent: bfloat16 [4, 2048, 576], P('fsdp', 'ctx'), may hold values from -6 to 6
Outputs:
- output: bfloat16 [4, 2048, 576], P('fsdp', 'ctx')
- grad_input: bfloat16 [4, 2048, 576], P('fsdp', 'ctx')
- grad_wq: float32 [576, 576], P('fsdp')
- grad_wk: float32 [576, 192], P('fsdp')
- grad_wv: float32 [576, 192], P('fsdp')
- grad_wo: float32 [576, 576], P('fsdp')
- grad_w_gate: float32 [576, 1536], P('fsdp')
- grad_w_up: float32 [576, 1536], P('fsdp')
- grad_w_down: float32 [1536, 576], P('fsdp')
- grad_attn_gain: float32 [576], P('fsdp')
- grad_ffn_gain: float32 [576], P('fsdp')
The draws below stay inside these ranges and needn't reach their ends.
Inputs may be any that keep to these rules, and one draw needn't show every extreme that they name: A permutation: context slot c holds blocks slot_table[c] and 15 - slot_table[c] of every sequence. `seq_ids`: never falls along natural positions; in each sequence one document starts at the first position or ends at the last and covers at least 1152 positions.
All inputs are finite; a program needn't handle non-finite values.
Results may differ from the reference program's by a relative error of at most 0.024.
Values may be sent and summed in bfloat16 or wider, within the bound.
No kernel may reach another device: no remote copies, remote signals or barrier semaphores. Data moves between devices by JAX's collectives and lax.ppermute only.
A program may use at most 128 MiB of HBM per device.

```python
import math
import jax
import jax.numpy as jnp
from jax import lax

D = 576
HEADS = 9
KV_HEADS = 3
HEAD = 64
FF = 1536
BLK = 128
DOCS = 4
LENGTH = 2048
N_CTX = 8
N_FSDP = 4


def draw_seq_ids(key, part):
    key = jax.random.fold_in(key, 11)
    subkeys = jax.random.split(key, 3)
    positions = jnp.arange(LENGTH, dtype=jnp.int32)
    long_length = LENGTH // 2 + BLK + jax.random.randint(subkeys[0], (N_FSDP, 1), 0, LENGTH // 4)
    remaining = LENGTH - long_length
    cut_points = jax.random.randint(subkeys[1], (N_FSDP, DOCS - 2), 0, 1 << 20) % remaining
    bounds = jnp.concatenate([long_length, long_length + jnp.sort(cut_points, axis=-1)], axis=-1)
    doc_ids = jnp.sum(positions[None, :, None] >= bounds[:, None, :], axis=-1).astype(jnp.int32)
    flipped_flag = jax.random.randint(subkeys[2], (N_FSDP, 1), 0, 2)
    mirrored = DOCS - 1 - doc_ids[:, ::-1]
    return jnp.where(flipped_flag == 1, mirrored, doc_ids).astype(jnp.int32)


def block_scale(stream_key, extent, cuts, smallest, largest):
    loudness = 1.0
    for dim, blocks in cuts:
        steps = jax.random.uniform(jax.random.fold_in(jax.random.fold_in(stream_key, 6), dim), (blocks,), jnp.float32, smallest / len(cuts), largest / len(cuts))
        loudness = loudness * jnp.repeat(jnp.exp(steps), extent[dim] // blocks).reshape((-1,) + (1,) * (len(extent) - 1 - dim))
    return loudness


def normal_values(key, extent, spread, reach, cuts=(), kind=jnp.bfloat16):
    array = spread * jax.random.normal(key, extent, jnp.float32)
    if cuts:
        array = array * block_scale(key, extent, cuts, -0.22, 0.18)
    return jnp.clip(array, -reach, reach).astype(kind)


def setup_inputs(seed: int = 0) -> dict:
    keys = jax.random.split(jax.random.key(seed), 14)
    return {
        "layer_input": normal_values(keys[0], (N_FSDP, LENGTH, D), 1.0, 6.0, ((0, 4), (1, 8))),
        "slot_table": jax.random.permutation(keys[1], N_CTX).astype(jnp.int32),
        "seq_ids": draw_seq_ids(jax.random.fold_in(keys[13], 71), 0),
        "w_query": normal_values(keys[3], (D, D), (D // 4) ** -0.5, 0.5, ((0, 4),)),
        "w_key": normal_values(keys[4], (D, KV_HEADS * HEAD), D ** -0.5, 0.25, ((0, 4),)),
        "w_value": normal_values(keys[5], (D, KV_HEADS * HEAD), D ** -0.5, 0.25, ((0, 4),)),
        "w_out": normal_values(keys[6], (D, D), 4 ** -0.5, 3.0, ((0, 4),)),
        "w_gate": normal_values(keys[7], (D, FF), D ** -0.5, 0.25, ((0, 4),)),
        "w_up": normal_values(keys[8], (D, FF), D ** -0.5, 0.25, ((0, 4),)),
        "w_down": normal_values(keys[9], (FF, D), FF ** -0.5, 0.15625, ((0, 4),)),
        "attn_gain": jnp.clip(1.0 + 0.1 * jax.random.normal(keys[10], (D,), jnp.float32), 0.5, 1.5).astype(jnp.bfloat16),
        "ffn_gain": jnp.clip(1.0 + 0.1 * jax.random.normal(keys[11], (D,), jnp.float32), 0.5, 1.5).astype(jnp.bfloat16),
        "cotangent": normal_values(keys[12], (N_FSDP, LENGTH, D), 1.0, 6.0, ((0, 4), (1, 8))),
    }


epsilon = 1e-05
rope_base = 100000.0
precise = lax.Precision.HIGHEST

@jax.custom_vjp
def low(v):
    return lax.optimization_barrier(v.astype(jnp.bfloat16)).astype(jnp.float32)

@jax.custom_vjp
def low_back(v):
    return v

def low_keep(v):
    return (low(v), None)

def low_pass(kept, grad):
    return (grad,)

def back_keep(v):
    return (v, None)

def back_low(kept, grad):
    return (low(grad),)
low.defvjp(low_keep, low_pass)
low_back.defvjp(back_keep, back_low)

def rotary_tables(positions):
    half_width = HEAD // 2
    frequencies = rope_base ** (-(jnp.arange(half_width, dtype=jnp.float32) * 2.0 / HEAD))
    angles = positions.astype(jnp.float32)[:, None] * frequencies[None, :]
    return (jnp.cos(angles), jnp.sin(angles))

def rotate(values, cos_table, sin_table):
    half_width = HEAD // 2
    first_half = values[..., :half_width]
    second_half = values[..., half_width:]
    cos_part = cos_table[:, None, :]
    sin_part = sin_table[:, None, :]
    return jnp.concatenate([first_half * cos_part - second_half * sin_part, second_half * cos_part + first_half * sin_part], axis=-1)

def rms_scaled(values, gain_vec):
    return values * lax.rsqrt(lax.optimization_barrier(jnp.mean(values * values, axis=-1, keepdims=True)) + epsilon) * gain_vec

def project(first_matrix, second_matrix):
    return jnp.dot(first_matrix, second_matrix, precision=precise)

def decoder_layer(tokens, w_query, w_key, w_value, w_out, w_gate, w_up, w_down, attn_gain, ffn_gain, documents):
    length = tokens.shape[0]
    positions = jnp.arange(length, dtype=jnp.int32)
    groups = HEADS // KV_HEADS
    cos_table, sin_table = rotary_tables(positions)
    normed = low(rms_scaled(tokens, attn_gain))
    queries = low_back(project(normed, w_query)).reshape(length, HEADS, HEAD)
    keys_raw = low_back(project(normed, w_key)).reshape(length, KV_HEADS, HEAD)
    values = low(low_back(project(normed, w_value))).reshape(length, KV_HEADS, HEAD)
    queries = low(rotate(queries, cos_table, sin_table) * HEAD ** (-0.5)).reshape(length, KV_HEADS, groups, HEAD)
    keys_rot = low(rotate(keys_raw, cos_table, sin_table))
    query_rows = math.gcd(length, 512)
    piece_count = length // query_rows

    def attend(pieces):
        query_piece, query_pos, query_doc = pieces
        scores = low_back(jnp.einsum('qhgd,khd->hgqk', query_piece, keys_rot, precision=precise))
        visible = (positions[None, :] <= query_pos[:, None]) & (documents[None, :] == query_doc[:, None])
        scores = jnp.where(visible, scores, -1e+30)
        probs = jax.nn.softmax(scores, axis=-1)
        return jnp.einsum('hgqk,khd->qhgd', low(probs), values, precision=precise)
    attended = lax.map(jax.checkpoint(attend), (queries.reshape(piece_count, query_rows, KV_HEADS, groups, HEAD), positions.reshape(piece_count, query_rows), documents.reshape(piece_count, query_rows)))
    attended = low(low_back(attended.reshape(length, HEADS * HEAD)))
    hidden = tokens + low_back(project(attended, w_out))
    normed_two = low(rms_scaled(hidden, ffn_gain))
    gate_value = low_back(project(normed_two, w_gate))
    up_value = low_back(project(normed_two, w_up))
    activation = low(jax.nn.silu(gate_value) * up_value)
    return hidden + low_back(project(activation, w_down))

def reference(layer_input, slot_table, seq_ids, w_query, w_key, w_value, w_out, w_gate, w_up, w_down, attn_gain, ffn_gain, cotangent):
    offsets = jnp.arange(2 * BLK, dtype=jnp.int32)
    blocks = jnp.where(offsets[None, :] < BLK, slot_table[:, None], 2 * N_CTX - 1 - slot_table[:, None])
    slot_pos = (blocks * BLK + offsets[None, :] % BLK).reshape(LENGTH).astype(jnp.int32)
    weights = tuple((weight_arg.astype(jnp.float32) for weight_arg in (w_query, w_key, w_value, w_out, w_gate, w_up, w_down, attn_gain, ffn_gain)))
    outputs = []
    input_grads = []
    totals = [jnp.zeros(weight_arg.shape, jnp.float32) for weight_arg in weights]
    for group_index in range(N_FSDP):
        tokens = jnp.zeros((LENGTH, D), jnp.float32).at[slot_pos].set(layer_input[group_index].astype(jnp.float32))
        seed_grad = jnp.zeros((LENGTH, D), jnp.float32).at[slot_pos].set(cotangent[group_index].astype(jnp.float32))
        documents = seq_ids[group_index]

        def forward(tokens_in, *params):
            return decoder_layer(tokens_in, *params, documents)
        result, pullback = jax.vjp(forward, tokens, *weights)
        gradients = pullback(seed_grad)
        outputs.append(result[slot_pos].astype(jnp.bfloat16))
        input_grads.append(gradients[0][slot_pos].astype(jnp.bfloat16))
        totals = [running + update for running, update in zip(totals, gradients[1:])]
    return (jnp.stack(outputs), jnp.stack(input_grads), totals[0], totals[1], totals[2], totals[3], totals[4], totals[5], totals[6], totals[7], totals[8])
```

```python
import jax
import jax.numpy as jnp
from jax import lax
from jax.experimental import pallas as pl
from jax.experimental.pallas import tpu as pltpu
from jax.sharding import PartitionSpec as P

D = 576
HEADS = 9
KV_HEADS = 3
HEAD = 64


epsilon = 1e-05
rope_base = 100000.0


def rotary_tables(positions):
    half_width = HEAD // 2
    frequencies = rope_base ** (-(jnp.arange(half_width, dtype=jnp.float32) * 2.0 / HEAD))
    angles = positions.astype(jnp.float32)[:, None] * frequencies[None, :]
    return (jnp.cos(angles), jnp.sin(angles))


def rotate(values, cos_table, sin_table):
    half_width = HEAD // 2
    first_half = values[..., :half_width]
    second_half = values[..., half_width:]
    cos_part = cos_table[:, None, :]
    sin_part = sin_table[:, None, :]
    return jnp.concatenate(
        [
            first_half * cos_part - second_half * sin_part,
            second_half * cos_part + first_half * sin_part,
        ],
        axis=-1,
    )


def rotate_back(values, cos_table, sin_table):
    half_width = HEAD // 2
    first_half = values[..., :half_width]
    second_half = values[..., half_width:]
    cos_part = cos_table[:, None, :]
    sin_part = sin_table[:, None, :]
    return jnp.concatenate(
        [
            first_half * cos_part + second_half * sin_part,
            second_half * cos_part - first_half * sin_part,
        ],
        axis=-1,
    )


def matmul(first_matrix, second_matrix):
    return jnp.dot(first_matrix, second_matrix, preferred_element_type=jnp.float32)


def contract_rows(first_matrix, second_matrix):
    return lax.dot_general(
        first_matrix, second_matrix, (((0,), (0,)), ((), ())), preferred_element_type=jnp.float32
    )


def times_transposed(first_matrix, second_matrix):
    return lax.dot_general(
        first_matrix, second_matrix, (((1,), (1,)), ((), ())), preferred_element_type=jnp.float32
    )


def norm_back(grad_normed, unit_rows, inv_root, gain_vec):
    scaled_grad = grad_normed * gain_vec
    return inv_root * (
        scaled_grad - unit_rows * jnp.mean(scaled_grad * unit_rows, axis=-1, keepdims=True)
    )


def swap(value, axis, offset):
    count = lax.axis_size(axis)
    return lax.ppermute(value, axis, [(i, i ^ offset) for i in range(count)])


def chip_swap(value, offset):
    return swap(value, "ctx", 2 * offset)


def core_swap(value):
    return swap(value, "ctx", 1)


def by_owner(pieces, index):
    bit = 1
    while bit < len(pieces):
        flag = (index & bit) != 0
        pieces = [jnp.where(flag, pieces[i ^ bit], pieces[i]) for i in range(len(pieces))]
        bit = bit * 2
    return pieces


def gather_rows(piece):
    count = lax.axis_size("fsdp")
    index = lax.axis_index("fsdp")
    pieces = [piece] + [swap(piece, "fsdp", i) for i in range(1, count)]
    return jnp.stack(by_owner(pieces, index))


def gather_chips(piece):
    chips = lax.axis_size("ctx") // 2
    own = [piece] + [chip_swap(piece, i) for i in range(1, chips)]
    return own + [core_swap(value) for value in own]


def place(pieces, shape, target, table=None):
    count = len(pieces)
    chips = count // 2
    scalars = [] if table is None else [table]

    def kernel(*refs):
        ins = refs[len(scalars) : len(scalars) + count]
        out = refs[-1]
        index = lax.axis_index("ctx")
        chip, core = index // 2, index % 2
        for n in range(count):
            target(out, ins[n], chip ^ (n % chips), core ^ (n // chips), *refs[: len(scalars)])

    return pl.pallas_call(
        kernel,
        out_shape=jax.ShapeDtypeStruct(shape, pieces[0].dtype),
        in_specs=[pl.BlockSpec(memory_space=pltpu.SMEM)] * len(scalars)
        + [pl.BlockSpec(memory_space=pltpu.VMEM)] * count,
        out_specs=pl.BlockSpec(memory_space=pltpu.VMEM),
        compiler_params=pltpu.CompilerParams(vmem_limit_bytes=56 * 1024 * 1024),
    )(*scalars, *pieces)


def store_chip_core(out, piece, to_chip, to_core):
    out[to_chip, to_core] = piece[...]


def store_core_chip(out, piece, to_chip, to_core):
    out[to_core, to_chip] = piece[...]


def store_chip_rows_core(out, piece, to_chip, to_core):
    out[to_chip, :, to_core] = piece[...]


def store_rows_chip_core(out, piece, to_chip, to_core):
    out[:, to_chip, to_core] = piece[...]


def store_blocks(out, piece, to_chip, to_core, table):
    block_len = out.shape[1]
    block = table[to_chip * 2 + to_core]
    out[block] = piece[:block_len]
    out[out.shape[0] - 1 - block] = piece[block_len:]


def dot_nt(first_matrix, second_matrix):
    return lax.dot_general(
        first_matrix, second_matrix, (((1,), (1,)), ((), ())), preferred_element_type=jnp.float32
    )


def dot_tn(first_matrix, second_matrix):
    return lax.dot_general(
        first_matrix, second_matrix, (((0,), (0,)), ((), ())), preferred_element_type=jnp.float32
    )


def heads_to_rows(values, group):
    groups = HEADS // KV_HEADS
    return jnp.concatenate(
        [
            values[:, (group * groups + i) * HEAD : (group * groups + i + 1) * HEAD]
            for i in range(groups)
        ],
        axis=0,
    )


def rows_to_heads(parts, block_len):
    groups = HEADS // KV_HEADS
    return jnp.concatenate(
        [part[i * block_len : (i + 1) * block_len] for part in parts for i in range(groups)],
        axis=1,
    )


def attention_forward(bounds, query_rot, pairs_all, first_key, last_key):
    row_count = query_rot.shape[0]
    block_len = row_count // 2
    groups = HEADS // KV_HEADS
    kv_width = KV_HEADS * HEAD
    wide = groups * block_len

    def kernel(bounds_ref, query_ref, pairs_ref, first_ref, last_ref, out_ref, log_ref):
        for b in range(2):
            rows = slice(b * block_len, (b + 1) * block_len)
            query_block = query_ref[rows, :]
            queries = [heads_to_rows(query_block, g) for g in range(KV_HEADS)]
            first = jnp.concatenate([first_ref[b : b + 1, :]] * groups, axis=1)
            last = jnp.concatenate([last_ref[b : b + 1, :]] * groups, axis=1)

            def step(j, state):
                start = pl.multiple_of(j * row_count, row_count)
                pos = start + lax.broadcasted_iota(jnp.int32, (row_count, wide), 0)
                visible = (pos >= first) & (pos <= last)
                result = []
                for g in range(KV_HEADS):
                    top, total, acc = state[g]
                    key_piece = pairs_ref[pl.ds(start, row_count), g * HEAD : (g + 1) * HEAD]
                    value_piece = pairs_ref[
                        pl.ds(start, row_count), kv_width + g * HEAD : kv_width + (g + 1) * HEAD
                    ]
                    scores = jnp.where(visible, dot_nt(key_piece, queries[g]), -1e30)
                    new_top = jnp.maximum(top, jnp.max(scores, axis=0, keepdims=True))
                    weights = jnp.exp(scores - new_top)
                    rescale = jnp.exp(top - new_top)
                    total = total * rescale + jnp.sum(weights, axis=0, keepdims=True)
                    acc = acc * rescale + dot_tn(value_piece, weights.astype(jnp.bfloat16))
                    result.append((new_top, total, acc))
                return tuple(result)

            state = lax.fori_loop(
                bounds_ref[2 * b],
                bounds_ref[2 * b + 1],
                step,
                tuple(
                    (
                        jnp.full((1, wide), -1e30, jnp.float32),
                        jnp.zeros((1, wide), jnp.float32),
                        jnp.zeros((HEAD, wide), jnp.float32),
                    )
                    for _ in range(KV_HEADS)
                ),
            )
            parts = []
            for g in range(KV_HEADS):
                top, total, acc = state[g]
                parts.append((acc / total).T)
                n = b * KV_HEADS + g
                log_ref[n : n + 1, :] = top + jnp.log(total)
            out_ref[rows, :] = rows_to_heads(parts, block_len)

    vmem = pl.BlockSpec(memory_space=pltpu.VMEM)
    return pl.pallas_call(
        kernel,
        out_shape=(
            jax.ShapeDtypeStruct((row_count, D), jnp.float32),
            jax.ShapeDtypeStruct((2 * KV_HEADS, wide), jnp.float32),
        ),
        in_specs=[pl.BlockSpec(memory_space=pltpu.SMEM)] + [vmem] * 4,
        out_specs=(vmem, vmem),
        compiler_params=pltpu.CompilerParams(vmem_limit_bytes=56 * 1024 * 1024),
        cost_estimate=pl.CostEstimate(
            flops=8 * 1024**3, bytes_accessed=4 * 1024**2, transcendentals=0
        ),
    )(bounds, query_rot, pairs_all, first_key, last_key)


def attention_backward(
    bounds, table, query_rot, pairs_all, first_key, last_key, log_total, attended, grad_attended
):
    row_count = query_rot.shape[0]
    block_len = row_count // 2
    groups = HEADS // KV_HEADS
    kv_width = KV_HEADS * HEAD
    wide = groups * block_len
    slots = table.shape[0]

    def kernel(
        bounds_ref,
        table_ref,
        query_ref,
        pairs_ref,
        first_ref,
        last_ref,
        log_ref,
        attended_ref,
        grad_ref,
        query_grad_ref,
        kept_ref,
        sent_ref,
        pair_grad_ref,
    ):
        pair_grad_ref[...] = jnp.zeros_like(pair_grad_ref)
        for b in range(2):
            rows = slice(b * block_len, (b + 1) * block_len)
            query_block = query_ref[rows, :]
            grad_block = grad_ref[rows, :]
            product = grad_block.astype(jnp.float32) * attended_ref[rows, :]
            queries = [heads_to_rows(query_block, g) for g in range(KV_HEADS)]
            grads = [heads_to_rows(grad_block, g) for g in range(KV_HEADS)]
            deltas = [
                jnp.sum(heads_to_rows(product, g).T, axis=0, keepdims=True)
                for g in range(KV_HEADS)
            ]
            first = jnp.concatenate([first_ref[b : b + 1, :]] * groups, axis=1)
            last = jnp.concatenate([last_ref[b : b + 1, :]] * groups, axis=1)

            def step(j, state):
                start = pl.multiple_of(j * row_count, row_count)
                pos = start + lax.broadcasted_iota(jnp.int32, (row_count, wide), 0)
                visible = (pos >= first) & (pos <= last)
                result = []
                key_grads = []
                value_grads = []
                for g in range(KV_HEADS):
                    key_piece = pairs_ref[pl.ds(start, row_count), g * HEAD : (g + 1) * HEAD]
                    value_piece = pairs_ref[
                        pl.ds(start, row_count), kv_width + g * HEAD : kv_width + (g + 1) * HEAD
                    ]
                    n = b * KV_HEADS + g
                    scores = dot_nt(key_piece, queries[g])
                    weights = jnp.where(visible, jnp.exp(scores - log_ref[n : n + 1, :]), 0.0)
                    weight_grad = dot_nt(value_piece, grads[g])
                    score_grad = (weights * (weight_grad - deltas[g])).astype(jnp.bfloat16)
                    value_grads.append(matmul(weights.astype(jnp.bfloat16), grads[g]))
                    key_grads.append(matmul(score_grad, queries[g]))
                    result.append(state[g] + dot_tn(key_piece, score_grad))
                pair_grad_ref[pl.ds(start, row_count), :] += jnp.concatenate(
                    key_grads + value_grads, axis=1
                )
                return tuple(result)

            state = lax.fori_loop(
                bounds_ref[2 * b],
                bounds_ref[2 * b + 1],
                step,
                tuple(jnp.zeros((HEAD, wide), jnp.float32) for _ in range(KV_HEADS)),
            )
            query_grad_ref[rows, :] = rows_to_heads([part.T for part in state], block_len)
        core = lax.axis_index("ctx") % 2
        for chip in range(slots // 2):
            for ref, owner in ((kept_ref, core), (sent_ref, 1 - core)):
                block = table_ref[chip * 2 + owner]
                other = 2 * slots - 1 - block
                for part, place_of in ((0, block), (1, other)):
                    source = pl.multiple_of(place_of * block_len, block_len)
                    ref[chip, part * block_len : (part + 1) * block_len, :] = pair_grad_ref[
                        pl.ds(source, block_len), :
                    ].astype(ref.dtype)

    vmem = pl.BlockSpec(memory_space=pltpu.VMEM)
    smem = pl.BlockSpec(memory_space=pltpu.SMEM)
    pair_shape = (slots // 2, row_count, 2 * kv_width)
    return pl.pallas_call(
        kernel,
        out_shape=(
            jax.ShapeDtypeStruct((row_count, D), jnp.float32),
            jax.ShapeDtypeStruct(pair_shape, jnp.float32),
            jax.ShapeDtypeStruct(pair_shape, jnp.bfloat16),
        ),
        in_specs=[smem, smem] + [vmem] * 7,
        out_specs=(vmem, vmem, vmem),
        scratch_shapes=[pltpu.VMEM((slots * row_count, 2 * kv_width), jnp.float32)],
        compiler_params=pltpu.CompilerParams(vmem_limit_bytes=56 * 1024 * 1024),
        cost_estimate=pl.CostEstimate(
            flops=16 * 1024**3, bytes_accessed=8 * 1024**2, transcendentals=0
        ),
    )(bounds, table, query_rot, pairs_all, first_key, last_key, log_total, attended, grad_attended)


def pick(values, index, axis=0):
    return lax.dynamic_index_in_dim(values, index, axis, keepdims=False)


def sum_chips(values):
    chips = lax.axis_size("ctx") // 2
    chip = lax.axis_index("ctx") // 2
    total = pick(values, chip).astype(jnp.float32)
    for i in range(1, chips):
        total = total + chip_swap(pick(values, chip ^ i), i).astype(jnp.float32)
    return total


def sum_rows(values):
    count = lax.axis_size("fsdp")
    index = lax.axis_index("fsdp")
    total = pick(values, index).astype(jnp.float32)
    for i in range(1, count):
        total = total + swap(pick(values, index ^ i), "fsdp", i).astype(jnp.float32)
    return total


def local(
    layer_input,
    slot_table,
    seq_ids,
    w_query,
    w_key,
    w_value,
    w_out,
    w_gate,
    w_up,
    w_down,
    attn_gain,
    ffn_gain,
    cotangent,
):
    ctx_count = lax.axis_size("ctx")
    ctx_index = lax.axis_index("ctx")
    row_count = layer_input.shape[1]
    block_len = row_count // 2
    key_count = row_count * ctx_count
    kv_width = KV_HEADS * HEAD
    scaling = HEAD ** (-0.5)
    chips = ctx_count // 2
    chip = ctx_index // 2
    core = ctx_index % 2
    shards_count = lax.axis_size("fsdp")
    shard_rows = w_query.shape[0]
    shard_down = w_down.shape[0]
    ff = w_gate.shape[1]
    mixed = w_query.shape[1] + 2 * kv_width + w_out.shape[1]
    lanes = ff // chips
    mixed_lanes = mixed // chips
    half_rows = shard_rows // 2
    down_rows = shard_down // ctx_count
    mixed_shard = jnp.concatenate([w_query, w_key, w_value, w_out], axis=1)
    mixed_piece = lax.dynamic_slice(
        mixed_shard, (core * half_rows, chip * mixed_lanes), (half_rows, mixed_lanes)
    )
    gains = jnp.concatenate([attn_gain, ffn_gain])
    gain_rows = -(-2 * shard_rows // mixed_lanes)
    gains = jnp.pad(gains, (0, gain_rows * mixed_lanes - 2 * shard_rows))
    mixed_rows = gather_rows(
        jnp.concatenate([mixed_piece, gains.reshape(gain_rows, mixed_lanes)], axis=0)
    )
    gains_all = mixed_rows[:, half_rows:].reshape(shards_count, gain_rows * mixed_lanes)
    gain_one = gains_all[:, :shard_rows].reshape(D).astype(jnp.float32)
    gain_two = gains_all[:, shard_rows : 2 * shard_rows].reshape(D).astype(jnp.float32)
    mixed_all = place(
        gather_chips(mixed_rows[:, :half_rows]),
        (chips, shards_count, 2, half_rows, mixed_lanes),
        store_chip_rows_core,
    )
    mixed_all = mixed_all.reshape(chips, D, mixed_lanes).transpose(1, 0, 2).reshape(D, mixed)
    wq_all = mixed_all[:, :D]
    wk_all = mixed_all[:, D : D + kv_width]
    wv_all = mixed_all[:, D + kv_width : D + 2 * kv_width]
    wo_all = mixed_all[:, D + 2 * kv_width :]
    gate_or_up = jnp.where(core == 0, w_gate, w_up)
    wide_piece = lax.dynamic_slice(gate_or_up, (0, chip * lanes), (shard_rows, lanes))
    wide_all = place(
        gather_chips(gather_rows(wide_piece)),
        (2, chips, shards_count, shard_rows, lanes),
        store_core_chip,
    )
    wide_all = wide_all.reshape(2, chips, D, lanes).transpose(0, 2, 1, 3).reshape(2, D, ff)
    gate_all, up_all = wide_all[0], wide_all[1]
    down_piece = lax.dynamic_slice(
        w_down, (ctx_index * down_rows, 0), (down_rows, w_down.shape[1])
    )
    down_all = place(
        gather_chips(gather_rows(down_piece)),
        (shards_count, chips, 2, down_rows, w_down.shape[1]),
        store_rows_chip_core,
    ).reshape(ff, w_down.shape[1])
    own_block = lax.dynamic_index_in_dim(slot_table, ctx_index, 0, keepdims=False)
    own_blocks = jnp.stack([own_block, 2 * ctx_count - 1 - own_block])
    block_pos = own_blocks[:, None] * block_len + jnp.arange(block_len, dtype=jnp.int32)[None, :]
    query_pos = block_pos.reshape(row_count)
    documents = seq_ids[0]
    query_doc = jnp.stack(
        [
            lax.dynamic_slice(documents, (own_block * block_len,), (block_len,)),
            lax.dynamic_slice(documents, (own_blocks[1] * block_len,), (block_len,)),
        ]
    )
    first_key = jnp.sum(
        (documents[None, :, None] < query_doc[:, None, :]).astype(jnp.int32), axis=1
    )
    bounds = jnp.stack(
        [jnp.min(first_key, axis=1) // row_count, own_blocks // 2 + 1], axis=1
    ).reshape(4)
    cos_table, sin_table = rotary_tables(query_pos)
    tokens = layer_input[0].astype(jnp.float32)
    inv_one = lax.rsqrt(jnp.mean(tokens * tokens, axis=-1, keepdims=True) + epsilon)
    unit_one = tokens * inv_one
    hidden_one = (unit_one * gain_one).astype(jnp.bfloat16)
    query_raw = matmul(hidden_one, wq_all).reshape(row_count, HEADS, HEAD)
    key_raw = matmul(hidden_one, wk_all).reshape(row_count, KV_HEADS, HEAD)
    value_low = matmul(hidden_one, wv_all).astype(jnp.bfloat16)
    query_rot = (
        (rotate(query_raw, cos_table, sin_table) * scaling)
        .astype(jnp.bfloat16)
        .reshape(row_count, D)
    )
    key_rot = (
        rotate(key_raw, cos_table, sin_table).astype(jnp.bfloat16).reshape(row_count, kv_width)
    )
    pairs_all = place(
        gather_chips(jnp.concatenate([key_rot, value_low], axis=1)),
        (2 * ctx_count, block_len, 2 * kv_width),
        store_blocks,
        slot_table,
    ).reshape(key_count, 2 * kv_width)
    attended, log_total = attention_forward(bounds, query_rot, pairs_all, first_key, block_pos)
    attn_low = attended.astype(jnp.bfloat16)
    residual = tokens + matmul(attn_low, wo_all)
    inv_two = lax.rsqrt(jnp.mean(residual * residual, axis=-1, keepdims=True) + epsilon)
    unit_two = residual * inv_two
    hidden_two = (unit_two * gain_two).astype(jnp.bfloat16)
    gate_value = matmul(hidden_two, gate_all)
    up_value = matmul(hidden_two, up_all)
    gate_sigmoid = jax.nn.sigmoid(gate_value)
    silu_gate = gate_value * gate_sigmoid
    activation = (silu_gate * up_value).astype(jnp.bfloat16)
    output = (residual + matmul(activation, down_all)).astype(jnp.bfloat16)
    grad_out = cotangent[0]
    grad_down_w = contract_rows(activation, grad_out)
    grad_activation = times_transposed(grad_out, down_all)
    grad_gate_low = (
        grad_activation * up_value * gate_sigmoid * (1.0 + gate_value * (1.0 - gate_sigmoid))
    ).astype(jnp.bfloat16)
    grad_up_low = (grad_activation * silu_gate).astype(jnp.bfloat16)
    wide_kept = contract_rows(hidden_two, jnp.where(core == 0, grad_gate_low, grad_up_low))
    wide_sent = contract_rows(hidden_two, jnp.where(core == 0, grad_up_low, grad_gate_low))
    wide_sum = (wide_kept + core_swap(wide_sent.astype(jnp.bfloat16)).astype(jnp.float32)).astype(
        jnp.bfloat16
    )
    wide_sum = wide_sum.reshape(D, chips, lanes).transpose(1, 0, 2)
    wide_sum = sum_chips(wide_sum).astype(jnp.bfloat16).reshape(shards_count, shard_rows, lanes)
    wide_part = sum_rows(wide_sum).astype(jnp.bfloat16)
    wide_grads = place(
        gather_chips(wide_part),
        (2, chips, shard_rows, lanes),
        store_core_chip,
    )
    wide_grads = wide_grads.transpose(0, 2, 1, 3).reshape(2, shard_rows, ff).astype(jnp.float32)
    grad_gate_w, grad_up_w = wide_grads[0], wide_grads[1]
    grad_down_w = grad_down_w.astype(jnp.bfloat16).reshape(
        shards_count, chips, 2, down_rows, w_down.shape[1]
    )
    down_sum = (
        pick(grad_down_w, core, 2).astype(jnp.float32)
        + core_swap(pick(grad_down_w, 1 - core, 2)).astype(jnp.float32)
    ).astype(jnp.bfloat16)
    down_sum = sum_chips(down_sum.transpose(1, 0, 2, 3)).astype(jnp.bfloat16)
    down_part = sum_rows(down_sum).astype(jnp.bfloat16)
    grad_down_w = (
        place(
            gather_chips(down_part),
            (chips, 2, down_rows, w_down.shape[1]),
            store_chip_core,
        )
        .reshape(shard_down, w_down.shape[1])
        .astype(jnp.float32)
    )
    grad_hidden_two = times_transposed(grad_gate_low, gate_all) + times_transposed(
        grad_up_low, up_all
    )
    grad_residual = grad_out.astype(jnp.float32) + norm_back(
        grad_hidden_two, unit_two, inv_two, gain_two
    )
    grad_branch = grad_residual.astype(jnp.bfloat16)
    grad_out_w = contract_rows(attn_low, grad_branch)
    grad_attended = times_transposed(grad_branch, wo_all).astype(jnp.bfloat16)
    query_grad, pairs_kept, pairs_sent = attention_backward(
        bounds,
        slot_table,
        query_rot,
        pairs_all,
        first_key,
        block_pos,
        log_total,
        attended,
        grad_attended,
    )
    owned_grads = sum_chips(
        (pairs_kept + core_swap(pairs_sent).astype(jnp.float32)).astype(jnp.bfloat16)
    )
    grad_query_low = (
        (rotate_back(query_grad.reshape(row_count, HEADS, HEAD), cos_table, sin_table) * scaling)
        .reshape(row_count, D)
        .astype(jnp.bfloat16)
    )
    grad_key_low = (
        rotate_back(
            owned_grads[:, :kv_width].reshape(row_count, KV_HEADS, HEAD), cos_table, sin_table
        )
        .reshape(row_count, kv_width)
        .astype(jnp.bfloat16)
    )
    grad_value_low = owned_grads[:, kv_width:].astype(jnp.bfloat16)
    grad_query_w = contract_rows(hidden_one, grad_query_low)
    grad_key_w = contract_rows(hidden_one, grad_key_low)
    grad_value_w = contract_rows(hidden_one, grad_value_low)
    grad_hidden_one = (
        times_transposed(grad_query_low, wq_all)
        + times_transposed(grad_key_low, wk_all)
        + times_transposed(grad_value_low, wv_all)
    )
    grad_input = (grad_residual + norm_back(grad_hidden_one, unit_one, inv_one, gain_one)).astype(
        jnp.bfloat16
    )
    mixed_grads = jnp.concatenate(
        [grad_query_w, grad_key_w, grad_value_w, grad_out_w], axis=1
    ).astype(jnp.bfloat16)
    mixed_grads = (
        mixed_grads.reshape(D, chips, mixed_lanes)
        .transpose(1, 0, 2)
        .reshape(chips, shards_count, 2, half_rows, mixed_lanes)
    )
    mixed_sum = (
        pick(mixed_grads, core, 2).astype(jnp.float32)
        + core_swap(pick(mixed_grads, 1 - core, 2)).astype(jnp.float32)
    ).astype(jnp.bfloat16)
    mixed_sum = sum_chips(mixed_sum).astype(jnp.bfloat16)
    mixed_part = sum_rows(mixed_sum).astype(jnp.bfloat16)
    mixed_shards = place(
        gather_chips(mixed_part),
        (chips, 2, half_rows, mixed_lanes),
        store_chip_core,
    )
    mixed_shards = (
        mixed_shards.reshape(chips, shard_rows, mixed_lanes)
        .transpose(1, 0, 2)
        .reshape(shard_rows, mixed)
        .astype(jnp.float32)
    )
    grad_gain_one = (
        jnp.sum(
            mixed_shards[:, : D + 2 * kv_width]
            * mixed_shard[:, : D + 2 * kv_width].astype(jnp.float32),
            axis=1,
        )
        / attn_gain.astype(jnp.float32)
    )
    grad_gain_two = (
        jnp.sum(grad_gate_w * w_gate.astype(jnp.float32), axis=1)
        + jnp.sum(grad_up_w * w_up.astype(jnp.float32), axis=1)
    ) / ffn_gain.astype(jnp.float32)
    return (
        output[None],
        grad_input[None],
        mixed_shards[:, :D],
        mixed_shards[:, D : D + kv_width],
        mixed_shards[:, D + kv_width : D + 2 * kv_width],
        mixed_shards[:, D + 2 * kv_width :],
        grad_gate_w,
        grad_up_w,
        grad_down_w,
        grad_gain_one,
        grad_gain_two,
    )


def solution(mesh):
    placed = (
        P("fsdp", "ctx", None),
        P(),
        P("fsdp", None),
        P("fsdp", None),
        P("fsdp", None),
        P("fsdp", None),
        P("fsdp", None),
        P("fsdp", None),
        P("fsdp", None),
        P("fsdp", None),
        P("fsdp"),
        P("fsdp"),
        P("fsdp", "ctx", None),
    )
    return jax.shard_map(
        local,
        mesh=mesh,
        in_specs=placed,
        out_specs=(
            P("fsdp", "ctx", None),
            P("fsdp", "ctx", None),
            P("fsdp", None),
            P("fsdp", None),
            P("fsdp", None),
            P("fsdp", None),
            P("fsdp", None),
            P("fsdp", None),
            P("fsdp", None),
            P("fsdp"),
            P("fsdp"),
        ),
        check_vma=False,
    )
```

```python
import jax
import jax.numpy as jnp
from jax import lax
from jax.experimental import pallas as pl
from jax.experimental.pallas import tpu as pltpu
from jax.sharding import PartitionSpec as P

D = 576
HEADS = 9
KV_HEADS = 3
HEAD = 64
GROUPS = HEADS // KV_HEADS
KV_WIDTH = KV_HEADS * HEAD
TILE = 128

epsilon = 1e-05
rope_base = 100000.0

VMEM = pl.BlockSpec(memory_space=pltpu.VMEM)
SMEM = pl.BlockSpec(memory_space=pltpu.SMEM)


def run_kernel(kernel, out_shapes, inputs, scalars=0, scratch=(), microseconds=1):
    return pl.pallas_call(
        kernel,
        out_shape=tuple(jax.ShapeDtypeStruct(*out) for out in out_shapes),
        in_specs=[SMEM] * scalars + [VMEM] * (len(inputs) - scalars),
        out_specs=tuple(VMEM for _ in out_shapes),
        scratch_shapes=list(scratch),
        compiler_params=pltpu.CompilerParams(vmem_limit_bytes=60 * 1024 * 1024),
        cost_estimate=pl.CostEstimate(
            flops=microseconds * 1150 * 10**6, bytes_accessed=1024, transcendentals=0
        ),
    )(*inputs)


def rank():
    index = lax.axis_index("ctx")
    return index // 2, index % 2


def swap(value, axis, offset):
    count = lax.axis_size(axis)
    return lax.ppermute(value, axis, [(i, i ^ offset) for i in range(count)])


def chip_swap(value, offset):
    return swap(value, "ctx", 2 * offset)


def core_swap(value):
    return swap(value, "ctx", 1)


def by_owner(pieces, index):
    bit = 1
    while bit < len(pieces):
        flag = (index & bit) != 0
        pieces = [jnp.where(flag, pieces[i ^ bit], pieces[i]) for i in range(len(pieces))]
        bit = bit * 2
    return pieces


def gather_rows(piece, *others):
    count = lax.axis_size("fsdp")
    index = lax.axis_index("fsdp")
    values = piece[None]
    offset = 1
    while offset < count:
        if offset > 1 and others:
            values = after(values, *others)
        other = swap(values, "fsdp", offset)
        flag = (index & offset) != 0
        values = jnp.concatenate(
            [jnp.where(flag, other, values), jnp.where(flag, values, other)], axis=0
        )
        offset = offset * 2
    return values


def gather_half(piece, *others):
    half = lax.axis_size("fsdp") // 2
    index = lax.axis_index("fsdp")
    received = lax.ppermute(piece, ("ctx", "fsdp"), half_pairs())
    values = after(jnp.where(in_half(), piece, received)[None], *others)
    offset = 1
    while offset < half:
        other = swap(values, "fsdp", offset)
        flag = (index & offset) != 0
        values = jnp.concatenate(
            [jnp.where(flag, other, values), jnp.where(flag, values, other)], axis=0
        )
        offset = offset * 2
    return values


def gather_same_core(piece):
    return [piece] + [chip_swap(piece, i) for i in range(1, lax.axis_size("ctx") // 2)]


def gather_chips(piece):
    own = gather_same_core(piece)
    return own + [core_swap(value) for value in own]


def after(value, *others):
    return lax.optimization_barrier((value, others))[0]


def in_rank_order(pieces):
    chip, core = rank()
    chips = len(pieces) // 2
    own, other = by_owner(pieces[:chips], chip), by_owner(pieces[chips:], chip)
    ordered = [by_owner(list(pair), core) for pair in zip(own, other)]
    return [value for pair in ordered for value in pair]


def sum_cores(kept, sent):
    return (kept.astype(jnp.float32) + core_swap(sent).astype(jnp.float32)).astype(jnp.bfloat16)


def sum_chips(sums, *others):
    received = tuple(chip_swap(sums[i], i) for i in range(1, len(sums)))
    if others:
        received = after(received, *others)
    return sum((value.astype(jnp.float32) for value in received), sums[0].astype(jnp.float32))


def half_pairs():
    count = lax.axis_size("fsdp")
    half = count // 2
    return [
        (c * count + z, c * count + (z ^ half))
        for c in range(lax.axis_size("ctx"))
        for z in range(count)
        if z // half == c % 2
    ]


def in_half():
    half = lax.axis_size("fsdp") // 2
    return lax.axis_index("fsdp") // half == lax.axis_index("ctx") % 2


def sum_rows(values):
    count = lax.axis_size("fsdp")
    index = lax.axis_index("fsdp")

    def pick(offset):
        return lax.dynamic_index_in_dim(values, index ^ offset, 0, keepdims=False)

    total = pick(0).astype(jnp.float32)
    for i in range(1, count):
        total = total + swap(pick(i), "fsdp", i).astype(jnp.float32)
    return total


def first_piece(mixed, c, count):
    width = mixed.shape[1] // count
    return lax.dynamic_slice_in_dim(mixed, c * width, width, 1)


def wide_piece(gate, up, chip, core, chips):
    lanes = gate.shape[1] // chips
    q = chip % (chips // 2)
    wide = jnp.where(chip < chips // 2, gate, up)
    return lax.dynamic_slice_in_dim(wide, (core * (chips // 2) + q) * lanes, lanes, 1)


def stack_down(part, pile):
    width = D // pile
    return jnp.concatenate([part[:, n * width : (n + 1) * width] for n in range(pile)], axis=0)


def unstack_down(part, pile):
    rows = part.shape[0] // pile
    return jnp.concatenate([part[n * rows : (n + 1) * rows] for n in range(pile)], axis=1)


def by_core_slices(values):
    _, core = rank()
    values = values.reshape(-1, 2, *values.shape[1:])
    mine, theirs = (
        lax.dynamic_index_in_dim(values, side, 1, keepdims=False) for side in (core, 1 - core)
    )
    return jnp.concatenate(both_cores(mine, core_swap(theirs), core))


def both_cores(own, other, core):
    return jnp.where(core == 0, own, other), jnp.where(core == 0, other, own)


def gain_gradient(terms, gain_row):
    total = sum(terms[:, t : t + TILE] for t in range(0, terms.shape[1], TILE))
    return jnp.sum(total.T, axis=0, keepdims=True) / gain_row


def finish_first(pieces, shard, gain):
    count = len(pieces)
    chips = count // 2
    rows = shard.shape[0]
    used = 2 * KV_WIDTH + D

    def kernel(*refs):
        shard_ref, gain_ref = refs[count : count + 2]
        query, key, value, out, gain_grad, whole = refs[count + 2 :]
        chip, core = rank()
        for n in range(count):
            c = (chip ^ (n % chips)) * 2 + (core ^ (n // chips))
            whole[:, pl.ds(pl.multiple_of(c * TILE, TILE), TILE)] = refs[n][:rows, :].astype(
                jnp.float32
            )
        key[...] = whole[:, :KV_WIDTH]
        value[...] = whole[:, KV_WIDTH : 2 * KV_WIDTH]
        query[...] = whole[:, 2 * KV_WIDTH : used]
        for n in range(chips):
            columns = pl.ds(pl.multiple_of((chip ^ n) * TILE, TILE), TILE)
            pair = both_cores(
                refs[n][rows:, :].astype(jnp.float32),
                refs[n + chips][rows:, :].astype(jnp.float32),
                core,
            )
            for m in range(2):
                out[m * (rows // 2) : (m + 1) * (rows // 2), columns] = jnp.concatenate(
                    [part[:, m * (TILE // 2) : (m + 1) * (TILE // 2)] for part in pair], axis=1
                )
        out[:, chips * TILE :] = whole[:, used:]
        gain_grad[...] = gain_gradient(whole[...] * shard_ref[...].astype(jnp.float32), gain_ref[...])

    return run_kernel(
        kernel,
        [
            ((rows, D), jnp.float32),
            ((rows, KV_WIDTH), jnp.float32),
            ((rows, KV_WIDTH), jnp.float32),
            ((rows, D), jnp.float32),
            ((1, rows), jnp.float32),
        ],
        [*pieces, shard, gain],
        scratch=[pltpu.VMEM((rows, count * TILE), jnp.float32)],
    )


def finish_wide(pieces, w_gate, w_up, gain, pile):
    count = len(pieces)
    chips = count // 2
    rows, ff = w_gate.shape
    lanes = ff // chips
    down_rows = rows // pile
    low_lanes = D // pile

    def kernel(*refs):
        gate_ref, up_ref, gain_ref = refs[count : count + 3]
        gate, up, down, gain_grad, total = refs[count + 3 :]
        chip, core = rank()
        total[...] = jnp.zeros_like(total)
        for n in range(count):
            to_chip, to_core = chip ^ (n % chips), core ^ (n // chips)
            column = (to_core * (chips // 2) + to_chip % (chips // 2)) * lanes
            columns = pl.ds(pl.multiple_of(column, TILE), lanes)
            for kind, out, weight in ((0, gate, gate_ref), (1, up, up_ref)):

                @pl.when(to_chip // (chips // 2) == kind)
                def _():
                    part = refs[n][:, :lanes].astype(jnp.float32)
                    out[:, columns] = part
                    total[...] += part * weight[:, columns].astype(jnp.float32)

            start = pl.multiple_of((to_chip * 2 + to_core) * down_rows, 16)
            for m in range(pile):
                down[pl.ds(start, down_rows), m * low_lanes : (m + 1) * low_lanes] = refs[n][
                    m * down_rows : (m + 1) * down_rows, lanes:
                ].astype(jnp.float32)
        gain_grad[...] = gain_gradient(total[...], gain_ref[...])

    return run_kernel(
        kernel,
        [
            ((rows, ff), jnp.float32),
            ((rows, ff), jnp.float32),
            ((count * down_rows, D), jnp.float32),
            ((1, rows), jnp.float32),
        ],
        [*pieces, w_gate, w_up, gain],
        scratch=[pltpu.VMEM((rows, lanes), jnp.float32)],
    )


def dot(first_matrix, second_matrix):
    return jnp.dot(first_matrix, second_matrix, preferred_element_type=jnp.float32)


def dot_nt(first_matrix, second_matrix):
    return lax.dot_general(
        first_matrix, second_matrix, (((1,), (1,)), ((), ())), preferred_element_type=jnp.float32
    )


def dot_tn(first_matrix, second_matrix):
    return lax.dot_general(
        first_matrix, second_matrix, (((0,), (0,)), ((), ())), preferred_element_type=jnp.float32
    )


def norm_back(grad_normed, unit_rows, inv_root, gain_vec):
    scaled_grad = grad_normed * gain_vec
    return inv_root * (
        scaled_grad - unit_rows * jnp.mean(scaled_grad * unit_rows, axis=-1, keepdims=True)
    )


def inverse_root(rows):
    return lax.rsqrt(jnp.mean(rows * rows, axis=-1, keepdims=True) + epsilon)


def turn(values, cos_tile, sin_tile):
    lane = lax.broadcasted_iota(jnp.int32, values.shape, 1) % HEAD
    turned = jnp.where(
        lane < HEAD // 2,
        -pltpu.roll(values, TILE - HEAD // 2, 1),
        pltpu.roll(values, HEAD // 2, 1),
    )
    return values * cos_tile + turned * sin_tile


def turn_pairs(values, cos_tile, sin_tile):
    lane = lax.broadcasted_iota(jnp.int32, cos_tile.shape, 1)
    middle = values[:, TILE : 2 * TILE]
    return jnp.concatenate(
        [
            turn(values[:, :TILE], cos_tile, sin_tile),
            jnp.where(lane < HEAD, turn(middle, cos_tile, sin_tile), middle),
            values[:, 2 * TILE :],
        ],
        axis=1,
    )


def normalize(token_pieces, gain):
    row_count = token_pieces[0].shape[0]
    chips = len(token_pieces)

    def kernel(*refs):
        gain_ref, hidden_ref = refs[chips:]
        for n in range(chips):
            tokens = refs[n][...].astype(jnp.float32)
            hidden_ref[n] = ((tokens * inverse_root(tokens)) * gain_ref[...]).astype(jnp.bfloat16)

    return run_kernel(
        kernel, [((chips, row_count, D), jnp.bfloat16)], [*token_pieces, gain], microseconds=3
    )[0]


def project(direct, table, hidden_half, first, cos_all, sin_all):
    chips, row_count, _ = hidden_half.shape
    block_len = row_count // 2
    count = 2 * chips
    columns_all = count * TILE if direct else first[0].shape[1]
    shards = lax.axis_size("fsdp")
    rows = D // shards

    def kernel(table_ref, hidden_ref, cos_ref, sin_ref, *refs):
        first_refs = refs[: len(first)]
        query_ref, pairs_ref = refs[len(first) : len(first) + 2]
        chip, core = rank()
        if direct:
            mixed_ref = refs[-1]
            for n in range(count):
                c = (chip ^ (n % chips)) * 2 + (core ^ (n // chips))
                columns = pl.ds(pl.multiple_of(c * TILE, TILE), TILE)
                for z in range(shards):
                    mixed_ref[z * rows : (z + 1) * rows, columns] = first_refs[n][z, :rows, :]
        else:
            mixed_ref = first_refs[0]
        for n in range(chips):
            hidden = hidden_ref[n]
            pairs = dot(hidden, mixed_ref[:, : 2 * KV_WIDTH])
            block = table_ref[(chip ^ n) * 2 + core]
            queries = dot(hidden, mixed_ref[:, 2 * KV_WIDTH :]) if n == 0 else None
            for part, place in ((0, block), (1, 2 * count - 1 - block)):
                source = pl.ds(pl.multiple_of(place * block_len, block_len), block_len)
                own = slice(part * block_len, (part + 1) * block_len)
                cos_tile, sin_tile = cos_ref[source, :], sin_ref[source, :]
                pairs_ref[n, own, :] = turn_pairs(pairs[own], cos_tile, sin_tile).astype(
                    jnp.bfloat16
                )
                if n == 0:
                    for start in range(0, D, TILE):
                        width = min(TILE, D - start)
                        turned = turn(queries[own, start : start + TILE], cos_tile, sin_tile)
                        query_ref[own, start : start + width] = (
                            (turned * HEAD ** (-0.5)).astype(jnp.bfloat16)[:, :width]
                        )

    outs = [((row_count, D), jnp.bfloat16), ((chips, row_count, 2 * KV_WIDTH), jnp.bfloat16)]
    if direct:
        outs += [((D, columns_all), jnp.bfloat16)]
    result = run_kernel(
        kernel, outs, [table, hidden_half, cos_all, sin_all, *first], scalars=1, microseconds=5
    )
    return result if direct else (*result, first[0])


def natural_order(out, table_ref, halves):
    chip, core = rank()
    chips, row_count, _ = halves[0].shape
    block_len = row_count // 2
    for a in range(2):
        for n in range(chips):
            block = table_ref[(chip ^ n) * 2 + (core ^ a)]
            for part, place in ((0, block), (1, 4 * chips - 1 - block)):
                rows = pl.ds(pl.multiple_of(place * block_len, block_len), block_len)
                out[rows, :] = halves[a][n, part * block_len : (part + 1) * block_len, :]


def heads_to_rows(values, group):
    return jnp.concatenate(
        [
            values[:, (group * GROUPS + i) * HEAD : (group * GROUPS + i + 1) * HEAD]
            for i in range(GROUPS)
        ],
        axis=0,
    )


def attention_forward(bounds, table, query_rot, pair_halves, first_key, last_key):
    row_count = query_rot.shape[0]
    block_len = row_count // 2
    wide = GROUPS * block_len

    def kernel(
        bounds_ref,
        table_ref,
        query_ref,
        own_ref,
        other_ref,
        first_ref,
        last_ref,
        out_ref,
        log_ref,
        pairs_ref,
    ):
        natural_order(pairs_ref, table_ref, (own_ref, other_ref))
        for b in range(2):
            rows = slice(b * block_len, (b + 1) * block_len)
            query_block = query_ref[rows, :]
            queries = [heads_to_rows(query_block, g) for g in range(KV_HEADS)]
            first = jnp.concatenate([first_ref[b : b + 1, :]] * GROUPS, axis=1)
            last = jnp.concatenate([last_ref[b : b + 1, :]] * GROUPS, axis=1)

            def step(j, state):
                start = pl.multiple_of(j * row_count, row_count)
                pos = start + lax.broadcasted_iota(jnp.int32, (row_count, wide), 0)
                visible = (pos >= first) & (pos <= last)
                result = []
                for g in range(KV_HEADS):
                    top, total, acc = state[g]
                    key_piece = pairs_ref[pl.ds(start, row_count), g * HEAD : (g + 1) * HEAD]
                    value_piece = pairs_ref[
                        pl.ds(start, row_count), KV_WIDTH + g * HEAD : KV_WIDTH + (g + 1) * HEAD
                    ]
                    scores = jnp.where(visible, dot_nt(key_piece, queries[g]), -1e30)
                    new_top = jnp.maximum(top, jnp.max(scores, axis=0, keepdims=True))
                    weights = jnp.exp(scores - new_top)
                    rescale = jnp.exp(top - new_top)
                    total = total * rescale + jnp.sum(weights, axis=0, keepdims=True)
                    acc = acc * rescale + dot_tn(value_piece, weights.astype(jnp.bfloat16))
                    result.append((new_top, total, acc))
                return tuple(result)

            state = lax.fori_loop(
                bounds_ref[2 * b],
                bounds_ref[2 * b + 1],
                step,
                tuple(
                    (
                        jnp.full((1, wide), -1e30, jnp.float32),
                        jnp.zeros((1, wide), jnp.float32),
                        jnp.zeros((HEAD, wide), jnp.float32),
                    )
                    for _ in range(KV_HEADS)
                ),
            )
            parts = []
            for g in range(KV_HEADS):
                top, total, acc = state[g]
                part = (acc / total).T
                parts += [part[i * block_len : (i + 1) * block_len] for i in range(GROUPS)]
                n = b * KV_HEADS + g
                log_ref[n : n + 1, :] = top + jnp.log(total)
            out_ref[rows, :] = jnp.concatenate(parts, axis=1)

    return run_kernel(
        kernel,
        [((row_count, D), jnp.float32), ((2 * KV_HEADS, wide), jnp.float32)],
        [bounds, table, query_rot, *pair_halves, first_key, last_key],
        scalars=2,
        scratch=[pltpu.VMEM((table.shape[0] * row_count, 2 * KV_WIDTH), jnp.bfloat16)],
        microseconds=12,
    )


def fill_out_weights(out_w_ref, own_ref, other_ref, down_rows):
    _, core = rank()
    half, rows, _ = other_ref.shape
    for n in range(half):
        pair = both_cores(own_ref[n, down_rows:, :], other_ref[n], core)
        for owner in range(2):
            start = (owner * half + n) * rows
            out_w_ref[start : start + rows, :] = pair[owner]


def mix(attended, tokens, low_own, out_other, gain):
    row_count = tokens.shape[0]
    down_rows = low_own.shape[1] - out_other.shape[1]

    def kernel(
        attended_ref, tokens_ref, own_ref, other_ref, gain_ref, residual_ref, hidden_ref, out_w_ref
    ):
        fill_out_weights(out_w_ref, own_ref, other_ref, down_rows)
        attn_low = attended_ref[...].astype(jnp.bfloat16)
        residual = tokens_ref[...].astype(jnp.float32) + dot(attn_low, out_w_ref[...])
        residual_ref[...] = residual
        hidden_ref[...] = ((residual * inverse_root(residual)) * gain_ref[...]).astype(jnp.bfloat16)

    return run_kernel(
        kernel,
        [((row_count, D), jnp.float32), ((row_count, D), jnp.bfloat16)],
        [attended, tokens, low_own, out_other, gain],
        scratch=[pltpu.VMEM((D, D), jnp.bfloat16)],
        microseconds=2,
    )


def feed_forward(direct, hidden, hidden_other, grad_out, grad_other, wide, low_own, ff, shards):
    row_count = hidden.shape[0]
    width = ff // 2
    chips = lax.axis_size("ctx") // 2
    lanes = ff // chips
    rows = D // shards
    down_rows = ff // shards
    half = shards // 2
    steps = 2
    chunk = width // steps
    slice_rows = down_rows // (2 * chips)
    pile = rows // slice_rows

    def kernel(hidden_ref, hidden_other_ref, grad_ref, grad_other_ref, low_ref, *refs):
        wide_refs, refs = refs[: len(wide)], refs[len(wide) :]
        out_ref, hidden_grad_ref, sent_ref = refs[:3]
        wide_grads = refs[3 : 3 + (chips if direct else 2)]
        wide_ref, gate_grad_ref, down_ref, low_ref_f32 = refs[-4:]
        chip, _ = rank()
        for n in range(half):
            down_ref[n * down_rows : (n + 1) * down_rows, :] = low_ref[n, :down_rows, :]
        if direct:
            for i in range(chips):
                q = chip ^ i
                columns = pl.ds(pl.multiple_of((q % (chips // 2)) * lanes, TILE), lanes)
                wide_ref[q // (chips // 2), :, columns] = wide_refs[i][...].reshape(D, lanes)
        else:
            for kind in range(2):
                wide_ref[kind] = wide_refs[kind][...]
        hidden_all = jnp.concatenate([hidden_ref[...], hidden_other_ref[...]], axis=0)
        grad_all = jnp.concatenate([grad_ref[...], grad_other_ref[...]], axis=0)
        hidden_t = hidden_all.T
        result = jnp.zeros((2 * row_count, D), jnp.float32)
        grad_hidden = jnp.zeros((2 * row_count, D), jnp.float32)
        for j in range(steps):
            columns = slice(j * chunk, (j + 1) * chunk)
            gate_w, up_w = wide_ref[0, :, columns], wide_ref[1, :, columns]
            down_w = down_ref[columns, :]
            gate_value, up_value = dot(hidden_all, gate_w), dot(hidden_all, up_w)
            sigmoid = 1.0 / (1.0 + jnp.exp(-gate_value))
            silu = gate_value * sigmoid
            activation = (silu * up_value).astype(jnp.bfloat16)
            result += dot(activation, down_w)
            grad_activation = dot_nt(grad_all, down_w)
            grad_gate = (
                grad_activation * up_value * sigmoid * (1.0 + gate_value * (1.0 - sigmoid))
            ).astype(jnp.bfloat16)
            grad_up = (grad_activation * silu).astype(jnp.bfloat16)
            grad_hidden += dot_nt(grad_gate, gate_w) + dot_nt(grad_up, up_w)
            gate_grad_ref[0, :, columns] = grad_gate
            gate_grad_ref[1, :, columns] = grad_up
            low = dot(activation.T, grad_all)
            if direct:
                low_ref_f32[...] = low
                for i in range(chips):
                    for g in range(2):
                        start = pl.multiple_of(((chip ^ i) * 2 + g) * slice_rows, 16)
                        part = low_ref_f32[pl.ds(start, slice_rows), :].astype(jnp.bfloat16)
                        wide_grads[i][2 * j + g, :, lanes:] = stack_down(part, pile)
            else:
                refs[5][columns, :] = low.astype(jnp.bfloat16)
        out_ref[...] = result[:row_count]
        hidden_grad_ref[...] = grad_hidden[:row_count]
        sent_ref[0] = result[row_count:].astype(jnp.bfloat16)
        sent_ref[1] = grad_hidden[row_count:].astype(jnp.bfloat16)
        if direct:
            for i in range(chips):
                q = chip ^ i
                columns = pl.ds(pl.multiple_of((q % (chips // 2)) * lanes, TILE), lanes)
                operand = gate_grad_ref[q // (chips // 2), :, columns]
                wide_grads[i][:, :, :lanes] = (
                    dot(hidden_t, operand).astype(jnp.bfloat16).reshape(shards, rows, lanes)
                )
        else:
            for kind in range(2):
                wide_grads[kind][...] = dot(hidden_t, gate_grad_ref[kind]).astype(jnp.bfloat16)

    outs = [
        ((row_count, D), jnp.float32),
        ((row_count, D), jnp.float32),
        ((2, row_count, D), jnp.bfloat16),
    ]
    outs += (
        [((shards, rows, lanes + D // pile), jnp.bfloat16)] * chips
        if direct
        else [((D, width), jnp.bfloat16)] * 2 + [((width, D), jnp.bfloat16)]
    )
    return run_kernel(
        kernel,
        outs,
        [hidden, hidden_other, grad_out, grad_other, low_own, *wide],
        scratch=[
            pltpu.VMEM((2, D, width), jnp.bfloat16),
            pltpu.VMEM((2, 2 * row_count, width), jnp.bfloat16),
            pltpu.VMEM((width, D), jnp.bfloat16),
            pltpu.VMEM((chunk, D), jnp.float32),
        ],
        microseconds=12,
    )


def unmix(
    residual, out_kept, grad_kept, received, grad_out, attended, low_own, out_other, gain
):
    row_count = residual.shape[0]
    down_rows = low_own.shape[1] - out_other.shape[1]

    def kernel(
        residual_ref,
        out_kept_ref,
        grad_kept_ref,
        received_ref,
        grad_out_ref,
        attended_ref,
        own_ref,
        other_ref,
        gain_ref,
        output_ref,
        residual_grad_ref,
        attended_grad_ref,
        out_grad_ref,
        out_w_ref,
    ):
        fill_out_weights(out_w_ref, own_ref, other_ref, down_rows)
        residual = residual_ref[...]
        result = residual + out_kept_ref[...] + received_ref[0].astype(jnp.float32)
        output_ref[...] = result.astype(jnp.bfloat16)
        grad_hidden = grad_kept_ref[...] + received_ref[1].astype(jnp.float32)
        inv_two = inverse_root(residual)
        residual_grad = grad_out_ref[...].astype(jnp.float32) + norm_back(
            grad_hidden, residual * inv_two, inv_two, gain_ref[...]
        )
        residual_grad_ref[...] = residual_grad
        grad_branch = residual_grad.astype(jnp.bfloat16)
        attended_grad_ref[...] = dot_nt(grad_branch, out_w_ref[...]).astype(jnp.bfloat16)
        out_grad_ref[...] = dot_tn(
            attended_ref[...].astype(jnp.bfloat16), grad_branch
        ).astype(jnp.bfloat16)

    return run_kernel(
        kernel,
        [
            ((row_count, D), jnp.bfloat16),
            ((row_count, D), jnp.float32),
            ((row_count, D), jnp.bfloat16),
            ((D, D), jnp.bfloat16),
        ],
        [
            residual,
            out_kept,
            grad_kept,
            received,
            grad_out,
            attended,
            low_own,
            out_other,
            gain,
        ],
        scratch=[pltpu.VMEM((D, D), jnp.bfloat16)],
        microseconds=4,
    )


def attention_backward(
    bounds,
    table,
    query_rot,
    pair_halves,
    first_key,
    last_key,
    log_total,
    attended,
    grad_attended,
    cos_all,
    sin_all,
    cos_own,
    sin_own,
):
    row_count = query_rot.shape[0]
    block_len = row_count // 2
    wide = GROUPS * block_len
    slots = table.shape[0]
    chips = slots // 2
    half = HEAD // 2

    def kernel(
        bounds_ref,
        table_ref,
        query_ref,
        own_ref,
        other_ref,
        first_ref,
        last_ref,
        log_ref,
        attended_ref,
        grad_ref,
        cos_ref,
        sin_ref,
        cos_own_ref,
        sin_own_ref,
        query_t_ref,
        kept_ref,
        sent_ref,
        pairs_ref,
        pair_grad_ref,
    ):
        natural_order(pairs_ref, table_ref, (own_ref, other_ref))
        pair_grad_ref[...] = jnp.zeros_like(pair_grad_ref)
        for b in range(2):
            rows = slice(b * block_len, (b + 1) * block_len)
            query_block = query_ref[rows, :]
            grad_block = grad_ref[rows, :]
            product = grad_block.astype(jnp.float32) * attended_ref[rows, :]
            queries = [heads_to_rows(query_block, g) for g in range(KV_HEADS)]
            grads = [heads_to_rows(grad_block, g) for g in range(KV_HEADS)]
            deltas = [
                jnp.sum(heads_to_rows(product, g).T, axis=0, keepdims=True)
                for g in range(KV_HEADS)
            ]
            first = jnp.concatenate([first_ref[b : b + 1, :]] * GROUPS, axis=1)
            last = jnp.concatenate([last_ref[b : b + 1, :]] * GROUPS, axis=1)

            def step(j, state):
                start = pl.multiple_of(j * row_count, row_count)
                pos = start + lax.broadcasted_iota(jnp.int32, (row_count, wide), 0)
                visible = (pos >= first) & (pos <= last)
                result = []
                key_grads = []
                value_grads = []
                for g in range(KV_HEADS):
                    key_piece = pairs_ref[pl.ds(start, row_count), g * HEAD : (g + 1) * HEAD]
                    value_piece = pairs_ref[
                        pl.ds(start, row_count), KV_WIDTH + g * HEAD : KV_WIDTH + (g + 1) * HEAD
                    ]
                    n = b * KV_HEADS + g
                    scores = dot_nt(key_piece, queries[g])
                    weights = jnp.where(visible, jnp.exp(scores - log_ref[n : n + 1, :]), 0.0)
                    weight_grad = dot_nt(value_piece, grads[g])
                    score_grad = (weights * (weight_grad - deltas[g])).astype(jnp.bfloat16)
                    value_grads.append(dot(weights.astype(jnp.bfloat16), grads[g]))
                    key_grads.append(dot(score_grad, queries[g]))
                    result.append(state[g] + dot_tn(key_piece, score_grad))
                pair_grad_ref[pl.ds(start, row_count), :] += jnp.concatenate(
                    key_grads + value_grads, axis=1
                )
                return tuple(result)

            state = lax.fori_loop(
                bounds_ref[2 * b],
                bounds_ref[2 * b + 1],
                step,
                tuple(jnp.zeros((HEAD, wide), jnp.float32) for _ in range(KV_HEADS)),
            )
            cos_part, sin_part = cos_own_ref[:, rows], sin_own_ref[:, rows]
            for g in range(KV_HEADS):
                for i in range(GROUPS):
                    part = state[g][:, i * block_len : (i + 1) * block_len]
                    top, bottom = part[:half], part[half:]
                    h = (g * GROUPS + i) * HEAD
                    query_t_ref[h : h + half, rows] = (
                        (top * cos_part + bottom * sin_part) * HEAD ** (-0.5)
                    ).astype(jnp.bfloat16)
                    query_t_ref[h + half : h + HEAD, rows] = (
                        (bottom * cos_part - top * sin_part) * HEAD ** (-0.5)
                    ).astype(jnp.bfloat16)

        chip, core = rank()
        for i in range(chips):
            for ref, to_core in ((kept_ref, core), (sent_ref, 1 - core)):
                block = table_ref[(chip ^ i) * 2 + to_core]
                for part, place in ((0, block), (1, 2 * slots - 1 - block)):
                    source = pl.ds(pl.multiple_of(place * block_len, block_len), block_len)
                    ref[i, part * block_len : (part + 1) * block_len, :] = turn_pairs(
                        pair_grad_ref[source, :], cos_ref[source, :], -sin_ref[source, :]
                    ).astype(jnp.bfloat16)

    half_shape = ((chips, row_count, 2 * KV_WIDTH), jnp.bfloat16)
    return run_kernel(
        kernel,
        [((D, row_count), jnp.bfloat16), half_shape, half_shape],
        [
            bounds,
            table,
            query_rot,
            *pair_halves,
            first_key,
            last_key,
            log_total,
            attended,
            grad_attended,
            cos_all,
            sin_all,
            cos_own,
            sin_own,
        ],
        scalars=2,
        scratch=[
            pltpu.VMEM((slots * row_count, 2 * KV_WIDTH), jnp.bfloat16),
            pltpu.VMEM((slots * row_count, 2 * KV_WIDTH), jnp.float32),
        ],
        microseconds=16,
    )


def query_gradients(query_t, hidden_half):
    row_count = query_t.shape[1]

    def kernel(query_t_ref, hidden_ref, query_ref, weight_ref):
        query_ref[...] = query_t_ref[...].T
        weight_ref[...] = dot(query_t_ref[...], hidden_ref[0]).T.astype(jnp.bfloat16)

    return run_kernel(
        kernel,
        [((row_count, D), jnp.bfloat16), ((D, D), jnp.bfloat16)],
        [query_t, hidden_half],
        microseconds=2,
    )


def first_gradients(direct, kept, received, hidden_half, query_w, out_grad, shards):
    chips, row_count, _ = kept.shape
    rest = D - HEAD
    columns_all = 2 * KV_WIDTH + D + HEAD
    rows = D // shards

    def kernel(kept_ref, received_ref, hidden_ref, query_w_ref, out_grad_ref, *refs):
        pair_refs, outs = refs[:chips], refs[chips:-1]
        mixed_ref = refs[-1]
        total = jnp.zeros((2 * KV_WIDTH, D), jnp.float32)
        for i in range(chips):
            pairs = (
                kept_ref[i].astype(jnp.float32) + received_ref[i].astype(jnp.float32)
            ).astype(jnp.bfloat16)
            pair_refs[i][...] = pairs
            total += dot_tn(pairs, hidden_ref[i])
        mixed_ref[:, : 2 * KV_WIDTH] = total.T.astype(jnp.bfloat16)
        mixed_ref[:, 2 * KV_WIDTH : 2 * KV_WIDTH + D] = query_w_ref[...]
        mixed_ref[:, 2 * KV_WIDTH + D :] = out_grad_ref[:, rest:]
        if not direct:
            outs[0][...] = mixed_ref[...]
            return
        chip, core = rank()
        for n in range(2 * chips):
            c = (chip ^ (n % chips)) * 2 + (core ^ (n // chips))
            part = mixed_ref[:, pl.ds(pl.multiple_of(c * TILE, TILE), TILE)]
            tile = out_grad_ref[:, pl.ds(pl.multiple_of((c // 2) * TILE, TILE), TILE)]
            unit = jnp.where(c % 2 == 0, tile[:, : TILE // 2], tile[:, TILE // 2 :])
            for z in range(shards):
                outs[n][z, :rows, :] = part[z * rows : (z + 1) * rows]
                middle = z * rows + rows // 2
                outs[n][z, rows:, : TILE // 2] = unit[z * rows : middle]
                outs[n][z, rows:, TILE // 2 :] = unit[middle : (z + 1) * rows]

    outs = [((row_count, 2 * KV_WIDTH), jnp.bfloat16)] * chips
    outs += (
        [((shards, rows + rows // 2, TILE), jnp.bfloat16)] * (2 * chips)
        if direct
        else [((D, columns_all), jnp.bfloat16)]
    )
    result = run_kernel(
        kernel,
        outs,
        [kept, received, hidden_half, query_w, out_grad],
        scratch=[pltpu.VMEM((D, columns_all), jnp.bfloat16)],
        microseconds=3,
    )
    return result[:chips], result[chips:]


def local(
    layer_input,
    slot_table,
    seq_ids,
    w_query,
    w_key,
    w_value,
    w_out,
    w_gate,
    w_up,
    w_down,
    attn_gain,
    ffn_gain,
    cotangent,
):
    count = lax.axis_size("ctx")
    chips = count // 2
    index = lax.axis_index("ctx")
    chip, core = rank()
    shards = lax.axis_size("fsdp")
    rows, ff = w_gate.shape
    row_count = layer_input.shape[1]
    block_len = row_count // 2
    length = row_count * count
    direct = (
        rows % 16 == 0 and (ff // chips) % TILE == 0 and count * TILE == D + 2 * KV_WIDTH + HEAD
    )

    mixed_shard = jnp.concatenate(
        [w_key, w_value, w_query, jnp.zeros((rows, HEAD), jnp.bfloat16)], axis=1
    )
    piece = first_piece(mixed_shard, index, count)
    gains = jnp.concatenate([attn_gain, ffn_gain])
    gains = jnp.pad(gains, (0, 16 * piece.shape[1] - 2 * rows)).reshape(16, piece.shape[1])
    tokens_low = layer_input[0]
    token_pieces = [tokens_low] + [chip_swap(tokens_low, i) for i in range(1, chips)]
    first_rows = gather_rows(jnp.concatenate([piece, gains], axis=0))
    gains_all = first_rows[:, rows:].reshape(shards, -1).astype(jnp.float32)
    gain_one = gains_all[:, :rows].reshape(1, D)
    gain_two = gains_all[:, rows : 2 * rows].reshape(1, D)
    hidden_half = normalize(token_pieces, gain_one)
    first_own = gather_same_core(after(first_rows, hidden_half))
    first_pieces = first_own + [core_swap(v) for v in first_own]
    wide_rows = gather_rows(wide_piece(w_gate, w_up, chip, core, chips), first_rows)
    low_shard = after(jnp.concatenate([w_down, w_out], axis=0), wide_rows)
    wide_pieces = gather_same_core(wide_rows)
    low_own = gather_half(low_shard)
    out_other = core_swap(low_own[:, w_down.shape[0] :])
    grad_out = cotangent[0]
    first = (
        first_pieces
        if direct
        else [
            jnp.concatenate(
                [v[:, :rows].reshape(D, -1) for v in in_rank_order(first_pieces)], axis=1
            )
        ]
    )

    own_block = lax.dynamic_index_in_dim(slot_table, index, 0, keepdims=False)
    own_blocks = jnp.stack([own_block, 2 * count - 1 - own_block])
    block_pos = own_blocks[:, None] * block_len + jnp.arange(block_len, dtype=jnp.int32)[None, :]
    documents = seq_ids[0]
    query_doc = jnp.stack(
        [
            lax.dynamic_slice(documents, (own_blocks[i] * block_len,), (block_len,))
            for i in range(2)
        ]
    )
    first_key = jnp.sum(
        (documents[None, :, None] < query_doc[:, None, :]).astype(jnp.int32), axis=1
    )
    bounds = jnp.stack(
        [jnp.min(first_key, axis=1) // row_count, own_blocks // 2 + 1], axis=1
    ).reshape(4)
    frequencies = rope_base ** (-(jnp.arange(HEAD // 2, dtype=jnp.float32) * 2.0 / HEAD))
    angles = jnp.arange(length, dtype=jnp.int32).astype(jnp.float32)[:, None] * frequencies[None, :]
    cos_all = jnp.tile(jnp.cos(angles), (1, 2 * TILE // HEAD))
    sin_all = jnp.tile(jnp.sin(angles), (1, 2 * TILE // HEAD))
    own_angles = frequencies[:, None] * block_pos.reshape(1, row_count).astype(jnp.float32)
    cos_own, sin_own = jnp.cos(own_angles), jnp.sin(own_angles)

    query_rot, own_pairs, mixed = project(
        direct, slot_table, hidden_half, first, cos_all, sin_all
    )
    pair_halves = (own_pairs, core_swap(own_pairs))
    attended, log_total = attention_forward(
        bounds, slot_table, query_rot, pair_halves, first_key, block_pos
    )
    grad_other = core_swap(after(grad_out, attended))
    residual, hidden_two = mix(attended, tokens_low, low_own, out_other, gain_two)
    if direct:
        wide = wide_pieces
    else:
        whole = [v.reshape(D, -1) for v in by_owner(wide_pieces, chip)]
        wide = [jnp.concatenate(whole[n : n + chips // 2], axis=1) for n in (0, chips // 2)]
    out_kept, grad_kept, sent, *wide_grads = feed_forward(
        direct,
        hidden_two,
        core_swap(hidden_two),
        grad_out,
        grad_other,
        wide,
        low_own,
        ff,
        shards,
    )
    lanes = ff // chips
    slice_rows = w_down.shape[0] // count
    pile = rows // slice_rows
    if not direct:
        gate_grad, up_grad, down_grad = wide_grads
        down_grad = down_grad.reshape(shards // 2, chips, 2, slice_rows, pile, D // pile)
        down_grad = down_grad.transpose(0, 2, 1, 4, 3, 5).reshape(shards, chips, rows, D // pile)
        wide_grads = [
            jnp.concatenate(
                [
                    lax.dynamic_slice_in_dim(
                        jnp.where(c < chips // 2, gate_grad, up_grad),
                        (c % (chips // 2)) * lanes,
                        lanes,
                        1,
                    ).reshape(shards, rows, lanes),
                    lax.dynamic_index_in_dim(down_grad, c, 1, keepdims=False),
                ],
                axis=2,
            )
            for c in (chip ^ i for i in range(chips))
        ]
    output, grad_residual, grad_attended, out_grad = unmix(
        residual,
        out_kept,
        grad_kept,
        core_swap(sent),
        grad_out,
        attended,
        low_own,
        out_other,
        gain_two,
    )

    query_t, pairs_kept, pairs_sent = attention_backward(
        bounds,
        slot_table,
        query_rot,
        pair_halves,
        first_key,
        block_pos,
        log_total,
        attended,
        grad_attended,
        cos_all,
        sin_all,
        cos_own,
        sin_own,
    )
    pairs_received = core_swap(pairs_sent)
    grad_query, query_w = query_gradients(query_t, hidden_half)
    pair_sums, mixed_grads = first_gradients(
        direct, pairs_kept, pairs_received, hidden_half, query_w, out_grad, shards
    )
    if not direct:
        targets = [(chip ^ i) * 2 + (core ^ a) for a in range(2) for i in range(chips)]
        units = [
            first_piece(out_grad[:, : D - HEAD], c, count)
            .reshape(shards, 2, rows // 2, -1)
            .transpose(0, 2, 1, 3)
            .reshape(shards, rows // 2, -1)
            for c in targets
        ]
        mixed_grads = [
            jnp.concatenate(
                [first_piece(mixed_grads[0], c, count).reshape(shards, rows, -1), unit], axis=1
            )
            for c, unit in zip(targets, units)
        ]
    mixed_sums = [sum_cores(*pair) for pair in zip(mixed_grads[:chips], mixed_grads[chips:])]
    first_sum = sum_chips(mixed_sums).astype(jnp.bfloat16)
    first_part = sum_rows(first_sum).astype(jnp.bfloat16)
    first_all = gather_chips(first_part)
    wide_sum = sum_chips(wide_grads, query_t).astype(jnp.bfloat16)
    wide_sum = jnp.concatenate(
        [wide_sum[:, :, :lanes], by_core_slices(wide_sum[:, :, lanes:])], axis=2
    )
    wide_part = sum_rows(wide_sum).astype(jnp.bfloat16)
    wide_all = gather_chips(wide_part)
    owned = sum_chips(after(tuple(pair_sums), first_sum)).astype(jnp.bfloat16)
    grad_hidden_one = dot_nt(
        jnp.concatenate([owned, grad_query], axis=1), mixed[:, : 2 * KV_WIDTH + D]
    )
    tokens = tokens_low.astype(jnp.float32)
    inv_one = inverse_root(tokens)
    grad_input = (
        grad_residual + norm_back(grad_hidden_one, tokens * inv_one, inv_one, gain_one)
    ).astype(jnp.bfloat16)

    gain_rows = [v.astype(jnp.float32).reshape(1, rows) for v in (attn_gain, ffn_gain)]
    if direct:
        gate_grad, up_grad, down_grad, gain_grad_two = finish_wide(
            wide_all, w_gate, w_up, gain_rows[1], pile
        )
        query_w, key_w, value_w, out_w, gain_grad_one = finish_first(
            first_all, mixed_shard, gain_rows[0]
        )
    else:
        own, other = by_owner(wide_all[:chips], chip), by_owner(wide_all[chips:], chip)
        cores = both_cores(jnp.stack(own), jnp.stack(other), core)
        down_grad = jnp.concatenate(
            [unstack_down(cores[c % 2][c // 2][:, lanes:], pile) for c in range(count)]
        ).astype(jnp.float32)
        gate_grad, up_grad = (
            jnp.concatenate(
                [cores[k][n + q][:, :lanes] for k in range(2) for q in range(chips // 2)], axis=1
            ).astype(jnp.float32)
            for n in (0, chips // 2)
        )
        ordered = in_rank_order(first_all)
        first_grad = jnp.concatenate([v[:rows] for v in ordered], axis=1).astype(jnp.float32)
        units = [
            v[rows:].reshape(rows // 2, 2, -1).transpose(1, 0, 2).reshape(rows, -1) for v in ordered
        ]
        key_w, value_w, query_w, last = jnp.split(
            first_grad, [KV_WIDTH, 2 * KV_WIDTH, 2 * KV_WIDTH + D], axis=1
        )
        out_w = jnp.concatenate([*[v.astype(jnp.float32) for v in units], last], axis=1)
        used = 2 * KV_WIDTH + D
        gain_grad_one = (
            jnp.sum(
                first_grad[:, :used] * mixed_shard[:, :used].astype(jnp.float32),
                axis=1,
            )
            / gain_rows[0]
        )
        gain_grad_two = (
            jnp.sum(
                gate_grad * w_gate.astype(jnp.float32) + up_grad * w_up.astype(jnp.float32),
                axis=1,
            )
            / gain_rows[1]
        )
    return (
        output[None],
        grad_input[None],
        query_w,
        key_w,
        value_w,
        out_w,
        gate_grad,
        up_grad,
        down_grad,
        gain_grad_one.reshape(rows),
        gain_grad_two.reshape(rows),
    )


def solution(mesh):
    placed = (
        P("fsdp", "ctx", None),
        P(),
        P("fsdp", None),
        P("fsdp", None),
        P("fsdp", None),
        P("fsdp", None),
        P("fsdp", None),
        P("fsdp", None),
        P("fsdp", None),
        P("fsdp", None),
        P("fsdp"),
        P("fsdp"),
        P("fsdp", "ctx", None),
    )
    return jax.shard_map(
        local,
        mesh=mesh,
        in_specs=placed,
        out_specs=(
            P("fsdp", "ctx", None),
            P("fsdp", "ctx", None),
            P("fsdp", None),
            P("fsdp", None),
            P("fsdp", None),
            P("fsdp", None),
            P("fsdp", None),
            P("fsdp", None),
            P("fsdp", None),
            P("fsdp"),
            P("fsdp"),
        ),
        check_vma=False,
    )
```

```python
import jax
import jax.numpy as jnp
from jax import lax
from jax.experimental import pallas as pl
from jax.experimental.pallas import tpu as pltpu
from jax.sharding import PartitionSpec as P

D = 576
HEADS = 9
KV_HEADS = 3
HEAD = 64
GROUPS = HEADS // KV_HEADS
KV_WIDTH = KV_HEADS * HEAD
TILE = 128

epsilon = 1e-05
rope_base = 100000.0

VMEM = pl.BlockSpec(memory_space=pltpu.VMEM)
SMEM = pl.BlockSpec(memory_space=pltpu.SMEM)


def run_kernel(kernel, out_shapes, inputs, scalars=0, scratch=(), microseconds=1):
    return pl.pallas_call(
        kernel,
        out_shape=tuple(jax.ShapeDtypeStruct(*out) for out in out_shapes),
        in_specs=[SMEM] * scalars + [VMEM] * (len(inputs) - scalars),
        out_specs=tuple(VMEM for _ in out_shapes),
        scratch_shapes=list(scratch),
        compiler_params=pltpu.CompilerParams(vmem_limit_bytes=60 * 1024 * 1024),
        cost_estimate=pl.CostEstimate(
            flops=microseconds * 1150 * 10**6, bytes_accessed=1024, transcendentals=0
        ),
    )(*inputs)


def rank():
    index = lax.axis_index("ctx")
    return index // 2, index % 2


def swap(value, axis, offset):
    count = lax.axis_size(axis)
    return lax.ppermute(value, axis, [(i, i ^ offset) for i in range(count)])


def chip_swap(value, offset):
    return swap(value, "ctx", 2 * offset)


def core_swap(value):
    return swap(value, "ctx", 1)


def by_owner(pieces, index):
    bit = 1
    while bit < len(pieces):
        flag = (index & bit) != 0
        pieces = [jnp.where(flag, pieces[i ^ bit], pieces[i]) for i in range(len(pieces))]
        bit = bit * 2
    return pieces


def in_order(own, other, offset):
    flag = (lax.axis_index("fsdp") & offset) != 0
    return jnp.concatenate([jnp.where(flag, other, own), jnp.where(flag, own, other)], axis=0)


def start_gather_rows(piece, *others):
    count = lax.axis_size("fsdp")
    values = piece[None]
    offset = 1
    while offset < count // 2:
        values = in_order(values, swap(values, "fsdp", offset), offset)
        offset = offset * 2
    values = after(values, *others)
    return values, swap(values, "fsdp", offset)


def gather_rows(piece, *others):
    count = lax.axis_size("fsdp")
    index = lax.axis_index("fsdp")
    values = piece[None]
    offset = 1
    while offset < count:
        if offset > 1 and others:
            values = after(values, *others)
        other = swap(values, "fsdp", offset)
        flag = (index & offset) != 0
        values = jnp.concatenate(
            [jnp.where(flag, other, values), jnp.where(flag, values, other)], axis=0
        )
        offset = offset * 2
    return values


def start_gather_half(piece):
    received = lax.ppermute(piece, ("ctx", "fsdp"), half_pairs())
    return jnp.where(in_half(), piece, received)[None]


def finish_gather_half(values):
    offset = 1
    while offset < lax.axis_size("fsdp") // 2:
        values = in_order(values, swap(values, "fsdp", offset), offset)
        offset = offset * 2
    return values


def gather_same_core(piece):
    return [piece] + [chip_swap(piece, i) for i in range(1, lax.axis_size("ctx") // 2)]


def gather_chips(piece):
    own = gather_same_core(piece)
    return own + [core_swap(value) for value in own]


def after(value, *others):
    return lax.optimization_barrier((value, others))[0]


def in_rank_order(pieces):
    chip, core = rank()
    chips = len(pieces) // 2
    own, other = by_owner(pieces[:chips], chip), by_owner(pieces[chips:], chip)
    ordered = [by_owner(list(pair), core) for pair in zip(own, other)]
    return [value for pair in ordered for value in pair]


def sum_cores(kept, sent):
    return (kept.astype(jnp.float32) + core_swap(sent).astype(jnp.float32)).astype(jnp.bfloat16)


def sum_chips(sums, *others):
    received = tuple(chip_swap(sums[i], i) for i in range(1, len(sums)))
    if others:
        received = after(received, *others)
    return sum((value.astype(jnp.float32) for value in received), sums[0].astype(jnp.float32))


def half_pairs():
    count = lax.axis_size("fsdp")
    half = count // 2
    return [
        (c * count + z, c * count + (z ^ half))
        for c in range(lax.axis_size("ctx"))
        for z in range(count)
        if z // half == c % 2
    ]


def in_half():
    half = lax.axis_size("fsdp") // 2
    return lax.axis_index("fsdp") // half == lax.axis_index("ctx") % 2


def sum_rows(values):
    count = lax.axis_size("fsdp")
    index = lax.axis_index("fsdp")

    def pick(offset):
        return lax.dynamic_index_in_dim(values, index ^ offset, 0, keepdims=False)

    total = pick(0).astype(jnp.float32)
    for i in range(1, count):
        total = total + swap(pick(i), "fsdp", i).astype(jnp.float32)
    return total


def first_piece(mixed, c, count):
    width = mixed.shape[1] // count
    return lax.dynamic_slice_in_dim(mixed, c * width, width, 1)


def wide_piece(gate, up, chip, core, chips):
    lanes = gate.shape[1] // chips
    q = chip % (chips // 2)
    wide = jnp.where(chip < chips // 2, gate, up)
    return lax.dynamic_slice_in_dim(wide, (core * (chips // 2) + q) * lanes, lanes, 1)


def stack_down(part, pile):
    width = D // pile
    return jnp.concatenate([part[:, n * width : (n + 1) * width] for n in range(pile)], axis=0)


def unstack_down(part, pile):
    rows = part.shape[0] // pile
    return jnp.concatenate([part[n * rows : (n + 1) * rows] for n in range(pile)], axis=1)


def by_core_slices(values):
    _, core = rank()
    values = values.reshape(-1, 2, *values.shape[1:])
    mine, theirs = (
        lax.dynamic_index_in_dim(values, side, 1, keepdims=False) for side in (core, 1 - core)
    )
    return jnp.concatenate(both_cores(mine, core_swap(theirs), core))


def both_cores(own, other, core):
    return jnp.where(core == 0, own, other), jnp.where(core == 0, other, own)


def gain_gradient(terms, gain_row):
    total = sum(terms[:, t : t + TILE] for t in range(0, terms.shape[1], TILE))
    return jnp.sum(total.T, axis=0, keepdims=True) / gain_row


def finish_first(pieces, shard, gain):
    count = len(pieces)
    chips = count // 2
    rows = shard.shape[0]
    used = 2 * KV_WIDTH + D

    def kernel(*refs):
        shard_ref, gain_ref = refs[count : count + 2]
        query, key, value, out, gain_grad, whole = refs[count + 2 :]
        chip, core = rank()
        for n in range(count):
            c = (chip ^ (n % chips)) * 2 + (core ^ (n // chips))
            whole[:, pl.ds(pl.multiple_of(c * TILE, TILE), TILE)] = refs[n][:rows, :].astype(
                jnp.float32
            )
        key[...] = whole[:, :KV_WIDTH]
        value[...] = whole[:, KV_WIDTH : 2 * KV_WIDTH]
        query[...] = whole[:, 2 * KV_WIDTH : used]
        for n in range(chips):
            columns = pl.ds(pl.multiple_of((chip ^ n) * TILE, TILE), TILE)
            pair = both_cores(
                refs[n][rows:, :].astype(jnp.float32),
                refs[n + chips][rows:, :].astype(jnp.float32),
                core,
            )
            for m in range(2):
                out[m * (rows // 2) : (m + 1) * (rows // 2), columns] = jnp.concatenate(
                    [part[:, m * (TILE // 2) : (m + 1) * (TILE // 2)] for part in pair], axis=1
                )
        out[:, chips * TILE :] = whole[:, used:]
        terms = whole[...] * shard_ref[...].astype(jnp.float32)
        lane = lax.broadcasted_iota(jnp.int32, terms.shape, 1)
        gain_grad[...] = gain_gradient(jnp.where(lane < used, terms, 0.0), gain_ref[...])

    return run_kernel(
        kernel,
        [
            ((rows, D), jnp.float32),
            ((rows, KV_WIDTH), jnp.float32),
            ((rows, KV_WIDTH), jnp.float32),
            ((rows, D), jnp.float32),
            ((1, rows), jnp.float32),
        ],
        [*pieces, shard, gain],
        scratch=[pltpu.VMEM((rows, count * TILE), jnp.float32)],
    )


def finish_wide(pieces, w_gate, w_up, gain, pile):
    count = len(pieces)
    chips = count // 2
    rows, ff = w_gate.shape
    lanes = ff // chips
    down_rows = rows // pile
    low_lanes = D // pile

    def kernel(*refs):
        gate_ref, up_ref, gain_ref = refs[count : count + 3]
        gate, up, down, gain_grad, total, low = refs[count + 3 :]
        chip, core = rank()
        total[...] = jnp.zeros_like(total)
        for n in range(count):
            to_chip, to_core = chip ^ (n % chips), core ^ (n // chips)
            column = (to_core * (chips // 2) + to_chip % (chips // 2)) * lanes
            columns = pl.ds(pl.multiple_of(column, TILE), lanes)
            for kind, out, weight in ((0, gate, gate_ref), (1, up, up_ref)):

                @pl.when(to_chip // (chips // 2) == kind)
                def _():
                    part = refs[n][:, :lanes].astype(jnp.float32)
                    out[:, columns] = part
                    total[...] += part * weight[:, columns].astype(jnp.float32)

            start = pl.multiple_of((to_chip * 2 + to_core) * down_rows, 16)
            for m in range(pile):
                low[pl.ds(start, down_rows), m * low_lanes : (m + 1) * low_lanes] = refs[n][
                    m * down_rows : (m + 1) * down_rows, lanes:
                ].astype(jnp.float32)
        down[...] = low[...].T
        gain_grad[...] = gain_gradient(total[...], gain_ref[...])

    return run_kernel(
        kernel,
        [
            ((rows, ff), jnp.float32),
            ((rows, ff), jnp.float32),
            ((D, count * down_rows), jnp.float32),
            ((1, rows), jnp.float32),
        ],
        [*pieces, w_gate, w_up, gain],
        scratch=[
            pltpu.VMEM((rows, lanes), jnp.float32),
            pltpu.VMEM((count * down_rows, D), jnp.float32),
        ],
    )


def dot(first_matrix, second_matrix):
    return jnp.dot(first_matrix, second_matrix, preferred_element_type=jnp.float32)


def dot_nt(first_matrix, second_matrix):
    return lax.dot_general(
        first_matrix, second_matrix, (((1,), (1,)), ((), ())), preferred_element_type=jnp.float32
    )


def dot_tn(first_matrix, second_matrix):
    return lax.dot_general(
        first_matrix, second_matrix, (((0,), (0,)), ((), ())), preferred_element_type=jnp.float32
    )


def norm_back(grad_normed, unit_rows, inv_root, gain_vec):
    scaled_grad = grad_normed * gain_vec
    return inv_root * (
        scaled_grad - unit_rows * jnp.mean(scaled_grad * unit_rows, axis=-1, keepdims=True)
    )


def inverse_root(rows):
    return lax.rsqrt(jnp.mean(rows * rows, axis=-1, keepdims=True) + epsilon)


def turn(values, cos_tile, sin_tile):
    lane = lax.broadcasted_iota(jnp.int32, values.shape, 1) % HEAD
    turned = jnp.where(
        lane < HEAD // 2,
        -pltpu.roll(values, TILE - HEAD // 2, 1),
        pltpu.roll(values, HEAD // 2, 1),
    )
    return values * cos_tile + turned * sin_tile


def turn_pairs(values, cos_tile, sin_tile):
    lane = lax.broadcasted_iota(jnp.int32, cos_tile.shape, 1)
    middle = values[:, TILE : 2 * TILE]
    return jnp.concatenate(
        [
            turn(values[:, :TILE], cos_tile, sin_tile),
            jnp.where(lane < HEAD, turn(middle, cos_tile, sin_tile), middle),
            values[:, 2 * TILE :],
        ],
        axis=1,
    )


def normalize(token_pieces, gain):
    row_count = token_pieces[0].shape[0]
    chips = len(token_pieces)

    def kernel(*refs):
        gain_ref, hidden_ref = refs[chips:]
        for n in range(chips):
            tokens = refs[n][...].astype(jnp.float32)
            hidden_ref[n] = ((tokens * inverse_root(tokens)) * gain_ref[...]).astype(jnp.bfloat16)

    return run_kernel(
        kernel, [((chips, row_count, D), jnp.bfloat16)], [*token_pieces, gain], microseconds=3
    )[0]


def project(direct, table, hidden_half, first, cos_all, sin_all):
    chips, row_count, _ = hidden_half.shape
    block_len = row_count // 2
    count = 2 * chips
    columns_all = count * TILE if direct else first[0].shape[1]
    shards = lax.axis_size("fsdp")
    rows = D // shards

    def kernel(table_ref, hidden_ref, cos_ref, sin_ref, *refs):
        first_refs = refs[: len(first)]
        query_ref, pairs_ref = refs[len(first) : len(first) + 2]
        chip, core = rank()
        if direct:
            mixed_ref, out_w_ref = refs[-2:]
            for n in range(count):
                c = (chip ^ (n % chips)) * 2 + (core ^ (n // chips))
                columns = pl.ds(pl.multiple_of(c * TILE, TILE), TILE)
                for z in range(shards):
                    mixed_ref[z * rows : (z + 1) * rows, columns] = first_refs[n][z, :rows, :]
            for n in range(chips):
                columns = pl.ds(pl.multiple_of((chip ^ n) * TILE, TILE), TILE)
                for z in range(shards):
                    pair = both_cores(
                        first_refs[n][z, rows : rows + rows // 2, :].astype(jnp.float32),
                        first_refs[n + chips][z, rows : rows + rows // 2, :].astype(jnp.float32),
                        core,
                    )
                    half = TILE // 2
                    block = jnp.concatenate(
                        [
                            jnp.concatenate([part[:, m * half : (m + 1) * half] for part in pair], axis=1)
                            for m in range(2)
                        ],
                        axis=0,
                    )
                    out_w_ref[z * rows : (z + 1) * rows, columns] = block.astype(jnp.bfloat16)
            out_w_ref[:, chips * TILE :] = mixed_ref[:, 2 * KV_WIDTH + D :]
        else:
            mixed_ref = first_refs[0]
        for n in range(chips):
            hidden = hidden_ref[n]
            pairs = dot(hidden, mixed_ref[:, : 2 * KV_WIDTH])
            block = table_ref[(chip ^ n) * 2 + core]
            queries = dot(hidden, mixed_ref[:, 2 * KV_WIDTH :]) if n == 0 else None
            for part, place in ((0, block), (1, 2 * count - 1 - block)):
                source = pl.ds(pl.multiple_of(place * block_len, block_len), block_len)
                own = slice(part * block_len, (part + 1) * block_len)
                cos_tile, sin_tile = cos_ref[source, :], sin_ref[source, :]
                pairs_ref[n, own, :] = turn_pairs(pairs[own], cos_tile, sin_tile).astype(
                    jnp.bfloat16
                )
                if n == 0:
                    for start in range(0, D, TILE):
                        width = min(TILE, D - start)
                        turned = turn(queries[own, start : start + TILE], cos_tile, sin_tile)
                        query_ref[own, start : start + width] = (
                            (turned * HEAD ** (-0.5)).astype(jnp.bfloat16)[:, :width]
                        )

    outs = [((row_count, D), jnp.bfloat16), ((chips, row_count, 2 * KV_WIDTH), jnp.bfloat16)]
    if direct:
        outs += [((D, columns_all), jnp.bfloat16), ((D, D), jnp.bfloat16)]
    result = run_kernel(
        kernel, outs, [table, hidden_half, cos_all, sin_all, *first], scalars=1, microseconds=5
    )
    return result if direct else (*result, *first)


def natural_order(out, table_ref, halves):
    chip, core = rank()
    chips, row_count, _ = halves[0].shape
    block_len = row_count // 2
    for a in range(2):
        for n in range(chips):
            block = table_ref[(chip ^ n) * 2 + (core ^ a)]
            for part, place in ((0, block), (1, 4 * chips - 1 - block)):
                rows = pl.ds(pl.multiple_of(place * block_len, block_len), block_len)
                out[rows, :] = halves[a][n, part * block_len : (part + 1) * block_len, :]


def heads_to_rows(values, group):
    return jnp.concatenate(
        [
            values[:, (group * GROUPS + i) * HEAD : (group * GROUPS + i + 1) * HEAD]
            for i in range(GROUPS)
        ],
        axis=0,
    )


def attention_forward(bounds, table, query_rot, pair_halves, first_key, last_key):
    row_count = query_rot.shape[0]
    block_len = row_count // 2
    wide = GROUPS * block_len

    def kernel(
        bounds_ref,
        table_ref,
        query_ref,
        own_ref,
        other_ref,
        first_ref,
        last_ref,
        out_ref,
        log_ref,
        pairs_ref,
    ):
        natural_order(pairs_ref, table_ref, (own_ref, other_ref))
        for b in range(2):
            rows = slice(b * block_len, (b + 1) * block_len)
            query_block = query_ref[rows, :]
            queries = [heads_to_rows(query_block, g) for g in range(KV_HEADS)]
            first = jnp.concatenate([first_ref[b : b + 1, :]] * GROUPS, axis=1)
            last = jnp.concatenate([last_ref[b : b + 1, :]] * GROUPS, axis=1)

            def step(j, state):
                start = pl.multiple_of(j * row_count, row_count)
                pos = start + lax.broadcasted_iota(jnp.int32, (row_count, wide), 0)
                visible = (pos >= first) & (pos <= last)
                result = []
                for g in range(KV_HEADS):
                    top, total, acc = state[g]
                    key_piece = pairs_ref[pl.ds(start, row_count), g * HEAD : (g + 1) * HEAD]
                    value_piece = pairs_ref[
                        pl.ds(start, row_count), KV_WIDTH + g * HEAD : KV_WIDTH + (g + 1) * HEAD
                    ]
                    scores = jnp.where(visible, dot_nt(key_piece, queries[g]), -1e30)
                    new_top = jnp.maximum(top, jnp.max(scores, axis=0, keepdims=True))
                    weights = jnp.exp(scores - new_top)
                    rescale = jnp.exp(top - new_top)
                    total = total * rescale + jnp.sum(weights, axis=0, keepdims=True)
                    acc = acc * rescale + dot_tn(value_piece, weights.astype(jnp.bfloat16))
                    result.append((new_top, total, acc))
                return tuple(result)

            state = lax.fori_loop(
                bounds_ref[2 * b],
                bounds_ref[2 * b + 1],
                step,
                tuple(
                    (
                        jnp.full((1, wide), -1e30, jnp.float32),
                        jnp.zeros((1, wide), jnp.float32),
                        jnp.zeros((HEAD, wide), jnp.float32),
                    )
                    for _ in range(KV_HEADS)
                ),
            )
            parts = []
            for g in range(KV_HEADS):
                top, total, acc = state[g]
                part = (acc / total).T
                parts += [part[i * block_len : (i + 1) * block_len] for i in range(GROUPS)]
                n = b * KV_HEADS + g
                log_ref[n : n + 1, :] = top + jnp.log(total)
            out_ref[rows, :] = jnp.concatenate(parts, axis=1)

    return run_kernel(
        kernel,
        [((row_count, D), jnp.float32), ((2 * KV_HEADS, wide), jnp.float32)],
        [bounds, table, query_rot, *pair_halves, first_key, last_key],
        scalars=2,
        scratch=[pltpu.VMEM((table.shape[0] * row_count, 2 * KV_WIDTH), jnp.bfloat16)],
        microseconds=12,
    )


def mix(attended, tokens, out_w, gain):
    row_count = tokens.shape[0]

    def kernel(
        attended_ref, tokens_ref, out_w_ref, gain_ref, residual_ref, hidden_ref
    ):
        attn_low = attended_ref[...].astype(jnp.bfloat16)
        residual = tokens_ref[...].astype(jnp.float32) + dot(attn_low, out_w_ref[...])
        residual_ref[...] = residual
        hidden_ref[...] = ((residual * inverse_root(residual)) * gain_ref[...]).astype(jnp.bfloat16)

    return run_kernel(
        kernel,
        [((row_count, D), jnp.float32), ((row_count, D), jnp.bfloat16)],
        [attended, tokens, out_w, gain],
        microseconds=2,
    )


def feed_forward(direct, hidden, hidden_other, grad_out, grad_other, wide, low_own, ff, shards):
    row_count = hidden.shape[0]
    width = ff // 2
    chips = lax.axis_size("ctx") // 2
    lanes = ff // chips
    rows = D // shards
    down_rows = ff // shards
    half = shards // 2
    steps = 2
    chunk = width // steps
    slice_rows = down_rows // (2 * chips)
    pile = rows // slice_rows

    def kernel(hidden_ref, hidden_other_ref, grad_ref, grad_other_ref, low_ref, *refs):
        wide_refs, refs = refs[: len(wide)], refs[len(wide) :]
        out_ref, hidden_grad_ref, sent_ref = refs[:3]
        wide_grads = refs[3 : 3 + (chips if direct else 2)]
        wide_ref, gate_grad_ref, down_ref, low_ref_f32 = refs[-4:]
        chip, _ = rank()
        for n in range(half):
            down_ref[n * down_rows : (n + 1) * down_rows, :] = low_ref[n]
        if direct:
            for i in range(chips):
                q = chip ^ i
                columns = pl.ds(pl.multiple_of((q % (chips // 2)) * lanes, TILE), lanes)
                wide_ref[q // (chips // 2), :, columns] = wide_refs[i][...].reshape(D, lanes)
        else:
            for kind in range(2):
                wide_ref[kind] = wide_refs[kind][...]
        hidden_all = jnp.concatenate([hidden_ref[...], hidden_other_ref[...]], axis=0)
        grad_all = jnp.concatenate([grad_ref[...], grad_other_ref[...]], axis=0)
        hidden_t = hidden_all.T
        result = jnp.zeros((2 * row_count, D), jnp.float32)
        grad_hidden = jnp.zeros((2 * row_count, D), jnp.float32)
        for j in range(steps):
            columns = slice(j * chunk, (j + 1) * chunk)
            gate_w, up_w = wide_ref[0, :, columns], wide_ref[1, :, columns]
            down_w = down_ref[columns, :]
            gate_value, up_value = dot(hidden_all, gate_w), dot(hidden_all, up_w)
            sigmoid = 1.0 / (1.0 + jnp.exp(-gate_value))
            silu = gate_value * sigmoid
            activation = (silu * up_value).astype(jnp.bfloat16)
            result += dot(activation, down_w)
            grad_activation = dot_nt(grad_all, down_w)
            grad_gate = (
                grad_activation * up_value * sigmoid * (1.0 + gate_value * (1.0 - sigmoid))
            ).astype(jnp.bfloat16)
            grad_up = (grad_activation * silu).astype(jnp.bfloat16)
            grad_hidden += dot_nt(grad_gate, gate_w) + dot_nt(grad_up, up_w)
            gate_grad_ref[0, :, columns] = grad_gate
            gate_grad_ref[1, :, columns] = grad_up
            low = dot(activation.T, grad_all)
            if direct:
                low_ref_f32[...] = low
                for i in range(chips):
                    for g in range(2):
                        start = pl.multiple_of(((chip ^ i) * 2 + g) * slice_rows, 16)
                        part = low_ref_f32[pl.ds(start, slice_rows), :].astype(jnp.bfloat16)
                        wide_grads[i][2 * j + g, :, lanes:] = stack_down(part, pile)
            else:
                refs[5][columns, :] = low.astype(jnp.bfloat16)
        out_ref[...] = result[:row_count]
        hidden_grad_ref[...] = grad_hidden[:row_count]
        sent_ref[:, :, D:] = jnp.zeros((2, row_count, -D % TILE), jnp.bfloat16)
        sent_ref[0, :, :D] = result[row_count:].astype(jnp.bfloat16)
        sent_ref[1, :, :D] = grad_hidden[row_count:].astype(jnp.bfloat16)
        if direct:
            for i in range(chips):
                q = chip ^ i
                columns = pl.ds(pl.multiple_of((q % (chips // 2)) * lanes, TILE), lanes)
                operand = gate_grad_ref[q // (chips // 2), :, columns]
                wide_grads[i][:, :, :lanes] = (
                    dot(hidden_t, operand).astype(jnp.bfloat16).reshape(shards, rows, lanes)
                )
        else:
            for kind in range(2):
                wide_grads[kind][...] = dot(hidden_t, gate_grad_ref[kind]).astype(jnp.bfloat16)

    outs = [
        ((row_count, D), jnp.float32),
        ((row_count, D), jnp.float32),
        ((2, row_count, -(-D // TILE) * TILE), jnp.bfloat16),
    ]
    outs += (
        [((shards, rows, lanes + D // pile), jnp.bfloat16)] * chips
        if direct
        else [((D, width), jnp.bfloat16)] * 2 + [((width, D), jnp.bfloat16)]
    )
    return run_kernel(
        kernel,
        outs,
        [hidden, hidden_other, grad_out, grad_other, low_own, *wide],
        scratch=[
            pltpu.VMEM((2, D, width), jnp.bfloat16),
            pltpu.VMEM((2, 2 * row_count, width), jnp.bfloat16),
            pltpu.VMEM((width, D), jnp.bfloat16),
            pltpu.VMEM((chunk, D), jnp.float32),
        ],
        microseconds=12,
    )


def unmix(
    residual, out_kept, grad_kept, received, grad_out, attended, out_w, gain
):
    row_count = residual.shape[0]

    def kernel(
        residual_ref,
        out_kept_ref,
        grad_kept_ref,
        received_ref,
        grad_out_ref,
        attended_ref,
        out_w_ref,
        gain_ref,
        output_ref,
        residual_grad_ref,
        attended_grad_ref,
        out_grad_ref,
    ):
        residual = residual_ref[...]
        result = residual + out_kept_ref[...] + received_ref[0, :, :D].astype(jnp.float32)
        output_ref[...] = result.astype(jnp.bfloat16).T
        grad_hidden = grad_kept_ref[...] + received_ref[1, :, :D].astype(jnp.float32)
        inv_two = inverse_root(residual)
        residual_grad = grad_out_ref[...].astype(jnp.float32) + norm_back(
            grad_hidden, residual * inv_two, inv_two, gain_ref[...]
        )
        residual_grad_ref[...] = residual_grad
        grad_branch = residual_grad.astype(jnp.bfloat16)
        attended_grad_ref[...] = dot_nt(grad_branch, out_w_ref[...]).astype(jnp.bfloat16)
        out_grad_ref[...] = dot_tn(
            attended_ref[...].astype(jnp.bfloat16), grad_branch
        ).astype(jnp.bfloat16)

    return run_kernel(
        kernel,
        [
            ((D, row_count), jnp.bfloat16),
            ((row_count, D), jnp.float32),
            ((row_count, D), jnp.bfloat16),
            ((D, D), jnp.bfloat16),
        ],
        [
            residual,
            out_kept,
            grad_kept,
            received,
            grad_out,
            attended,
            out_w,
            gain,
        ],
        microseconds=4,
    )


def attention_backward(
    bounds,
    table,
    query_rot,
    pair_halves,
    first_key,
    last_key,
    log_total,
    attended,
    grad_attended,
    cos_all,
    sin_all,
    cos_own,
    sin_own,
    hidden_half,
):
    row_count = query_rot.shape[0]
    block_len = row_count // 2
    wide = GROUPS * block_len
    slots = table.shape[0]
    chips = slots // 2
    half = HEAD // 2

    def kernel(
        bounds_ref,
        table_ref,
        query_ref,
        own_ref,
        other_ref,
        first_ref,
        last_ref,
        log_ref,
        attended_ref,
        grad_ref,
        cos_ref,
        sin_ref,
        cos_own_ref,
        sin_own_ref,
        hidden_ref,
        query_grad_ref,
        query_w_ref,
        kept_ref,
        *refs,
    ):
        sent_refs = refs[:chips]
        pairs_ref, pair_grad_ref, query_t_ref = refs[chips:]
        natural_order(pairs_ref, table_ref, (own_ref, other_ref))
        pair_grad_ref[...] = jnp.zeros_like(pair_grad_ref)
        for b in range(2):
            rows = slice(b * block_len, (b + 1) * block_len)
            query_block = query_ref[rows, :]
            grad_block = grad_ref[rows, :]
            product = grad_block.astype(jnp.float32) * attended_ref[rows, :]
            queries = [heads_to_rows(query_block, g) for g in range(KV_HEADS)]
            grads = [heads_to_rows(grad_block, g) for g in range(KV_HEADS)]
            deltas = [
                jnp.sum(heads_to_rows(product, g).T, axis=0, keepdims=True)
                for g in range(KV_HEADS)
            ]
            first = jnp.concatenate([first_ref[b : b + 1, :]] * GROUPS, axis=1)
            last = jnp.concatenate([last_ref[b : b + 1, :]] * GROUPS, axis=1)

            def step(j, state):
                start = pl.multiple_of(j * row_count, row_count)
                pos = start + lax.broadcasted_iota(jnp.int32, (row_count, wide), 0)
                visible = (pos >= first) & (pos <= last)
                result = []
                key_grads = []
                value_grads = []
                for g in range(KV_HEADS):
                    key_piece = pairs_ref[pl.ds(start, row_count), g * HEAD : (g + 1) * HEAD]
                    value_piece = pairs_ref[
                        pl.ds(start, row_count), KV_WIDTH + g * HEAD : KV_WIDTH + (g + 1) * HEAD
                    ]
                    n = b * KV_HEADS + g
                    scores = dot_nt(key_piece, queries[g])
                    weights = jnp.where(visible, jnp.exp(scores - log_ref[n : n + 1, :]), 0.0)
                    weight_grad = dot_nt(value_piece, grads[g])
                    score_grad = (weights * (weight_grad - deltas[g])).astype(jnp.bfloat16)
                    value_grads.append(dot(weights.astype(jnp.bfloat16), grads[g]))
                    key_grads.append(dot(score_grad, queries[g]))
                    result.append(state[g] + dot_tn(key_piece, score_grad))
                pair_grad_ref[pl.ds(start, row_count), :] += jnp.concatenate(
                    key_grads + value_grads, axis=1
                )
                return tuple(result)

            state = lax.fori_loop(
                bounds_ref[2 * b],
                bounds_ref[2 * b + 1],
                step,
                tuple(jnp.zeros((HEAD, wide), jnp.float32) for _ in range(KV_HEADS)),
            )
            cos_part, sin_part = cos_own_ref[:, rows], sin_own_ref[:, rows]
            for g in range(KV_HEADS):
                for i in range(GROUPS):
                    part = state[g][:, i * block_len : (i + 1) * block_len]
                    top, bottom = part[:half], part[half:]
                    h = (g * GROUPS + i) * HEAD
                    query_t_ref[h : h + half, rows] = (
                        (top * cos_part + bottom * sin_part) * HEAD ** (-0.5)
                    ).astype(jnp.bfloat16)
                    query_t_ref[h + half : h + HEAD, rows] = (
                        (bottom * cos_part - top * sin_part) * HEAD ** (-0.5)
                    ).astype(jnp.bfloat16)

        query_grad_ref[...] = query_t_ref[...].T
        query_w_ref[...] = dot(query_t_ref[...], hidden_ref[0]).T.astype(jnp.bfloat16)
        chip, core = rank()
        for i in range(chips):
            for ref, to_core in ((kept_ref.at[i], core), (sent_refs[i], 1 - core)):
                block = table_ref[(chip ^ i) * 2 + to_core]
                for part, place in ((0, block), (1, 2 * slots - 1 - block)):
                    source = pl.ds(pl.multiple_of(place * block_len, block_len), block_len)
                    ref[part * block_len : (part + 1) * block_len, :] = turn_pairs(
                        pair_grad_ref[source, :], cos_ref[source, :], -sin_ref[source, :]
                    ).astype(jnp.bfloat16)

    half_shape = ((chips, row_count, 2 * KV_WIDTH), jnp.bfloat16)
    return run_kernel(
        kernel,
        [((row_count, D), jnp.bfloat16), ((D, D), jnp.bfloat16), half_shape]
        + [((row_count, 2 * KV_WIDTH), jnp.bfloat16)] * chips,
        [
            bounds,
            table,
            query_rot,
            *pair_halves,
            first_key,
            last_key,
            log_total,
            attended,
            grad_attended,
            cos_all,
            sin_all,
            cos_own,
            sin_own,
            hidden_half,
        ],
        scalars=2,
        scratch=[
            pltpu.VMEM((slots * row_count, 2 * KV_WIDTH), jnp.bfloat16),
            pltpu.VMEM((slots * row_count, 2 * KV_WIDTH), jnp.float32),
            pltpu.VMEM((D, row_count), jnp.bfloat16),
        ],
        microseconds=18,
    )


def first_gradients(direct, kept, received, hidden_half, query_w, out_grad, shards):
    chips, row_count, _ = kept.shape
    rest = D - HEAD
    columns_all = 2 * KV_WIDTH + D + HEAD
    rows = D // shards

    def kernel(kept_ref, hidden_ref, query_w_ref, out_grad_ref, *refs):
        received_refs, refs = refs[:chips], refs[chips:]
        pair_refs, outs = refs[:chips], refs[chips:-1]
        mixed_ref = refs[-1]
        total = jnp.zeros((2 * KV_WIDTH, D), jnp.float32)
        for i in range(chips):
            pairs = (
                kept_ref[i].astype(jnp.float32) + received_refs[i][...].astype(jnp.float32)
            ).astype(jnp.bfloat16)
            if direct:
                for n in range(2 * KV_WIDTH // TILE):
                    pair_refs[i][n * row_count : (n + 1) * row_count, :] = pairs[
                        :, n * TILE : (n + 1) * TILE
                    ]
            else:
                pair_refs[i][...] = pairs
            total += dot_tn(pairs, hidden_ref[i])
        mixed_ref[:, : 2 * KV_WIDTH] = total.T.astype(jnp.bfloat16)
        mixed_ref[:, 2 * KV_WIDTH : 2 * KV_WIDTH + D] = query_w_ref[...]
        mixed_ref[:, 2 * KV_WIDTH + D :] = out_grad_ref[:, rest:]
        if not direct:
            outs[0][...] = mixed_ref[...]
            return
        chip, core = rank()
        for n in range(2 * chips):
            c = (chip ^ (n % chips)) * 2 + (core ^ (n // chips))
            part = mixed_ref[:, pl.ds(pl.multiple_of(c * TILE, TILE), TILE)]
            tile = out_grad_ref[:, pl.ds(pl.multiple_of((c // 2) * TILE, TILE), TILE)]
            unit = jnp.where(c % 2 == 0, tile[:, : TILE // 2], tile[:, TILE // 2 :])
            for z in range(shards):
                outs[n][z, :rows, :] = part[z * rows : (z + 1) * rows]
                middle = z * rows + rows // 2
                outs[n][z, rows:, : TILE // 2] = unit[z * rows : middle]
                outs[n][z, rows:, TILE // 2 :] = unit[middle : (z + 1) * rows]

    tiles = 2 * KV_WIDTH // TILE if direct else 1
    outs = [((row_count * tiles, 2 * KV_WIDTH // tiles), jnp.bfloat16)] * chips
    outs += (
        [((shards, rows + rows // 2, TILE), jnp.bfloat16)] * (2 * chips)
        if direct
        else [((D, columns_all), jnp.bfloat16)]
    )
    result = run_kernel(
        kernel,
        outs,
        [kept, hidden_half, query_w, out_grad, *received],
        scratch=[pltpu.VMEM((D, columns_all), jnp.bfloat16)],
        microseconds=0,
    )
    return result[:chips], result[chips:]


def local(
    layer_input,
    slot_table,
    seq_ids,
    w_query,
    w_key,
    w_value,
    w_out,
    w_gate,
    w_up,
    w_down,
    attn_gain,
    ffn_gain,
    cotangent,
):
    count = lax.axis_size("ctx")
    chips = count // 2
    index = lax.axis_index("ctx")
    chip, core = rank()
    shards = lax.axis_size("fsdp")
    rows, ff = w_gate.shape
    row_count = layer_input.shape[1]
    block_len = row_count // 2
    length = row_count * count
    direct = (
        rows % 16 == 0 and (ff // chips) % TILE == 0 and count * TILE == D + 2 * KV_WIDTH + HEAD
    )

    mixed_shard = jnp.concatenate(
        [w_key, w_value, w_query, w_out[:, D - HEAD :]], axis=1
    )
    piece = first_piece(mixed_shard, index, count)
    unit = first_piece(w_out[:, : D - HEAD], index, count)
    unit = jnp.concatenate([unit[: rows // 2], unit[rows // 2 :]], axis=1)
    gains = jnp.concatenate([attn_gain, ffn_gain])
    gains = jnp.pad(gains, (0, 16 * piece.shape[1] - 2 * rows)).reshape(16, piece.shape[1])
    tokens_low = layer_input[0]
    token_pieces = [tokens_low] + [chip_swap(tokens_low, i) for i in range(1, chips)]
    first_rows = gather_rows(jnp.concatenate([piece, unit, gains], axis=0))
    gains_all = first_rows[:, rows + rows // 2 :].reshape(shards, -1).astype(jnp.float32)
    gain_one = gains_all[:, :rows].reshape(1, D)
    gain_two = gains_all[:, rows : 2 * rows].reshape(1, D)
    hidden_half = normalize(token_pieces, gain_one)
    first_own = gather_same_core(after(first_rows, hidden_half))
    wide_own, wide_received = start_gather_rows(
        wide_piece(w_gate, w_up, chip, core, chips), first_rows
    )
    low_start = start_gather_half(after(w_down, hidden_half))
    first_pieces = first_own + [core_swap(v) for v in first_own]
    if direct:
        first = first_pieces
    else:
        ordered = in_rank_order(first_pieces)
        mixed_all = jnp.concatenate([v[:, :rows].reshape(D, -1) for v in ordered], axis=1)
        units = [
            v[:, rows : rows + rows // 2]
            .reshape(shards, rows // 2, 2, -1)
            .transpose(0, 2, 1, 3)
            .reshape(D, -1)
            for v in ordered
        ]
        first = [mixed_all, jnp.concatenate([*units, mixed_all[:, 2 * KV_WIDTH + D :]], axis=1)]

    own_block = lax.dynamic_index_in_dim(slot_table, index, 0, keepdims=False)
    own_blocks = jnp.stack([own_block, 2 * count - 1 - own_block])
    block_pos = own_blocks[:, None] * block_len + jnp.arange(block_len, dtype=jnp.int32)[None, :]
    documents = seq_ids[0]
    query_doc = jnp.stack(
        [
            lax.dynamic_slice(documents, (own_blocks[i] * block_len,), (block_len,))
            for i in range(2)
        ]
    )
    first_key = jnp.sum(
        (documents[None, :, None] < query_doc[:, None, :]).astype(jnp.int32), axis=1
    )
    bounds = jnp.stack(
        [jnp.min(first_key, axis=1) // row_count, own_blocks // 2 + 1], axis=1
    ).reshape(4)
    half_width = after(jnp.arange(HEAD // 2, dtype=jnp.float32), hidden_half)
    frequencies = rope_base ** (-(half_width * 2.0 / HEAD))
    angles = jnp.arange(length, dtype=jnp.int32).astype(jnp.float32)[:, None] * frequencies[None, :]
    cos_all = jnp.tile(jnp.cos(angles), (1, 2 * TILE // HEAD))
    sin_all = jnp.tile(jnp.sin(angles), (1, 2 * TILE // HEAD))
    own_angles = frequencies[:, None] * block_pos.reshape(1, row_count).astype(jnp.float32)
    cos_own, sin_own = jnp.cos(own_angles), jnp.sin(own_angles)

    wide_rows = in_order(wide_own, wide_received, shards // 2)
    query_rot, own_pairs, mixed, out_w_all = project(
        direct, slot_table, after(hidden_half, wide_rows, low_start, bounds, first_key, block_pos, cos_own, sin_own), first, cos_all, sin_all
    )
    pair_halves = (own_pairs, core_swap(own_pairs))
    wide_pieces = gather_same_core(wide_rows)
    low_own = finish_gather_half(after(low_start, wide_rows))
    grad_out = cotangent[0]
    attended, log_total = attention_forward(
        bounds, slot_table, query_rot, pair_halves, first_key, block_pos
    )
    grad_other = core_swap(after(grad_out, attended))
    residual, hidden_two = mix(attended, tokens_low, out_w_all, gain_two)
    if direct:
        wide = wide_pieces
    else:
        whole = [v.reshape(D, -1) for v in by_owner(wide_pieces, chip)]
        wide = [jnp.concatenate(whole[n : n + chips // 2], axis=1) for n in (0, chips // 2)]
    out_kept, grad_kept, sent, *wide_grads = feed_forward(
        direct,
        hidden_two,
        core_swap(hidden_two),
        grad_out,
        grad_other,
        wide,
        low_own,
        ff,
        shards,
    )
    lanes = ff // chips
    slice_rows = w_down.shape[0] // count
    pile = rows // slice_rows
    if not direct:
        gate_grad, up_grad, down_grad = wide_grads
        down_grad = down_grad.reshape(shards // 2, chips, 2, slice_rows, pile, D // pile)
        down_grad = down_grad.transpose(0, 2, 1, 4, 3, 5).reshape(shards, chips, rows, D // pile)
        wide_grads = [
            jnp.concatenate(
                [
                    lax.dynamic_slice_in_dim(
                        jnp.where(c < chips // 2, gate_grad, up_grad),
                        (c % (chips // 2)) * lanes,
                        lanes,
                        1,
                    ).reshape(shards, rows, lanes),
                    lax.dynamic_index_in_dim(down_grad, c, 1, keepdims=False),
                ],
                axis=2,
            )
            for c in (chip ^ i for i in range(chips))
        ]
    output, grad_residual, grad_attended, out_grad = unmix(
        residual,
        out_kept,
        grad_kept,
        core_swap(sent),
        grad_out,
        attended,
        out_w_all,
        gain_two,
    )

    grad_query, query_w, pairs_kept, *pairs_sent = attention_backward(
        bounds,
        slot_table,
        query_rot,
        pair_halves,
        first_key,
        block_pos,
        log_total,
        attended,
        grad_attended,
        cos_all,
        sin_all,
        cos_own,
        sin_own,
        hidden_half,
    )
    pairs_received = [core_swap(v) for v in pairs_sent]
    pair_sums, mixed_grads = first_gradients(
        direct, pairs_kept, pairs_received, hidden_half, query_w, out_grad, shards
    )
    if not direct:
        targets = [(chip ^ i) * 2 + (core ^ a) for a in range(2) for i in range(chips)]
        units = [
            first_piece(out_grad[:, : D - HEAD], c, count)
            .reshape(shards, 2, rows // 2, -1)
            .transpose(0, 2, 1, 3)
            .reshape(shards, rows // 2, -1)
            for c in targets
        ]
        mixed_grads = [
            jnp.concatenate(
                [first_piece(mixed_grads[0], c, count).reshape(shards, rows, -1), unit], axis=1
            )
            for c, unit in zip(targets, units)
        ]
    mixed_sums = [sum_cores(*pair) for pair in zip(mixed_grads[:chips], mixed_grads[chips:])]
    if direct:
        shape = mixed_sums[0].shape
        split = shape[0] * shape[1]
        both_sum = sum_chips(
            [
                jnp.concatenate([one.reshape(split, TILE), other], axis=0)
                for one, other in zip(mixed_sums, pair_sums)
            ]
        ).astype(jnp.bfloat16)
        first_sum = both_sum[:split].reshape(shape)
        owned = jnp.concatenate(jnp.split(both_sum[split:], 2 * KV_WIDTH // TILE), axis=1)
    else:
        first_sum = sum_chips(mixed_sums).astype(jnp.bfloat16)
        owned = sum_chips(pair_sums).astype(jnp.bfloat16)
    first_part = sum_rows(first_sum).astype(jnp.bfloat16)
    first_all = gather_chips(first_part)
    wide_sum = sum_chips(wide_grads, pair_sums[0]).astype(jnp.bfloat16)
    wide_sum = jnp.concatenate(
        [wide_sum[:, :, :lanes], by_core_slices(wide_sum[:, :, lanes:])], axis=2
    )
    wide_part = sum_rows(after(wide_sum, mixed_sums)).astype(jnp.bfloat16)
    wide_all = gather_chips(wide_part)
    grad_hidden_one = dot_nt(
        jnp.concatenate([owned, grad_query], axis=1), mixed[:, : 2 * KV_WIDTH + D]
    )
    tokens = tokens_low.astype(jnp.float32)
    inv_one = inverse_root(tokens)
    grad_input = (
        grad_residual + norm_back(grad_hidden_one, tokens * inv_one, inv_one, gain_one)
    ).astype(jnp.bfloat16)

    gain_rows = [v.astype(jnp.float32).reshape(1, rows) for v in (attn_gain, ffn_gain)]
    if direct:
        gate_grad, up_grad, down_grad, gain_grad_two = finish_wide(
            wide_all, w_gate, w_up, gain_rows[1], pile
        )
        down_grad = down_grad.T
        query_w, key_w, value_w, out_w, gain_grad_one = finish_first(
            first_all, mixed_shard, gain_rows[0]
        )
    else:
        own, other = by_owner(wide_all[:chips], chip), by_owner(wide_all[chips:], chip)
        cores = both_cores(jnp.stack(own), jnp.stack(other), core)
        down_grad = jnp.concatenate(
            [unstack_down(cores[c % 2][c // 2][:, lanes:], pile) for c in range(count)]
        ).astype(jnp.float32)
        gate_grad, up_grad = (
            jnp.concatenate(
                [cores[k][n + q][:, :lanes] for k in range(2) for q in range(chips // 2)], axis=1
            ).astype(jnp.float32)
            for n in (0, chips // 2)
        )
        ordered = in_rank_order(first_all)
        first_grad = jnp.concatenate([v[:rows] for v in ordered], axis=1).astype(jnp.float32)
        units = [
            v[rows:].reshape(rows // 2, 2, -1).transpose(1, 0, 2).reshape(rows, -1) for v in ordered
        ]
        key_w, value_w, query_w, last = jnp.split(
            first_grad, [KV_WIDTH, 2 * KV_WIDTH, 2 * KV_WIDTH + D], axis=1
        )
        out_w = jnp.concatenate([*[v.astype(jnp.float32) for v in units], last], axis=1)
        used = 2 * KV_WIDTH + D
        gain_grad_one = (
            jnp.sum(
                first_grad[:, :used] * mixed_shard[:, :used].astype(jnp.float32),
                axis=1,
            )
            / gain_rows[0]
        )
        gain_grad_two = (
            jnp.sum(
                gate_grad * w_gate.astype(jnp.float32) + up_grad * w_up.astype(jnp.float32),
                axis=1,
            )
            / gain_rows[1]
        )
    return (
        output.T[None],
        grad_input[None],
        query_w,
        key_w,
        value_w,
        out_w,
        gate_grad,
        up_grad,
        down_grad,
        gain_grad_one.reshape(rows),
        gain_grad_two.reshape(rows),
    )


def solution(mesh):
    placed = (
        P("fsdp", "ctx", None),
        P(),
        P("fsdp", None),
        P("fsdp", None),
        P("fsdp", None),
        P("fsdp", None),
        P("fsdp", None),
        P("fsdp", None),
        P("fsdp", None),
        P("fsdp", None),
        P("fsdp"),
        P("fsdp"),
        P("fsdp", "ctx", None),
    )
    return jax.shard_map(
        local,
        mesh=mesh,
        in_specs=placed,
        out_specs=(
            P("fsdp", "ctx", None),
            P("fsdp", "ctx", None),
            P("fsdp", None),
            P("fsdp", None),
            P("fsdp", None),
            P("fsdp", None),
            P("fsdp", None),
            P("fsdp", None),
            P("fsdp", None),
            P("fsdp"),
            P("fsdp"),
        ),
        check_vma=False,
    )
```

```python
import jax
import jax.numpy as jnp
from jax import lax
from jax.experimental import pallas as pl
from jax.experimental.pallas import tpu as pltpu
from jax.sharding import PartitionSpec as P

D = 576
HEADS = 9
KV_HEADS = 3
HEAD = 64
GROUPS = HEADS // KV_HEADS
KV_WIDTH = KV_HEADS * HEAD
TILE = 128
DOCS = 4

epsilon = 1e-05
rope_base = 100000.0

VMEM = pl.BlockSpec(memory_space=pltpu.VMEM)
SMEM = pl.BlockSpec(memory_space=pltpu.SMEM)


def run_kernel(kernel, out_shapes, inputs, scalars=0, scratch=(), microseconds=1):
    return pl.pallas_call(
        kernel,
        out_shape=tuple(jax.ShapeDtypeStruct(*out) for out in out_shapes),
        in_specs=[SMEM] * scalars + [VMEM] * (len(inputs) - scalars),
        out_specs=tuple(VMEM for _ in out_shapes),
        scratch_shapes=list(scratch),
        compiler_params=pltpu.CompilerParams(vmem_limit_bytes=60 * 1024 * 1024),
        cost_estimate=pl.CostEstimate(
            flops=microseconds * 1150 * 10**6, bytes_accessed=1024, transcendentals=0
        ),
    )(*inputs)


def rank():
    index = lax.axis_index("ctx")
    return index // 2, index % 2


def swap(value, axis, offset):
    count = lax.axis_size(axis)
    return lax.ppermute(value, axis, [(i, i ^ offset) for i in range(count)])


def chip_swap(value, offset):
    return swap(value, "ctx", 2 * offset)


def core_swap(value):
    return swap(value, "ctx", 1)


def by_owner(pieces, index):
    bit = 1
    while bit < len(pieces):
        flag = (index & bit) != 0
        pieces = [jnp.where(flag, pieces[i ^ bit], pieces[i]) for i in range(len(pieces))]
        bit = bit * 2
    return pieces


def in_order(own, other, offset):
    flag = (lax.axis_index("fsdp") & offset) != 0
    return jnp.concatenate([jnp.where(flag, other, own), jnp.where(flag, own, other)], axis=0)


def start_gather_rows(piece, *others):
    count = lax.axis_size("fsdp")
    values = piece[None]
    offset = 1
    while offset < count // 2:
        values = in_order(values, swap(values, "fsdp", offset), offset)
        offset = offset * 2
    values = after(values, *others)
    return values, swap(values, "fsdp", offset)


def gather_rows(piece, *others):
    count = lax.axis_size("fsdp")
    index = lax.axis_index("fsdp")
    values = piece[None]
    offset = 1
    while offset < count:
        if offset > 1 and others:
            values = after(values, *others)
        other = swap(values, "fsdp", offset)
        flag = (index & offset) != 0
        values = jnp.concatenate(
            [jnp.where(flag, other, values), jnp.where(flag, values, other)], axis=0
        )
        offset = offset * 2
    return values


def start_gather_half(piece):
    received = lax.ppermute(piece, ("ctx", "fsdp"), half_pairs())
    return jnp.where(in_half(), piece, received)[None]


def finish_gather_half(values):
    offset = 1
    while offset < lax.axis_size("fsdp") // 2:
        values = in_order(values, swap(values, "fsdp", offset), offset)
        offset = offset * 2
    return values


def gather_same_core(piece):
    return [piece] + [chip_swap(piece, i) for i in range(1, lax.axis_size("ctx") // 2)]


def gather_chips(piece):
    own = gather_same_core(piece)
    return own + [core_swap(value) for value in own]


def after(value, *others):
    return lax.optimization_barrier((value, others))[0]


def in_rank_order(pieces):
    chip, core = rank()
    chips = len(pieces) // 2
    own, other = by_owner(pieces[:chips], chip), by_owner(pieces[chips:], chip)
    ordered = [by_owner(list(pair), core) for pair in zip(own, other)]
    return [value for pair in ordered for value in pair]


def sum_cores(kept, sent):
    return (kept.astype(jnp.float32) + core_swap(sent).astype(jnp.float32)).astype(jnp.bfloat16)


def sum_chips(sums, *others):
    received = tuple(chip_swap(sums[i], i) for i in range(1, len(sums)))
    if others:
        received = after(received, *others)
    return sum((value.astype(jnp.float32) for value in received), sums[0].astype(jnp.float32))


def half_pairs():
    count = lax.axis_size("fsdp")
    half = count // 2
    return [
        (c * count + z, c * count + (z ^ half))
        for c in range(lax.axis_size("ctx"))
        for z in range(count)
        if z // half == c % 2
    ]


def in_half():
    half = lax.axis_size("fsdp") // 2
    return lax.axis_index("fsdp") // half == lax.axis_index("ctx") % 2


def sum_rows(values):
    count = lax.axis_size("fsdp")
    index = lax.axis_index("fsdp")

    def pick(offset):
        return lax.dynamic_index_in_dim(values, index ^ offset, 0, keepdims=False)

    total = pick(0).astype(jnp.float32)
    for i in range(1, count):
        total = total + swap(pick(i), "fsdp", i).astype(jnp.float32)
    return total


def first_piece(mixed, c, count):
    width = mixed.shape[1] // count
    return lax.dynamic_slice_in_dim(mixed, c * width, width, 1)


def wide_piece(gate, up, chip, core, chips):
    lanes = gate.shape[1] // chips
    q = chip % (chips // 2)
    wide = jnp.where(chip < chips // 2, gate, up)
    return lax.dynamic_slice_in_dim(wide, (core * (chips // 2) + q) * lanes, lanes, 1)


def stack_down(part, pile):
    width = D // pile
    return jnp.concatenate([part[:, n * width : (n + 1) * width] for n in range(pile)], axis=0)


def unstack_down(part, pile):
    rows = part.shape[0] // pile
    return jnp.concatenate([part[n * rows : (n + 1) * rows] for n in range(pile)], axis=1)


def by_core_slices(values):
    _, core = rank()
    values = values.reshape(-1, 2, *values.shape[1:])
    mine, theirs = (
        lax.dynamic_index_in_dim(values, side, 1, keepdims=False) for side in (core, 1 - core)
    )
    return jnp.concatenate(both_cores(mine, core_swap(theirs), core))


def both_cores(own, other, core):
    return jnp.where(core == 0, own, other), jnp.where(core == 0, other, own)


def gain_gradient(terms, gain_row):
    total = sum(terms[:, t : t + TILE] for t in range(0, terms.shape[1], TILE))
    return jnp.sum(total.T, axis=0, keepdims=True) / gain_row


def finish_first(pieces, shard, gain):
    count = len(pieces)
    chips = count // 2
    rows = shard.shape[0]
    used = 2 * KV_WIDTH + D

    def kernel(*refs):
        shard_ref, gain_ref = refs[count : count + 2]
        query, key, value, out, gain_grad, whole = refs[count + 2 :]
        chip, core = rank()
        for n in range(count):
            c = (chip ^ (n % chips)) * 2 + (core ^ (n // chips))
            whole[:, pl.ds(pl.multiple_of(c * TILE, TILE), TILE)] = refs[n][:rows, :].astype(
                jnp.float32
            )
        key[...] = whole[:, :KV_WIDTH]
        value[...] = whole[:, KV_WIDTH : 2 * KV_WIDTH]
        query[...] = whole[:, 2 * KV_WIDTH : used]
        for n in range(chips):
            columns = pl.ds(pl.multiple_of((chip ^ n) * TILE, TILE), TILE)
            pair = both_cores(
                refs[n][rows:, :].astype(jnp.float32),
                refs[n + chips][rows:, :].astype(jnp.float32),
                core,
            )
            for m in range(2):
                out[m * (rows // 2) : (m + 1) * (rows // 2), columns] = jnp.concatenate(
                    [part[:, m * (TILE // 2) : (m + 1) * (TILE // 2)] for part in pair], axis=1
                )
        out[:, chips * TILE :] = whole[:, used:]
        terms = whole[...] * shard_ref[...].astype(jnp.float32)
        lane = lax.broadcasted_iota(jnp.int32, terms.shape, 1)
        gain_grad[...] = gain_gradient(jnp.where(lane < used, terms, 0.0), gain_ref[...])

    return run_kernel(
        kernel,
        [
            ((rows, D), jnp.float32),
            ((rows, KV_WIDTH), jnp.float32),
            ((rows, KV_WIDTH), jnp.float32),
            ((rows, D), jnp.float32),
            ((1, rows), jnp.float32),
        ],
        [*pieces, shard, gain],
        microseconds=2,
        scratch=[pltpu.VMEM((rows, count * TILE), jnp.float32)],
    )


def finish_wide(pieces, w_gate, w_up, gain, pile):
    count = len(pieces)
    chips = count // 2
    rows, ff = w_gate.shape
    lanes = ff // chips
    down_rows = rows // pile
    low_lanes = D // pile

    def kernel(*refs):
        gate_ref, up_ref, gain_ref = refs[count : count + 3]
        gate, up, down, gain_grad, total, low = refs[count + 3 :]
        chip, core = rank()
        total[...] = jnp.zeros_like(total)
        for n in range(count):
            to_chip, to_core = chip ^ (n % chips), core ^ (n // chips)
            column = (to_core * (chips // 2) + to_chip % (chips // 2)) * lanes
            columns = pl.ds(pl.multiple_of(column, TILE), lanes)
            for kind, out, weight in ((0, gate, gate_ref), (1, up, up_ref)):

                @pl.when(to_chip // (chips // 2) == kind)
                def _():
                    part = refs[n][:, :lanes].astype(jnp.float32)
                    out[:, columns] = part
                    total[...] += part * weight[:, columns].astype(jnp.float32)

            start = pl.multiple_of((to_chip * 2 + to_core) * down_rows, 16)
            for m in range(pile):
                low[pl.ds(start, down_rows), m * low_lanes : (m + 1) * low_lanes] = refs[n][
                    m * down_rows : (m + 1) * down_rows, lanes:
                ].astype(jnp.float32)
        down[...] = low[...].T
        gain_grad[...] = gain_gradient(total[...], gain_ref[...])

    return run_kernel(
        kernel,
        [
            ((rows, ff), jnp.float32),
            ((rows, ff), jnp.float32),
            ((D, count * down_rows), jnp.float32),
            ((1, rows), jnp.float32),
        ],
        [*pieces, w_gate, w_up, gain],
        microseconds=4,
        scratch=[
            pltpu.VMEM((rows, lanes), jnp.float32),
            pltpu.VMEM((count * down_rows, D), jnp.float32),
        ],
    )


def dot(first_matrix, second_matrix):
    return jnp.dot(first_matrix, second_matrix, preferred_element_type=jnp.float32)


def dot_nt(first_matrix, second_matrix):
    return lax.dot_general(
        first_matrix, second_matrix, (((1,), (1,)), ((), ())), preferred_element_type=jnp.float32
    )


def dot_tn(first_matrix, second_matrix):
    return lax.dot_general(
        first_matrix, second_matrix, (((0,), (0,)), ((), ())), preferred_element_type=jnp.float32
    )


def norm_back(grad_normed, unit_rows, inv_root, gain_vec):
    scaled_grad = grad_normed * gain_vec
    return inv_root * (
        scaled_grad - unit_rows * jnp.mean(scaled_grad * unit_rows, axis=-1, keepdims=True)
    )


def inverse_root(rows):
    return lax.rsqrt(jnp.mean(rows * rows, axis=-1, keepdims=True) + epsilon)


def turn(values, cos_tile, sin_tile):
    lane = lax.broadcasted_iota(jnp.int32, values.shape, 1) % HEAD
    turned = jnp.where(
        lane < HEAD // 2,
        -pltpu.roll(values, TILE - HEAD // 2, 1),
        pltpu.roll(values, HEAD // 2, 1),
    )
    return values * cos_tile + turned * sin_tile


def turn_pairs(values, cos_tile, sin_tile):
    lane = lax.broadcasted_iota(jnp.int32, cos_tile.shape, 1)
    middle = values[:, TILE : 2 * TILE]
    return jnp.concatenate(
        [
            turn(values[:, :TILE], cos_tile, sin_tile),
            jnp.where(lane < HEAD, turn(middle, cos_tile, sin_tile), middle),
            values[:, 2 * TILE :],
        ],
        axis=1,
    )


def normalize(token_pieces, gain):
    row_count = token_pieces[0].shape[0]
    chips = len(token_pieces)

    def kernel(*refs):
        gain_ref, hidden_ref = refs[chips:]
        for n in range(chips):
            tokens = refs[n][...].astype(jnp.float32)
            hidden_ref[n] = ((tokens * inverse_root(tokens)) * gain_ref[...]).astype(jnp.bfloat16)

    return run_kernel(
        kernel, [((chips, row_count, D), jnp.bfloat16)], [*token_pieces, gain], microseconds=3
    )[0]


def project(direct, table, hidden_half, first, cos_all, sin_all):
    chips, row_count, _ = hidden_half.shape
    block_len = row_count // 2
    count = 2 * chips
    columns_all = count * TILE if direct else first[0].shape[1]
    shards = lax.axis_size("fsdp")
    rows = D // shards

    def kernel(table_ref, hidden_ref, cos_ref, sin_ref, *refs):
        first_refs = refs[: len(first)]
        query_ref, pairs_ref = refs[len(first) : len(first) + 2]
        chip, core = rank()
        if direct:
            mixed_ref, out_w_ref = refs[-2:]
            for n in range(count):
                c = (chip ^ (n % chips)) * 2 + (core ^ (n // chips))
                columns = pl.ds(pl.multiple_of(c * TILE, TILE), TILE)
                for z in range(shards):
                    mixed_ref[z * rows : (z + 1) * rows, columns] = first_refs[n][z, :rows, :]
            for n in range(chips):
                columns = pl.ds(pl.multiple_of((chip ^ n) * TILE, TILE), TILE)
                for z in range(shards):
                    pair = both_cores(
                        first_refs[n][z, rows : rows + rows // 2, :].astype(jnp.float32),
                        first_refs[n + chips][z, rows : rows + rows // 2, :].astype(jnp.float32),
                        core,
                    )
                    half = TILE // 2
                    block = jnp.concatenate(
                        [
                            jnp.concatenate([part[:, m * half : (m + 1) * half] for part in pair], axis=1)
                            for m in range(2)
                        ],
                        axis=0,
                    )
                    out_w_ref[z * rows : (z + 1) * rows, columns] = block.astype(jnp.bfloat16)
            out_w_ref[:, chips * TILE :] = mixed_ref[:, 2 * KV_WIDTH + D :]
        else:
            mixed_ref = first_refs[0]
        for n in range(chips):
            hidden = hidden_ref[n]
            pairs = dot(hidden, mixed_ref[:, : 2 * KV_WIDTH])
            block = table_ref[(chip ^ n) * 2 + core]
            queries = dot(hidden, mixed_ref[:, 2 * KV_WIDTH :]) if n == 0 else None
            for part, place in ((0, block), (1, 2 * count - 1 - block)):
                source = pl.ds(pl.multiple_of(place * block_len, block_len), block_len)
                own = slice(part * block_len, (part + 1) * block_len)
                cos_tile, sin_tile = cos_ref[source, :], sin_ref[source, :]
                pairs_ref[n, own, :] = turn_pairs(pairs[own], cos_tile, sin_tile).astype(
                    jnp.bfloat16
                )
                if n == 0:
                    for start in range(0, D, TILE):
                        width = min(TILE, D - start)
                        turned = turn(queries[own, start : start + TILE], cos_tile, sin_tile)
                        query_ref[own, start : start + width] = (
                            (turned * HEAD ** (-0.5)).astype(jnp.bfloat16)[:, :width]
                        )

    outs = [((row_count, D), jnp.bfloat16), ((chips, row_count, 2 * KV_WIDTH), jnp.bfloat16)]
    if direct:
        outs += [((D, columns_all), jnp.bfloat16), ((D, D), jnp.bfloat16)]
    result = run_kernel(
        kernel, outs, [table, hidden_half, cos_all, sin_all, *first], scalars=1, microseconds=5
    )
    return result if direct else (*result, *first)


def natural_order(out, table_ref, halves):
    chip, core = rank()
    chips, row_count, _ = halves[0].shape
    block_len = row_count // 2
    for a in range(2):
        for n in range(chips):
            block = table_ref[(chip ^ n) * 2 + (core ^ a)]
            for part, place in ((0, block), (1, 4 * chips - 1 - block)):
                rows = pl.ds(pl.multiple_of(place * block_len, block_len), block_len)
                out[rows, :] = halves[a][n, part * block_len : (part + 1) * block_len, :]


def heads_to_rows(values, group):
    return jnp.concatenate(
        [
            values[:, (group * GROUPS + i) * HEAD : (group * GROUPS + i + 1) * HEAD]
            for i in range(GROUPS)
        ],
        axis=0,
    )


def visible_keys(table_ref, docs_ref, b):
    count, block_len = docs_ref.shape
    chip, core = rank()
    block = table_ref[chip * 2 + core]
    block = block if b == 0 else count - 1 - block
    docs = docs_ref[...]
    own = docs_ref[pl.ds(block, 1), :]
    first = jnp.zeros((1, block_len), jnp.float32)
    for doc in range(1, DOCS):
        before = jnp.sum((docs < doc).astype(jnp.float32), axis=0, keepdims=True)
        start = jnp.sum(before, axis=1, keepdims=True)
        first = jnp.where(own == doc, start, first)
    begin = jnp.min(first).astype(jnp.int32) // (2 * block_len)
    first = first.astype(jnp.int32)
    last = block * block_len + lax.broadcasted_iota(jnp.int32, (1, block_len), 1)
    return (
        jnp.concatenate([first] * GROUPS, axis=1),
        jnp.concatenate([last] * GROUPS, axis=1),
        begin,
        block // 2 + 1,
    )


def attention_forward(table, docs, query_rot, pair_halves):
    row_count = query_rot.shape[0]
    block_len = row_count // 2
    wide = GROUPS * block_len

    def kernel(
        table_ref,
        docs_ref,
        query_ref,
        own_ref,
        other_ref,
        out_ref,
        log_ref,
        pairs_ref,
    ):
        natural_order(pairs_ref, table_ref, (own_ref, other_ref))
        for b in range(2):
            rows = slice(b * block_len, (b + 1) * block_len)
            query_block = query_ref[rows, :]
            queries = [heads_to_rows(query_block, g) for g in range(KV_HEADS)]
            first, last, begin, end = visible_keys(table_ref, docs_ref, b)

            def step(j, state):
                start = pl.multiple_of(j * row_count, row_count)
                pos = start + lax.broadcasted_iota(jnp.int32, (row_count, wide), 0)
                visible = (pos >= first) & (pos <= last)
                result = []
                for g in range(KV_HEADS):
                    top, total, acc = state[g]
                    key_piece = pairs_ref[pl.ds(start, row_count), g * HEAD : (g + 1) * HEAD]
                    value_piece = pairs_ref[
                        pl.ds(start, row_count), KV_WIDTH + g * HEAD : KV_WIDTH + (g + 1) * HEAD
                    ]
                    scores = jnp.where(visible, dot_nt(key_piece, queries[g]), -1e30)
                    new_top = jnp.maximum(top, jnp.max(scores, axis=0, keepdims=True))
                    weights = jnp.exp(scores - new_top)
                    rescale = jnp.exp(top - new_top)
                    total = total * rescale + jnp.sum(weights, axis=0, keepdims=True)
                    acc = acc * rescale + dot_tn(value_piece, weights.astype(jnp.bfloat16))
                    result.append((new_top, total, acc))
                return tuple(result)

            state = lax.fori_loop(
                begin,
                end,
                step,
                tuple(
                    (
                        jnp.full((1, wide), -1e30, jnp.float32),
                        jnp.zeros((1, wide), jnp.float32),
                        jnp.zeros((HEAD, wide), jnp.float32),
                    )
                    for _ in range(KV_HEADS)
                ),
            )
            parts = []
            for g in range(KV_HEADS):
                top, total, acc = state[g]
                part = (acc / total).T
                parts += [part[i * block_len : (i + 1) * block_len] for i in range(GROUPS)]
                n = b * KV_HEADS + g
                log_ref[n : n + 1, :] = top + jnp.log(total)
            out_ref[rows, :] = jnp.concatenate(parts, axis=1)

    return run_kernel(
        kernel,
        [((row_count, D), jnp.float32), ((2 * KV_HEADS, wide), jnp.float32)],
        [table, docs, query_rot, *pair_halves],
        scalars=1,
        scratch=[pltpu.VMEM((table.shape[0] * row_count, 2 * KV_WIDTH), jnp.bfloat16)],
        microseconds=12,
    )


def mix(attended, tokens, out_w, gain):
    row_count = tokens.shape[0]

    def kernel(
        attended_ref, tokens_ref, out_w_ref, gain_ref, residual_ref, hidden_ref
    ):
        attn_low = attended_ref[...].astype(jnp.bfloat16)
        residual = tokens_ref[...].astype(jnp.float32) + dot(attn_low, out_w_ref[...])
        residual_ref[...] = residual
        hidden_ref[...] = ((residual * inverse_root(residual)) * gain_ref[...]).astype(jnp.bfloat16)

    return run_kernel(
        kernel,
        [((row_count, D), jnp.float32), ((row_count, D), jnp.bfloat16)],
        [attended, tokens, out_w, gain],
        microseconds=2,
    )


def feed_forward(direct, hidden, hidden_other, grad_out, grad_other, wide, low_own, ff, shards):
    row_count = hidden.shape[0]
    width = ff // 2
    chips = lax.axis_size("ctx") // 2
    lanes = ff // chips
    rows = D // shards
    down_rows = ff // shards
    half = shards // 2
    steps = 2
    chunk = width // steps
    slice_rows = down_rows // (2 * chips)
    pile = rows // slice_rows

    def kernel(hidden_ref, hidden_other_ref, grad_ref, grad_other_ref, low_ref, *refs):
        wide_refs, refs = refs[: len(wide)], refs[len(wide) :]
        out_ref, hidden_grad_ref, sent_ref = refs[:3]
        wide_grads = refs[3 : 3 + (chips if direct else 2)]
        wide_ref, gate_grad_ref, down_ref, low_ref_f32 = refs[-4:]
        chip, _ = rank()
        for n in range(half):
            down_ref[n * down_rows : (n + 1) * down_rows, :] = low_ref[n]
        if direct:
            for i in range(chips):
                q = chip ^ i
                columns = pl.ds(pl.multiple_of((q % (chips // 2)) * lanes, TILE), lanes)
                wide_ref[q // (chips // 2), :, columns] = wide_refs[i][...].reshape(D, lanes)
        else:
            for kind in range(2):
                wide_ref[kind] = wide_refs[kind][...]
        hidden_all = jnp.concatenate([hidden_ref[...], hidden_other_ref[...]], axis=0)
        grad_all = jnp.concatenate([grad_ref[...], grad_other_ref[...]], axis=0)
        hidden_t = hidden_all.T
        result = jnp.zeros((2 * row_count, D), jnp.float32)
        grad_hidden = jnp.zeros((2 * row_count, D), jnp.float32)
        for j in range(steps):
            columns = slice(j * chunk, (j + 1) * chunk)
            gate_w, up_w = wide_ref[0, :, columns], wide_ref[1, :, columns]
            down_w = down_ref[columns, :]
            gate_value, up_value = dot(hidden_all, gate_w), dot(hidden_all, up_w)
            sigmoid = 1.0 / (1.0 + jnp.exp(-gate_value))
            silu = gate_value * sigmoid
            activation = (silu * up_value).astype(jnp.bfloat16)
            result += dot(activation, down_w)
            grad_activation = dot_nt(grad_all, down_w)
            grad_gate = (
                grad_activation * up_value * sigmoid * (1.0 + gate_value * (1.0 - sigmoid))
            ).astype(jnp.bfloat16)
            grad_up = (grad_activation * silu).astype(jnp.bfloat16)
            grad_hidden += dot_nt(grad_gate, gate_w) + dot_nt(grad_up, up_w)
            gate_grad_ref[0, :, columns] = grad_gate
            gate_grad_ref[1, :, columns] = grad_up
            low = dot(activation.T, grad_all)
            if direct:
                low_ref_f32[...] = low
                for i in range(chips):
                    for g in range(2):
                        start = pl.multiple_of(((chip ^ i) * 2 + g) * slice_rows, 16)
                        part = low_ref_f32[pl.ds(start, slice_rows), :].astype(jnp.bfloat16)
                        wide_grads[i][2 * j + g, :, lanes:] = stack_down(part, pile)
            else:
                refs[5][columns, :] = low.astype(jnp.bfloat16)
        out_ref[...] = result[:row_count]
        hidden_grad_ref[...] = grad_hidden[:row_count]
        sent_ref[:, :, D:] = jnp.zeros((2, row_count, -D % TILE), jnp.bfloat16)
        sent_ref[0, :, :D] = result[row_count:].astype(jnp.bfloat16)
        sent_ref[1, :, :D] = grad_hidden[row_count:].astype(jnp.bfloat16)
        if direct:
            for i in range(chips):
                q = chip ^ i
                columns = pl.ds(pl.multiple_of((q % (chips // 2)) * lanes, TILE), lanes)
                operand = gate_grad_ref[q // (chips // 2), :, columns]
                wide_grads[i][:, :, :lanes] = (
                    dot(hidden_t, operand).astype(jnp.bfloat16).reshape(shards, rows, lanes)
                )
        else:
            for kind in range(2):
                wide_grads[kind][...] = dot(hidden_t, gate_grad_ref[kind]).astype(jnp.bfloat16)

    outs = [
        ((row_count, D), jnp.float32),
        ((row_count, D), jnp.float32),
        ((2, row_count, -(-D // TILE) * TILE), jnp.bfloat16),
    ]
    outs += (
        [((shards, rows, lanes + D // pile), jnp.bfloat16)] * chips
        if direct
        else [((D, width), jnp.bfloat16)] * 2 + [((width, D), jnp.bfloat16)]
    )
    return run_kernel(
        kernel,
        outs,
        [hidden, hidden_other, grad_out, grad_other, low_own, *wide],
        scratch=[
            pltpu.VMEM((2, D, width), jnp.bfloat16),
            pltpu.VMEM((2, 2 * row_count, width), jnp.bfloat16),
            pltpu.VMEM((width, D), jnp.bfloat16),
            pltpu.VMEM((chunk, D), jnp.float32),
        ],
        microseconds=12,
    )


def unmix(
    residual, out_kept, grad_kept, received, grad_out, attended, out_w, gain
):
    row_count = residual.shape[0]

    def kernel(
        residual_ref,
        out_kept_ref,
        grad_kept_ref,
        received_ref,
        grad_out_ref,
        attended_ref,
        out_w_ref,
        gain_ref,
        output_ref,
        residual_grad_ref,
        attended_grad_ref,
        out_grad_ref,
    ):
        residual = residual_ref[...]
        result = residual + out_kept_ref[...] + received_ref[0, :, :D].astype(jnp.float32)
        output_ref[...] = result.astype(jnp.bfloat16).T
        grad_hidden = grad_kept_ref[...] + received_ref[1, :, :D].astype(jnp.float32)
        inv_two = inverse_root(residual)
        residual_grad = grad_out_ref[...].astype(jnp.float32) + norm_back(
            grad_hidden, residual * inv_two, inv_two, gain_ref[...]
        )
        residual_grad_ref[...] = residual_grad
        grad_branch = residual_grad.astype(jnp.bfloat16)
        attended_grad_ref[...] = dot_nt(grad_branch, out_w_ref[...]).astype(jnp.bfloat16)
        out_grad_ref[...] = dot_tn(
            attended_ref[...].astype(jnp.bfloat16), grad_branch
        ).astype(jnp.bfloat16)

    return run_kernel(
        kernel,
        [
            ((D, row_count), jnp.bfloat16),
            ((row_count, D), jnp.float32),
            ((row_count, D), jnp.bfloat16),
            ((D, D), jnp.bfloat16),
        ],
        [
            residual,
            out_kept,
            grad_kept,
            received,
            grad_out,
            attended,
            out_w,
            gain,
        ],
        microseconds=4,
    )


def attention_backward(
    table,
    docs,
    query_rot,
    pair_halves,
    log_total,
    attended,
    grad_attended,
    cos_all,
    sin_all,
    cos_own,
    sin_own,
    hidden_half,
):
    row_count = query_rot.shape[0]
    block_len = row_count // 2
    wide = GROUPS * block_len
    slots = table.shape[0]
    chips = slots // 2
    half = HEAD // 2

    def kernel(
        table_ref,
        docs_ref,
        query_ref,
        own_ref,
        other_ref,
        log_ref,
        attended_ref,
        grad_ref,
        cos_ref,
        sin_ref,
        cos_own_ref,
        sin_own_ref,
        hidden_ref,
        query_grad_ref,
        query_w_ref,
        kept_ref,
        *refs,
    ):
        sent_refs = refs[:chips]
        pairs_ref, pair_grad_ref, query_t_ref = refs[chips:]
        natural_order(pairs_ref, table_ref, (own_ref, other_ref))
        pair_grad_ref[...] = jnp.zeros_like(pair_grad_ref)
        for b in range(2):
            rows = slice(b * block_len, (b + 1) * block_len)
            query_block = query_ref[rows, :]
            grad_block = grad_ref[rows, :]
            product = grad_block.astype(jnp.float32) * attended_ref[rows, :]
            queries = [heads_to_rows(query_block, g) for g in range(KV_HEADS)]
            grads = [heads_to_rows(grad_block, g) for g in range(KV_HEADS)]
            deltas = [
                jnp.sum(heads_to_rows(product, g).T, axis=0, keepdims=True)
                for g in range(KV_HEADS)
            ]
            first, last, begin, end = visible_keys(table_ref, docs_ref, b)

            def step(j, state):
                start = pl.multiple_of(j * row_count, row_count)
                pos = start + lax.broadcasted_iota(jnp.int32, (row_count, wide), 0)
                visible = (pos >= first) & (pos <= last)
                result = []
                key_grads = []
                value_grads = []
                for g in range(KV_HEADS):
                    key_piece = pairs_ref[pl.ds(start, row_count), g * HEAD : (g + 1) * HEAD]
                    value_piece = pairs_ref[
                        pl.ds(start, row_count), KV_WIDTH + g * HEAD : KV_WIDTH + (g + 1) * HEAD
                    ]
                    n = b * KV_HEADS + g
                    scores = dot_nt(key_piece, queries[g])
                    weights = jnp.where(visible, jnp.exp(scores - log_ref[n : n + 1, :]), 0.0)
                    weight_grad = dot_nt(value_piece, grads[g])
                    score_grad = (weights * (weight_grad - deltas[g])).astype(jnp.bfloat16)
                    value_grads.append(dot(weights.astype(jnp.bfloat16), grads[g]))
                    key_grads.append(dot(score_grad, queries[g]))
                    result.append(state[g] + dot_tn(key_piece, score_grad))
                pair_grad_ref[pl.ds(start, row_count), :] += jnp.concatenate(
                    key_grads + value_grads, axis=1
                )
                return tuple(result)

            state = lax.fori_loop(
                begin,
                end,
                step,
                tuple(jnp.zeros((HEAD, wide), jnp.float32) for _ in range(KV_HEADS)),
            )
            cos_part, sin_part = cos_own_ref[:, rows], sin_own_ref[:, rows]
            for g in range(KV_HEADS):
                for i in range(GROUPS):
                    part = state[g][:, i * block_len : (i + 1) * block_len]
                    top, bottom = part[:half], part[half:]
                    h = (g * GROUPS + i) * HEAD
                    query_t_ref[h : h + half, rows] = (
                        (top * cos_part + bottom * sin_part) * HEAD ** (-0.5)
                    ).astype(jnp.bfloat16)
                    query_t_ref[h + half : h + HEAD, rows] = (
                        (bottom * cos_part - top * sin_part) * HEAD ** (-0.5)
                    ).astype(jnp.bfloat16)

        query_grad_ref[...] = query_t_ref[...].T
        query_w_ref[...] = dot(query_t_ref[...], hidden_ref[0]).T.astype(jnp.bfloat16)
        chip, core = rank()
        for i in range(chips):
            for ref, to_core in ((kept_ref.at[i], core), (sent_refs[i], 1 - core)):
                block = table_ref[(chip ^ i) * 2 + to_core]
                for part, place in ((0, block), (1, 2 * slots - 1 - block)):
                    source = pl.ds(pl.multiple_of(place * block_len, block_len), block_len)
                    ref[part * block_len : (part + 1) * block_len, :] = turn_pairs(
                        pair_grad_ref[source, :], cos_ref[source, :], -sin_ref[source, :]
                    ).astype(jnp.bfloat16)

    half_shape = ((chips, row_count, 2 * KV_WIDTH), jnp.bfloat16)
    return run_kernel(
        kernel,
        [((row_count, D), jnp.bfloat16), ((D, D), jnp.bfloat16), half_shape]
        + [((row_count, 2 * KV_WIDTH), jnp.bfloat16)] * chips,
        [
            table,
            docs,
            query_rot,
            *pair_halves,
            log_total,
            attended,
            grad_attended,
            cos_all,
            sin_all,
            cos_own,
            sin_own,
            hidden_half,
        ],
        scalars=1,
        scratch=[
            pltpu.VMEM((slots * row_count, 2 * KV_WIDTH), jnp.bfloat16),
            pltpu.VMEM((slots * row_count, 2 * KV_WIDTH), jnp.float32),
            pltpu.VMEM((D, row_count), jnp.bfloat16),
        ],
        microseconds=18,
    )


def first_gradients(direct, kept, received, hidden_half, query_w, out_grad, shards):
    chips, row_count, _ = kept.shape
    rest = D - HEAD
    columns_all = 2 * KV_WIDTH + D + HEAD
    rows = D // shards

    def kernel(kept_ref, hidden_ref, query_w_ref, out_grad_ref, *refs):
        received_refs, refs = refs[:chips], refs[chips:]
        pair_refs, outs = refs[:chips], refs[chips:-1]
        mixed_ref = refs[-1]
        total = jnp.zeros((2 * KV_WIDTH, D), jnp.float32)
        for i in range(chips):
            pairs = (
                kept_ref[i].astype(jnp.float32) + received_refs[i][...].astype(jnp.float32)
            ).astype(jnp.bfloat16)
            if direct:
                for n in range(2 * KV_WIDTH // TILE):
                    pair_refs[i][n * row_count : (n + 1) * row_count, :] = pairs[
                        :, n * TILE : (n + 1) * TILE
                    ]
            else:
                pair_refs[i][...] = pairs
            total += dot_tn(pairs, hidden_ref[i])
        mixed_ref[:, : 2 * KV_WIDTH] = total.T.astype(jnp.bfloat16)
        mixed_ref[:, 2 * KV_WIDTH : 2 * KV_WIDTH + D] = query_w_ref[...]
        mixed_ref[:, 2 * KV_WIDTH + D :] = out_grad_ref[:, rest:]
        if not direct:
            outs[0][...] = mixed_ref[...]
            return
        chip, core = rank()
        for n in range(2 * chips):
            c = (chip ^ (n % chips)) * 2 + (core ^ (n // chips))
            part = mixed_ref[:, pl.ds(pl.multiple_of(c * TILE, TILE), TILE)]
            tile = out_grad_ref[:, pl.ds(pl.multiple_of((c // 2) * TILE, TILE), TILE)]
            unit = jnp.where(c % 2 == 0, tile[:, : TILE // 2], tile[:, TILE // 2 :])
            for z in range(shards):
                outs[n][z, :rows, :] = part[z * rows : (z + 1) * rows]
                middle = z * rows + rows // 2
                outs[n][z, rows:, : TILE // 2] = unit[z * rows : middle]
                outs[n][z, rows:, TILE // 2 :] = unit[middle : (z + 1) * rows]

    tiles = 2 * KV_WIDTH // TILE if direct else 1
    outs = [((row_count * tiles, 2 * KV_WIDTH // tiles), jnp.bfloat16)] * chips
    outs += (
        [((shards, rows + rows // 2, TILE), jnp.bfloat16)] * (2 * chips)
        if direct
        else [((D, columns_all), jnp.bfloat16)]
    )
    result = run_kernel(
        kernel,
        outs,
        [kept, hidden_half, query_w, out_grad, *received],
        scratch=[pltpu.VMEM((D, columns_all), jnp.bfloat16)],
        microseconds=0,
    )
    return result[:chips], result[chips:]


def local(
    layer_input,
    slot_table,
    seq_ids,
    w_query,
    w_key,
    w_value,
    w_out,
    w_gate,
    w_up,
    w_down,
    attn_gain,
    ffn_gain,
    cotangent,
):
    count = lax.axis_size("ctx")
    chips = count // 2
    index = lax.axis_index("ctx")
    chip, core = rank()
    shards = lax.axis_size("fsdp")
    rows, ff = w_gate.shape
    row_count = layer_input.shape[1]
    block_len = row_count // 2
    length = row_count * count
    direct = (
        rows % 16 == 0 and (ff // chips) % TILE == 0 and count * TILE == D + 2 * KV_WIDTH + HEAD
    )

    mixed_shard = jnp.concatenate(
        [w_key, w_value, w_query, w_out[:, D - HEAD :]], axis=1
    )
    piece = first_piece(mixed_shard, index, count)
    unit = first_piece(w_out[:, : D - HEAD], index, count)
    unit = jnp.concatenate([unit[: rows // 2], unit[rows // 2 :]], axis=1)
    gains = jnp.concatenate([attn_gain, ffn_gain])
    gains = jnp.pad(gains, (0, 16 * piece.shape[1] - 2 * rows)).reshape(16, piece.shape[1])
    tokens_low = layer_input[0]
    token_pieces = [tokens_low] + [chip_swap(tokens_low, i) for i in range(1, chips)]
    first_rows = gather_rows(jnp.concatenate([piece, unit, gains], axis=0))
    gains_all = first_rows[:, rows + rows // 2 :].reshape(shards, -1).astype(jnp.float32)
    gain_one = gains_all[:, :rows].reshape(1, D)
    gain_two = gains_all[:, rows : 2 * rows].reshape(1, D)
    hidden_half = normalize(token_pieces, gain_one)
    first_own = gather_same_core(after(first_rows, hidden_half))
    wide_own, wide_received = start_gather_rows(
        wide_piece(w_gate, w_up, chip, core, chips), first_rows
    )
    low_start = start_gather_half(after(w_down, hidden_half))
    first_pieces = first_own + [core_swap(v) for v in first_own]
    if direct:
        first = first_pieces
    else:
        ordered = in_rank_order(first_pieces)
        mixed_all = jnp.concatenate([v[:, :rows].reshape(D, -1) for v in ordered], axis=1)
        units = [
            v[:, rows : rows + rows // 2]
            .reshape(shards, rows // 2, 2, -1)
            .transpose(0, 2, 1, 3)
            .reshape(D, -1)
            for v in ordered
        ]
        first = [mixed_all, jnp.concatenate([*units, mixed_all[:, 2 * KV_WIDTH + D :]], axis=1)]

    docs = seq_ids[0].reshape(2 * count, block_len)
    own_block = lax.dynamic_index_in_dim(slot_table, index, 0, keepdims=False)
    own_blocks = jnp.stack([own_block, 2 * count - 1 - own_block])
    block_pos = own_blocks[:, None] * block_len + jnp.arange(block_len, dtype=jnp.int32)[None, :]
    half_width = after(jnp.arange(HEAD // 2, dtype=jnp.float32), hidden_half)
    frequencies = rope_base ** (-(half_width * 2.0 / HEAD))
    angles = jnp.arange(length, dtype=jnp.int32).astype(jnp.float32)[:, None] * frequencies[None, :]
    cos_all = jnp.tile(jnp.cos(angles), (1, 2 * TILE // HEAD))
    sin_all = jnp.tile(jnp.sin(angles), (1, 2 * TILE // HEAD))
    own_angles = frequencies[:, None] * block_pos.reshape(1, row_count).astype(jnp.float32)
    cos_own, sin_own = jnp.cos(own_angles), jnp.sin(own_angles)

    wide_rows = in_order(wide_own, wide_received, shards // 2)
    query_rot, own_pairs, mixed, out_w_all = project(
        direct, slot_table, after(hidden_half, wide_rows, low_start, cos_own, sin_own), first, cos_all, sin_all
    )
    pair_halves = (own_pairs, core_swap(own_pairs))
    wide_pieces = gather_same_core(wide_rows)
    low_own = finish_gather_half(after(low_start, wide_rows))
    grad_out = cotangent[0]
    attended, log_total = attention_forward(slot_table, docs, query_rot, pair_halves)
    grad_other = core_swap(after(grad_out, attended))
    residual, hidden_two = mix(attended, tokens_low, out_w_all, gain_two)
    if direct:
        wide = wide_pieces
    else:
        whole = [v.reshape(D, -1) for v in by_owner(wide_pieces, chip)]
        wide = [jnp.concatenate(whole[n : n + chips // 2], axis=1) for n in (0, chips // 2)]
    out_kept, grad_kept, sent, *wide_grads = feed_forward(
        direct,
        hidden_two,
        core_swap(hidden_two),
        grad_out,
        grad_other,
        wide,
        low_own,
        ff,
        shards,
    )
    lanes = ff // chips
    slice_rows = w_down.shape[0] // count
    pile = rows // slice_rows
    if not direct:
        gate_grad, up_grad, down_grad = wide_grads
        down_grad = down_grad.reshape(shards // 2, chips, 2, slice_rows, pile, D // pile)
        down_grad = down_grad.transpose(0, 2, 1, 4, 3, 5).reshape(shards, chips, rows, D // pile)
        wide_grads = [
            jnp.concatenate(
                [
                    lax.dynamic_slice_in_dim(
                        jnp.where(c < chips // 2, gate_grad, up_grad),
                        (c % (chips // 2)) * lanes,
                        lanes,
                        1,
                    ).reshape(shards, rows, lanes),
                    lax.dynamic_index_in_dim(down_grad, c, 1, keepdims=False),
                ],
                axis=2,
            )
            for c in (chip ^ i for i in range(chips))
        ]
    output, grad_residual, grad_attended, out_grad = unmix(
        residual,
        out_kept,
        grad_kept,
        core_swap(sent),
        grad_out,
        attended,
        out_w_all,
        gain_two,
    )

    grad_query, query_w, pairs_kept, *pairs_sent = attention_backward(
        slot_table,
        docs,
        query_rot,
        pair_halves,
        log_total,
        attended,
        grad_attended,
        cos_all,
        sin_all,
        cos_own,
        sin_own,
        hidden_half,
    )
    pairs_received = [core_swap(v) for v in pairs_sent]
    pair_sums, mixed_grads = first_gradients(
        direct, pairs_kept, pairs_received, hidden_half, query_w, out_grad, shards
    )
    if not direct:
        targets = [(chip ^ i) * 2 + (core ^ a) for a in range(2) for i in range(chips)]
        units = [
            first_piece(out_grad[:, : D - HEAD], c, count)
            .reshape(shards, 2, rows // 2, -1)
            .transpose(0, 2, 1, 3)
            .reshape(shards, rows // 2, -1)
            for c in targets
        ]
        mixed_grads = [
            jnp.concatenate(
                [first_piece(mixed_grads[0], c, count).reshape(shards, rows, -1), unit], axis=1
            )
            for c, unit in zip(targets, units)
        ]
    mixed_sums = [sum_cores(*pair) for pair in zip(mixed_grads[:chips], mixed_grads[chips:])]
    if direct:
        shape = mixed_sums[0].shape
        split = shape[0] * shape[1]
        both_sum = sum_chips(
            [
                jnp.concatenate([one.reshape(split, TILE), other], axis=0)
                for one, other in zip(mixed_sums, pair_sums)
            ]
        ).astype(jnp.bfloat16)
        first_sum = both_sum[:split].reshape(shape)
        owned = jnp.concatenate(jnp.split(both_sum[split:], 2 * KV_WIDTH // TILE), axis=1)
    else:
        first_sum = sum_chips(mixed_sums).astype(jnp.bfloat16)
        owned = sum_chips(pair_sums).astype(jnp.bfloat16)
    first_part = sum_rows(first_sum).astype(jnp.bfloat16)
    first_mine = gather_same_core(first_part)
    wide_sum = sum_chips(wide_grads, pair_sums[0]).astype(jnp.bfloat16)
    wide_sum = jnp.concatenate(
        [wide_sum[:, :, :lanes], by_core_slices(wide_sum[:, :, lanes:])], axis=2
    )
    wide_part = sum_rows(after(wide_sum, mixed_sums)).astype(jnp.bfloat16)
    wide_all = gather_chips(wide_part)
    grad_hidden_one = dot_nt(
        jnp.concatenate([owned, grad_query], axis=1), mixed[:, : 2 * KV_WIDTH + D]
    )
    tokens = tokens_low.astype(jnp.float32)
    inv_one = inverse_root(tokens)
    grad_input = (
        grad_residual + norm_back(grad_hidden_one, tokens * inv_one, inv_one, gain_one)
    ).astype(jnp.bfloat16)

    gain_rows = [v.astype(jnp.float32).reshape(1, rows) for v in (attn_gain, ffn_gain)]
    if direct:
        gate_grad, up_grad, down_grad, gain_grad_two = finish_wide(
            wide_all, w_gate, w_up, gain_rows[1], pile
        )
        down_grad = down_grad.T
        first_all = first_mine + [core_swap(v) for v in after(tuple(first_mine), gain_grad_two)]
        query_w, key_w, value_w, out_w, gain_grad_one = finish_first(
            first_all, mixed_shard, gain_rows[0]
        )
    else:
        own, other = by_owner(wide_all[:chips], chip), by_owner(wide_all[chips:], chip)
        cores = both_cores(jnp.stack(own), jnp.stack(other), core)
        down_grad = jnp.concatenate(
            [unstack_down(cores[c % 2][c // 2][:, lanes:], pile) for c in range(count)]
        ).astype(jnp.float32)
        gate_grad, up_grad = (
            jnp.concatenate(
                [cores[k][n + q][:, :lanes] for k in range(2) for q in range(chips // 2)], axis=1
            ).astype(jnp.float32)
            for n in (0, chips // 2)
        )
        ordered = in_rank_order(first_mine + [core_swap(v) for v in first_mine])
        first_grad = jnp.concatenate([v[:rows] for v in ordered], axis=1).astype(jnp.float32)
        units = [
            v[rows:].reshape(rows // 2, 2, -1).transpose(1, 0, 2).reshape(rows, -1) for v in ordered
        ]
        key_w, value_w, query_w, last = jnp.split(
            first_grad, [KV_WIDTH, 2 * KV_WIDTH, 2 * KV_WIDTH + D], axis=1
        )
        out_w = jnp.concatenate([*[v.astype(jnp.float32) for v in units], last], axis=1)
        used = 2 * KV_WIDTH + D
        gain_grad_one = (
            jnp.sum(
                first_grad[:, :used] * mixed_shard[:, :used].astype(jnp.float32),
                axis=1,
            )
            / gain_rows[0]
        )
        gain_grad_two = (
            jnp.sum(
                gate_grad * w_gate.astype(jnp.float32) + up_grad * w_up.astype(jnp.float32),
                axis=1,
            )
            / gain_rows[1]
        )
    return (
        output.T[None],
        grad_input[None],
        query_w,
        key_w,
        value_w,
        out_w,
        gate_grad,
        up_grad,
        down_grad,
        gain_grad_one.reshape(rows),
        gain_grad_two.reshape(rows),
    )


def solution(mesh):
    placed = (
        P("fsdp", "ctx", None),
        P(),
        P("fsdp", None),
        P("fsdp", None),
        P("fsdp", None),
        P("fsdp", None),
        P("fsdp", None),
        P("fsdp", None),
        P("fsdp", None),
        P("fsdp", None),
        P("fsdp"),
        P("fsdp"),
        P("fsdp", "ctx", None),
    )
    return jax.shard_map(
        local,
        mesh=mesh,
        in_specs=placed,
        out_specs=(
            P("fsdp", "ctx", None),
            P("fsdp", "ctx", None),
            P("fsdp", None),
            P("fsdp", None),
            P("fsdp", None),
            P("fsdp", None),
            P("fsdp", None),
            P("fsdp", None),
            P("fsdp", None),
            P("fsdp"),
            P("fsdp"),
        ),
        check_vma=False,
    )
```

```python
import jax
import jax.numpy as jnp
from jax import lax
from jax.experimental import pallas as pl
from jax.experimental.pallas import tpu as pltpu
from jax.sharding import PartitionSpec as P

D = 576
HEADS = 9
KV_HEADS = 3
HEAD = 64
GROUPS = HEADS // KV_HEADS
KV_WIDTH = KV_HEADS * HEAD
TILE = 128
DOCS = 4

epsilon = 1e-05
rope_base = 100000.0

VMEM = pl.BlockSpec(memory_space=pltpu.VMEM)
SMEM = pl.BlockSpec(memory_space=pltpu.SMEM)


def run_kernel(kernel, out_shapes, inputs, scalars=0, scratch=(), microseconds=1):
    return pl.pallas_call(
        kernel,
        out_shape=tuple(jax.ShapeDtypeStruct(*out) for out in out_shapes),
        in_specs=[SMEM] * scalars + [VMEM] * (len(inputs) - scalars),
        out_specs=tuple(VMEM for _ in out_shapes),
        scratch_shapes=list(scratch),
        compiler_params=pltpu.CompilerParams(vmem_limit_bytes=60 * 1024 * 1024),
        cost_estimate=pl.CostEstimate(
            flops=microseconds * 1150 * 10**6, bytes_accessed=1024, transcendentals=0
        ),
    )(*inputs)


def rank():
    index = lax.axis_index("ctx")
    return index // 2, index % 2


def swap(value, axis, offset):
    count = lax.axis_size(axis)
    return lax.ppermute(value, axis, [(i, i ^ offset) for i in range(count)])


def chip_swap(value, offset):
    return swap(value, "ctx", 2 * offset)


def core_swap(value):
    return swap(value, "ctx", 1)


def by_owner(pieces, index):
    bit = 1
    while bit < len(pieces):
        flag = (index & bit) != 0
        pieces = [jnp.where(flag, pieces[i ^ bit], pieces[i]) for i in range(len(pieces))]
        bit = bit * 2
    return pieces


def in_order(own, other, offset):
    flag = (lax.axis_index("fsdp") & offset) != 0
    return jnp.concatenate([jnp.where(flag, other, own), jnp.where(flag, own, other)], axis=0)


def start_gather_rows(piece, *others):
    count = lax.axis_size("fsdp")
    values = piece[None]
    offset = 1
    while offset < count // 2:
        values = in_order(values, swap(values, "fsdp", offset), offset)
        offset = offset * 2
    values = after(values, *others)
    return values, swap(values, "fsdp", offset)


def gather_rows(piece, *others):
    count = lax.axis_size("fsdp")
    index = lax.axis_index("fsdp")
    values = piece[None]
    offset = 1
    while offset < count:
        if offset > 1 and others:
            values = after(values, *others)
        other = swap(values, "fsdp", offset)
        flag = (index & offset) != 0
        values = jnp.concatenate(
            [jnp.where(flag, other, values), jnp.where(flag, values, other)], axis=0
        )
        offset = offset * 2
    return values


def start_gather_half(piece):
    received = lax.ppermute(piece, ("ctx", "fsdp"), half_pairs())
    return jnp.where(in_half(), piece, received)[None]


def finish_gather_half(values):
    offset = 1
    while offset < lax.axis_size("fsdp") // 2:
        values = in_order(values, swap(values, "fsdp", offset), offset)
        offset = offset * 2
    return values


def gather_same_core(piece):
    return [piece] + [chip_swap(piece, i) for i in range(1, lax.axis_size("ctx") // 2)]


def gather_chips(piece):
    own = gather_same_core(piece)
    return own + [core_swap(value) for value in own]


def after(value, *others):
    return lax.optimization_barrier((value, others))[0]


def in_rank_order(pieces):
    chip, core = rank()
    chips = len(pieces) // 2
    own, other = by_owner(pieces[:chips], chip), by_owner(pieces[chips:], chip)
    ordered = [by_owner(list(pair), core) for pair in zip(own, other)]
    return [value for pair in ordered for value in pair]


def sum_cores(kept, sent):
    return (kept.astype(jnp.float32) + core_swap(sent).astype(jnp.float32)).astype(jnp.bfloat16)


def sum_chips(sums, *others):
    received = tuple(chip_swap(sums[i], i) for i in range(1, len(sums)))
    if others:
        received = after(received, *others)
    return sum((value.astype(jnp.float32) for value in received), sums[0].astype(jnp.float32))


def half_pairs():
    count = lax.axis_size("fsdp")
    half = count // 2
    return [
        (c * count + z, c * count + (z ^ half))
        for c in range(lax.axis_size("ctx"))
        for z in range(count)
        if z // half == c % 2
    ]


def in_half():
    half = lax.axis_size("fsdp") // 2
    return lax.axis_index("fsdp") // half == lax.axis_index("ctx") % 2


def sum_rows(values):
    count = lax.axis_size("fsdp")
    index = lax.axis_index("fsdp")

    def pick(offset):
        return lax.dynamic_index_in_dim(values, index ^ offset, 0, keepdims=False)

    total = pick(0).astype(jnp.float32)
    for i in reversed(range(1, count)):
        total = total + swap(pick(i), "fsdp", i).astype(jnp.float32)
    return total


def first_piece(mixed, c, count):
    width = mixed.shape[1] // count
    return lax.dynamic_slice_in_dim(mixed, c * width, width, 1)


def wide_piece(gate, up, chip, core, chips):
    lanes = gate.shape[1] // chips
    q = chip % (chips // 2)
    wide = jnp.where(chip < chips // 2, gate, up)
    return lax.dynamic_slice_in_dim(wide, (core * (chips // 2) + q) * lanes, lanes, 1)


def stack_down(part, pile):
    width = D // pile
    return jnp.concatenate([part[:, n * width : (n + 1) * width] for n in range(pile)], axis=0)


def unstack_down(part, pile):
    rows = part.shape[0] // pile
    return jnp.concatenate([part[n * rows : (n + 1) * rows] for n in range(pile)], axis=1)


def by_core_slices(values):
    _, core = rank()
    values = values.reshape(-1, 2, *values.shape[1:])
    mine, theirs = (
        lax.dynamic_index_in_dim(values, side, 1, keepdims=False) for side in (core, 1 - core)
    )
    return jnp.concatenate(both_cores(mine, core_swap(theirs), core))


def both_cores(own, other, core):
    return jnp.where(core == 0, own, other), jnp.where(core == 0, other, own)


def gain_gradient(terms, gain_row):
    total = sum(terms[:, t : t + TILE] for t in range(0, terms.shape[1], TILE))
    return jnp.sum(total.T, axis=0, keepdims=True) / gain_row


def finish_first(pieces, shard, gain):
    count = len(pieces)
    chips = count // 2
    rows = shard.shape[0]
    used = 2 * KV_WIDTH + D

    def kernel(*refs):
        shard_ref, gain_ref = refs[count : count + 2]
        query, key, value, out, gain_grad, whole = refs[count + 2 :]
        chip, core = rank()
        for n in range(count):
            c = (chip ^ (n % chips)) * 2 + (core ^ (n // chips))
            whole[:, pl.ds(pl.multiple_of(c * TILE, TILE), TILE)] = refs[n][:rows, :].astype(
                jnp.float32
            )
        key[...] = whole[:, :KV_WIDTH]
        value[...] = whole[:, KV_WIDTH : 2 * KV_WIDTH]
        query[...] = whole[:, 2 * KV_WIDTH : used]
        for n in range(chips):
            columns = pl.ds(pl.multiple_of((chip ^ n) * TILE, TILE), TILE)
            pair = both_cores(
                refs[n][rows:, :].astype(jnp.float32),
                refs[n + chips][rows:, :].astype(jnp.float32),
                core,
            )
            for m in range(2):
                out[m * (rows // 2) : (m + 1) * (rows // 2), columns] = jnp.concatenate(
                    [part[:, m * (TILE // 2) : (m + 1) * (TILE // 2)] for part in pair], axis=1
                )
        out[:, chips * TILE :] = whole[:, used:]
        terms = whole[...] * shard_ref[...].astype(jnp.float32)
        lane = lax.broadcasted_iota(jnp.int32, terms.shape, 1)
        gain_grad[...] = gain_gradient(jnp.where(lane < used, terms, 0.0), gain_ref[...])

    return run_kernel(
        kernel,
        [
            ((rows, D), jnp.float32),
            ((rows, KV_WIDTH), jnp.float32),
            ((rows, KV_WIDTH), jnp.float32),
            ((rows, D), jnp.float32),
            ((1, rows), jnp.float32),
        ],
        [*pieces, shard, gain],
        microseconds=2,
        scratch=[pltpu.VMEM((rows, count * TILE), jnp.float32)],
    )


def finish_wide(pieces, w_gate, w_up, gain, pile):
    count = len(pieces)
    chips = count // 2
    rows, ff = w_gate.shape
    lanes = ff // chips
    down_rows = rows // pile
    low_lanes = D // pile

    def kernel(*refs):
        gate_ref, up_ref, gain_ref = refs[count : count + 3]
        gate, up, down, gain_grad, total, low = refs[count + 3 :]
        chip, core = rank()
        total[...] = jnp.zeros_like(total)
        for n in range(count):
            to_chip, to_core = chip ^ (n % chips), core ^ (n // chips)
            column = (to_core * (chips // 2) + to_chip % (chips // 2)) * lanes
            columns = pl.ds(pl.multiple_of(column, TILE), lanes)
            for kind, out, weight in ((0, gate, gate_ref), (1, up, up_ref)):

                @pl.when(to_chip // (chips // 2) == kind)
                def _():
                    part = refs[n][:, :lanes].astype(jnp.float32)
                    out[:, columns] = part
                    total[...] += part * weight[:, columns].astype(jnp.float32)

            start = pl.multiple_of((to_chip * 2 + to_core) * down_rows, 16)
            for m in range(pile):
                low[pl.ds(start, down_rows), m * low_lanes : (m + 1) * low_lanes] = refs[n][
                    m * down_rows : (m + 1) * down_rows, lanes:
                ].astype(jnp.float32)
        down[...] = low[...].T
        gain_grad[...] = gain_gradient(total[...], gain_ref[...])

    return run_kernel(
        kernel,
        [
            ((rows, ff), jnp.float32),
            ((rows, ff), jnp.float32),
            ((D, count * down_rows), jnp.float32),
            ((1, rows), jnp.float32),
        ],
        [*pieces, w_gate, w_up, gain],
        microseconds=4,
        scratch=[
            pltpu.VMEM((rows, lanes), jnp.float32),
            pltpu.VMEM((count * down_rows, D), jnp.float32),
        ],
    )


def dot(first_matrix, second_matrix):
    return jnp.dot(first_matrix, second_matrix, preferred_element_type=jnp.float32)


def dot_nt(first_matrix, second_matrix):
    return lax.dot_general(
        first_matrix, second_matrix, (((1,), (1,)), ((), ())), preferred_element_type=jnp.float32
    )


def dot_tn(first_matrix, second_matrix):
    return lax.dot_general(
        first_matrix, second_matrix, (((0,), (0,)), ((), ())), preferred_element_type=jnp.float32
    )


def norm_back(grad_normed, unit_rows, inv_root, gain_vec):
    scaled_grad = grad_normed * gain_vec
    return inv_root * (
        scaled_grad - unit_rows * jnp.mean(scaled_grad * unit_rows, axis=-1, keepdims=True)
    )


def inverse_root(rows):
    return lax.rsqrt(jnp.mean(rows * rows, axis=-1, keepdims=True) + epsilon)


def turn(values, cos_tile, sin_tile):
    lane = lax.broadcasted_iota(jnp.int32, values.shape, 1) % HEAD
    turned = jnp.where(
        lane < HEAD // 2,
        -pltpu.roll(values, TILE - HEAD // 2, 1),
        pltpu.roll(values, HEAD // 2, 1),
    )
    return values * cos_tile + turned * sin_tile


def turn_pairs(values, cos_tile, sin_tile):
    lane = lax.broadcasted_iota(jnp.int32, cos_tile.shape, 1)
    middle = values[:, TILE : 2 * TILE]
    return jnp.concatenate(
        [
            turn(values[:, :TILE], cos_tile, sin_tile),
            jnp.where(lane < HEAD, turn(middle, cos_tile, sin_tile), middle),
            values[:, 2 * TILE :],
        ],
        axis=1,
    )


def normalize(token_pieces, gain):
    row_count = token_pieces[0].shape[0]
    chips = len(token_pieces)

    def kernel(*refs):
        gain_ref, hidden_ref = refs[chips:]
        for n in range(chips):
            tokens = refs[n][...].astype(jnp.float32)
            hidden_ref[n] = ((tokens * inverse_root(tokens)) * gain_ref[...]).astype(jnp.bfloat16)

    return run_kernel(
        kernel, [((chips, row_count, D), jnp.bfloat16)], [*token_pieces, gain], microseconds=3
    )[0]


def project(direct, table, hidden_half, first, cos_all, sin_all):
    chips, row_count, _ = hidden_half.shape
    block_len = row_count // 2
    count = 2 * chips
    columns_all = count * TILE if direct else first[0].shape[1]
    shards = lax.axis_size("fsdp")
    rows = D // shards

    def kernel(table_ref, hidden_ref, cos_ref, sin_ref, *refs):
        first_refs = refs[: len(first)]
        query_ref, pairs_ref = refs[len(first) : len(first) + 2]
        chip, core = rank()
        if direct:
            mixed_ref, out_w_ref = refs[-2:]
            for n in range(count):
                c = (chip ^ (n % chips)) * 2 + (core ^ (n // chips))
                columns = pl.ds(pl.multiple_of(c * TILE, TILE), TILE)
                for z in range(shards):
                    mixed_ref[z * rows : (z + 1) * rows, columns] = first_refs[n][z, :rows, :]
            for n in range(chips):
                columns = pl.ds(pl.multiple_of((chip ^ n) * TILE, TILE), TILE)
                for z in range(shards):
                    pair = both_cores(
                        first_refs[n][z, rows : rows + rows // 2, :].astype(jnp.float32),
                        first_refs[n + chips][z, rows : rows + rows // 2, :].astype(jnp.float32),
                        core,
                    )
                    half = TILE // 2
                    block = jnp.concatenate(
                        [
                            jnp.concatenate([part[:, m * half : (m + 1) * half] for part in pair], axis=1)
                            for m in range(2)
                        ],
                        axis=0,
                    )
                    out_w_ref[z * rows : (z + 1) * rows, columns] = block.astype(jnp.bfloat16)
            out_w_ref[:, chips * TILE :] = mixed_ref[:, 2 * KV_WIDTH + D :]
        else:
            mixed_ref = first_refs[0]
        for n in range(chips):
            hidden = hidden_ref[n]
            pairs = dot(hidden, mixed_ref[:, : 2 * KV_WIDTH])
            block = table_ref[(chip ^ n) * 2 + core]
            queries = dot(hidden, mixed_ref[:, 2 * KV_WIDTH :]) if n == 0 else None
            for part, place in ((0, block), (1, 2 * count - 1 - block)):
                source = pl.ds(pl.multiple_of(place * block_len, block_len), block_len)
                own = slice(part * block_len, (part + 1) * block_len)
                cos_tile, sin_tile = cos_ref[source, :], sin_ref[source, :]
                pairs_ref[n, own, :] = turn_pairs(pairs[own], cos_tile, sin_tile).astype(
                    jnp.bfloat16
                )
                if n == 0:
                    for start in range(0, D, TILE):
                        width = min(TILE, D - start)
                        turned = turn(queries[own, start : start + TILE], cos_tile, sin_tile)
                        query_ref[own, start : start + width] = (
                            (turned * HEAD ** (-0.5)).astype(jnp.bfloat16)[:, :width]
                        )

    outs = [((row_count, D), jnp.bfloat16), ((chips, row_count, 2 * KV_WIDTH), jnp.bfloat16)]
    if direct:
        outs += [((D, columns_all), jnp.bfloat16), ((D, D), jnp.bfloat16)]
    result = run_kernel(
        kernel, outs, [table, hidden_half, cos_all, sin_all, *first], scalars=1, microseconds=5
    )
    return result if direct else (*result, *first)


def natural_order(out, table_ref, halves):
    chip, core = rank()
    chips, row_count, _ = halves[0].shape
    block_len = row_count // 2
    for a in range(2):
        for n in range(chips):
            block = table_ref[(chip ^ n) * 2 + (core ^ a)]
            for part, place in ((0, block), (1, 4 * chips - 1 - block)):
                rows = pl.ds(pl.multiple_of(place * block_len, block_len), block_len)
                out[rows, :] = halves[a][n, part * block_len : (part + 1) * block_len, :]


def heads_to_rows(values, group):
    return jnp.concatenate(
        [
            values[:, (group * GROUPS + i) * HEAD : (group * GROUPS + i + 1) * HEAD]
            for i in range(GROUPS)
        ],
        axis=0,
    )


def visible_keys(table_ref, docs_ref, b):
    count, block_len = docs_ref.shape
    chip, core = rank()
    block = table_ref[chip * 2 + core]
    block = block if b == 0 else count - 1 - block
    docs = docs_ref[...]
    own = docs_ref[pl.ds(block, 1), :]
    first = jnp.zeros((1, block_len), jnp.float32)
    for doc in range(1, DOCS):
        before = jnp.sum((docs < doc).astype(jnp.float32), axis=0, keepdims=True)
        start = jnp.sum(before, axis=1, keepdims=True)
        first = jnp.where(own == doc, start, first)
    begin = jnp.min(first).astype(jnp.int32) // (2 * block_len)
    first = first.astype(jnp.int32)
    last = block * block_len + lax.broadcasted_iota(jnp.int32, (1, block_len), 1)
    return (
        jnp.concatenate([first] * GROUPS, axis=1),
        jnp.concatenate([last] * GROUPS, axis=1),
        begin,
        block // 2 + 1,
    )


def attention_forward(table, docs, query_rot, pair_halves):
    row_count = query_rot.shape[0]
    block_len = row_count // 2
    wide = GROUPS * block_len

    def kernel(
        table_ref,
        docs_ref,
        query_ref,
        own_ref,
        other_ref,
        out_ref,
        log_ref,
        pairs_ref,
    ):
        natural_order(pairs_ref, table_ref, (own_ref, other_ref))
        for b in range(2):
            rows = slice(b * block_len, (b + 1) * block_len)
            query_block = query_ref[rows, :]
            queries = [heads_to_rows(query_block, g) for g in range(KV_HEADS)]
            first, last, begin, end = visible_keys(table_ref, docs_ref, b)

            def step(j, state):
                start = pl.multiple_of(j * row_count, row_count)
                pos = start + lax.broadcasted_iota(jnp.int32, (row_count, wide), 0)
                visible = (pos >= first) & (pos <= last)
                result = []
                for g in range(KV_HEADS):
                    top, total, acc = state[g]
                    key_piece = pairs_ref[pl.ds(start, row_count), g * HEAD : (g + 1) * HEAD]
                    value_piece = pairs_ref[
                        pl.ds(start, row_count), KV_WIDTH + g * HEAD : KV_WIDTH + (g + 1) * HEAD
                    ]
                    scores = jnp.where(visible, dot_nt(key_piece, queries[g]), -1e30)
                    new_top = jnp.maximum(top, jnp.max(scores, axis=0, keepdims=True))
                    weights = jnp.exp(scores - new_top)
                    rescale = jnp.exp(top - new_top)
                    total = total * rescale + jnp.sum(weights, axis=0, keepdims=True)
                    acc = acc * rescale + dot_tn(value_piece, weights.astype(jnp.bfloat16))
                    result.append((new_top, total, acc))
                return tuple(result)

            state = lax.fori_loop(
                begin,
                end,
                step,
                tuple(
                    (
                        jnp.full((1, wide), -1e30, jnp.float32),
                        jnp.zeros((1, wide), jnp.float32),
                        jnp.zeros((HEAD, wide), jnp.float32),
                    )
                    for _ in range(KV_HEADS)
                ),
            )
            parts = []
            for g in range(KV_HEADS):
                top, total, acc = state[g]
                part = (acc / total).T
                parts += [part[i * block_len : (i + 1) * block_len] for i in range(GROUPS)]
                n = b * KV_HEADS + g
                log_ref[n : n + 1, :] = top + jnp.log(total)
            out_ref[rows, :] = jnp.concatenate(parts, axis=1)

    return run_kernel(
        kernel,
        [((row_count, D), jnp.float32), ((2 * KV_HEADS, wide), jnp.float32)],
        [table, docs, query_rot, *pair_halves],
        scalars=1,
        scratch=[pltpu.VMEM((table.shape[0] * row_count, 2 * KV_WIDTH), jnp.bfloat16)],
        microseconds=12,
    )


def mix(attended, tokens, out_w, gain):
    row_count = tokens.shape[0]

    def kernel(
        attended_ref, tokens_ref, out_w_ref, gain_ref, residual_ref, hidden_ref
    ):
        attn_low = attended_ref[...].astype(jnp.bfloat16)
        residual = tokens_ref[...].astype(jnp.float32) + dot(attn_low, out_w_ref[...])
        residual_ref[...] = residual
        hidden_ref[...] = ((residual * inverse_root(residual)) * gain_ref[...]).astype(jnp.bfloat16)

    return run_kernel(
        kernel,
        [((row_count, D), jnp.float32), ((row_count, D), jnp.bfloat16)],
        [attended, tokens, out_w, gain],
        microseconds=2,
    )


def feed_forward(direct, hidden, hidden_other, grad_out, grad_other, wide, low_own, ff, shards):
    row_count = hidden.shape[0]
    width = ff // 2
    chips = lax.axis_size("ctx") // 2
    lanes = ff // chips
    rows = D // shards
    down_rows = ff // shards
    half = shards // 2
    steps = 1 if direct else 2
    chunk = width // steps
    per = chunk // down_rows
    slice_rows = down_rows // (2 * chips)
    pile = rows // slice_rows

    def kernel(hidden_ref, hidden_other_ref, grad_ref, grad_other_ref, low_ref, *refs):
        wide_refs, refs = refs[: len(wide)], refs[len(wide) :]
        out_ref, hidden_grad_ref, sent_ref = refs[:3]
        wide_grads = refs[3 : 3 + (chips if direct else 2)]
        wide_ref, gate_grad_ref, down_ref, low_ref_f32 = refs[-4:]
        chip, _ = rank()
        for n in range(half):
            down_ref[n * down_rows : (n + 1) * down_rows, :] = low_ref[n]
        if direct:
            for i in range(chips):
                q = chip ^ i
                columns = pl.ds(pl.multiple_of((q % (chips // 2)) * lanes, TILE), lanes)
                wide_ref[q // (chips // 2), :, columns] = wide_refs[i][...].reshape(D, lanes)
        else:
            for kind in range(2):
                wide_ref[kind] = wide_refs[kind][...]
        hidden_all = jnp.concatenate([hidden_ref[...], hidden_other_ref[...]], axis=0)
        grad_all = jnp.concatenate([grad_ref[...], grad_other_ref[...]], axis=0)
        hidden_t = hidden_all.T
        result = jnp.zeros((2 * row_count, D), jnp.float32)
        grad_hidden = jnp.zeros((2 * row_count, D), jnp.float32)
        for j in range(steps):
            columns = slice(j * chunk, (j + 1) * chunk)
            gate_w, up_w = wide_ref[0, :, columns], wide_ref[1, :, columns]
            down_w = down_ref[columns, :]
            gate_value, up_value = dot(hidden_all, gate_w), dot(hidden_all, up_w)
            sigmoid = 1.0 / (1.0 + jnp.exp(-gate_value))
            silu = gate_value * sigmoid
            activation = (silu * up_value).astype(jnp.bfloat16)
            result += dot(activation, down_w)
            grad_activation = dot_nt(grad_all, down_w)
            grad_gate = (
                grad_activation * up_value * sigmoid * (1.0 + gate_value * (1.0 - sigmoid))
            ).astype(jnp.bfloat16)
            grad_up = (grad_activation * silu).astype(jnp.bfloat16)
            grad_hidden += dot_nt(grad_gate, gate_w) + dot_nt(grad_up, up_w)
            gate_grad_ref[0, :, columns] = grad_gate
            gate_grad_ref[1, :, columns] = grad_up
            low = dot(activation.T, grad_all)
            if direct:
                low_ref_f32[...] = low
                for n in range(per):
                    for i in range(chips):
                        for g in range(2):
                            start = n * down_rows + ((chip ^ i) * 2 + g) * slice_rows
                            source = pl.ds(pl.multiple_of(start, 16), slice_rows)
                            part = low_ref_f32[source, :].astype(jnp.bfloat16)
                            wide_grads[i][2 * (j * per + n) + g, :, lanes:] = stack_down(part, pile)
            else:
                refs[5][columns, :] = low.astype(jnp.bfloat16)
        out_ref[...] = result[:row_count]
        hidden_grad_ref[...] = grad_hidden[:row_count]
        sent_ref[:, :, D:] = jnp.zeros((2, row_count, -D % TILE), jnp.bfloat16)
        sent_ref[0, :, :D] = result[row_count:].astype(jnp.bfloat16)
        sent_ref[1, :, :D] = grad_hidden[row_count:].astype(jnp.bfloat16)
        if direct:
            for i in range(chips):
                q = chip ^ i
                columns = pl.ds(pl.multiple_of((q % (chips // 2)) * lanes, TILE), lanes)
                operand = gate_grad_ref[q // (chips // 2), :, columns]
                wide_grads[i][:, :, :lanes] = (
                    dot(hidden_t, operand).astype(jnp.bfloat16).reshape(shards, rows, lanes)
                )
        else:
            for kind in range(2):
                wide_grads[kind][...] = dot(hidden_t, gate_grad_ref[kind]).astype(jnp.bfloat16)

    outs = [
        ((row_count, D), jnp.float32),
        ((row_count, D), jnp.float32),
        ((2, row_count, -(-D // TILE) * TILE), jnp.bfloat16),
    ]
    outs += (
        [((shards, rows, lanes + D // pile), jnp.bfloat16)] * chips
        if direct
        else [((D, width), jnp.bfloat16)] * 2 + [((width, D), jnp.bfloat16)]
    )
    return run_kernel(
        kernel,
        outs,
        [hidden, hidden_other, grad_out, grad_other, low_own, *wide],
        scratch=[
            pltpu.VMEM((2, D, width), jnp.bfloat16),
            pltpu.VMEM((2, 2 * row_count, width), jnp.bfloat16),
            pltpu.VMEM((width, D), jnp.bfloat16),
            pltpu.VMEM((chunk, D), jnp.float32),
        ],
        microseconds=12,
    )


def unmix(
    residual, out_kept, grad_kept, received, grad_out, attended, out_w, gain
):
    row_count = residual.shape[0]

    def kernel(
        residual_ref,
        out_kept_ref,
        grad_kept_ref,
        received_ref,
        grad_out_ref,
        attended_ref,
        out_w_ref,
        gain_ref,
        output_ref,
        residual_grad_ref,
        attended_grad_ref,
        out_grad_ref,
    ):
        residual = residual_ref[...]
        result = residual + out_kept_ref[...] + received_ref[0, :, :D].astype(jnp.float32)
        output_ref[...] = result.astype(jnp.bfloat16).T
        grad_hidden = grad_kept_ref[...] + received_ref[1, :, :D].astype(jnp.float32)
        inv_two = inverse_root(residual)
        residual_grad = grad_out_ref[...].astype(jnp.float32) + norm_back(
            grad_hidden, residual * inv_two, inv_two, gain_ref[...]
        )
        residual_grad_ref[...] = residual_grad
        grad_branch = residual_grad.astype(jnp.bfloat16)
        attended_grad_ref[...] = dot_nt(grad_branch, out_w_ref[...]).astype(jnp.bfloat16)
        out_grad_ref[...] = dot_tn(
            attended_ref[...].astype(jnp.bfloat16), grad_branch
        ).astype(jnp.bfloat16)

    return run_kernel(
        kernel,
        [
            ((D, row_count), jnp.bfloat16),
            ((row_count, D), jnp.float32),
            ((row_count, D), jnp.bfloat16),
            ((D, D), jnp.bfloat16),
        ],
        [
            residual,
            out_kept,
            grad_kept,
            received,
            grad_out,
            attended,
            out_w,
            gain,
        ],
        microseconds=4,
    )


def attention_backward(
    table,
    docs,
    query_rot,
    pair_halves,
    log_total,
    attended,
    grad_attended,
    cos_all,
    sin_all,
    cos_own,
    sin_own,
    hidden_half,
):
    row_count = query_rot.shape[0]
    block_len = row_count // 2
    wide = GROUPS * block_len
    slots = table.shape[0]
    chips = slots // 2
    half = HEAD // 2

    def kernel(
        table_ref,
        docs_ref,
        query_ref,
        own_ref,
        other_ref,
        log_ref,
        attended_ref,
        grad_ref,
        cos_ref,
        sin_ref,
        cos_own_ref,
        sin_own_ref,
        hidden_ref,
        query_grad_ref,
        query_w_ref,
        kept_ref,
        *refs,
    ):
        sent_refs = refs[:chips]
        pairs_ref, pair_grad_ref, query_t_ref = refs[chips:]
        natural_order(pairs_ref, table_ref, (own_ref, other_ref))
        pair_grad_ref[...] = jnp.zeros_like(pair_grad_ref)
        for b in range(2):
            rows = slice(b * block_len, (b + 1) * block_len)
            query_block = query_ref[rows, :]
            grad_block = grad_ref[rows, :]
            product = grad_block.astype(jnp.float32) * attended_ref[rows, :]
            queries = [heads_to_rows(query_block, g) for g in range(KV_HEADS)]
            grads = [heads_to_rows(grad_block, g) for g in range(KV_HEADS)]
            deltas = [
                jnp.sum(heads_to_rows(product, g).T, axis=0, keepdims=True)
                for g in range(KV_HEADS)
            ]
            first, last, begin, end = visible_keys(table_ref, docs_ref, b)

            def step(j, state):
                start = pl.multiple_of(j * row_count, row_count)
                pos = start + lax.broadcasted_iota(jnp.int32, (row_count, wide), 0)
                visible = (pos >= first) & (pos <= last)
                result = []
                key_grads = []
                value_grads = []
                for g in range(KV_HEADS):
                    key_piece = pairs_ref[pl.ds(start, row_count), g * HEAD : (g + 1) * HEAD]
                    value_piece = pairs_ref[
                        pl.ds(start, row_count), KV_WIDTH + g * HEAD : KV_WIDTH + (g + 1) * HEAD
                    ]
                    n = b * KV_HEADS + g
                    scores = dot_nt(key_piece, queries[g])
                    weights = jnp.where(visible, jnp.exp(scores - log_ref[n : n + 1, :]), 0.0)
                    weight_grad = dot_nt(value_piece, grads[g])
                    score_grad = (weights * (weight_grad - deltas[g])).astype(jnp.bfloat16)
                    value_grads.append(dot(weights.astype(jnp.bfloat16), grads[g]))
                    key_grads.append(dot(score_grad, queries[g]))
                    result.append(state[g] + dot_tn(key_piece, score_grad))
                pair_grad_ref[pl.ds(start, row_count), :] += jnp.concatenate(
                    key_grads + value_grads, axis=1
                )
                return tuple(result)

            state = lax.fori_loop(
                begin,
                end,
                step,
                tuple(jnp.zeros((HEAD, wide), jnp.float32) for _ in range(KV_HEADS)),
            )
            cos_part, sin_part = cos_own_ref[:, rows], sin_own_ref[:, rows]
            for g in range(KV_HEADS):
                for i in range(GROUPS):
                    part = state[g][:, i * block_len : (i + 1) * block_len]
                    top, bottom = part[:half], part[half:]
                    h = (g * GROUPS + i) * HEAD
                    query_t_ref[h : h + half, rows] = (
                        (top * cos_part + bottom * sin_part) * HEAD ** (-0.5)
                    ).astype(jnp.bfloat16)
                    query_t_ref[h + half : h + HEAD, rows] = (
                        (bottom * cos_part - top * sin_part) * HEAD ** (-0.5)
                    ).astype(jnp.bfloat16)

        query_grad_ref[...] = query_t_ref[...].T
        query_w_ref[...] = dot(query_t_ref[...], hidden_ref[0]).T.astype(jnp.bfloat16)
        chip, core = rank()
        for i in range(chips):
            for ref, to_core in ((kept_ref.at[i], core), (sent_refs[i], 1 - core)):
                block = table_ref[(chip ^ i) * 2 + to_core]
                for part, place in ((0, block), (1, 2 * slots - 1 - block)):
                    source = pl.ds(pl.multiple_of(place * block_len, block_len), block_len)
                    ref[part * block_len : (part + 1) * block_len, :] = turn_pairs(
                        pair_grad_ref[source, :], cos_ref[source, :], -sin_ref[source, :]
                    ).astype(jnp.bfloat16)

    half_shape = ((chips, row_count, 2 * KV_WIDTH), jnp.bfloat16)
    return run_kernel(
        kernel,
        [((row_count, D), jnp.bfloat16), ((D, D), jnp.bfloat16), half_shape]
        + [((row_count, 2 * KV_WIDTH), jnp.bfloat16)] * chips,
        [
            table,
            docs,
            query_rot,
            *pair_halves,
            log_total,
            attended,
            grad_attended,
            cos_all,
            sin_all,
            cos_own,
            sin_own,
            hidden_half,
        ],
        scalars=1,
        scratch=[
            pltpu.VMEM((slots * row_count, 2 * KV_WIDTH), jnp.bfloat16),
            pltpu.VMEM((slots * row_count, 2 * KV_WIDTH), jnp.float32),
            pltpu.VMEM((D, row_count), jnp.bfloat16),
        ],
        microseconds=18,
    )


def first_gradients(direct, kept, received, hidden_half, query_w, out_grad, shards):
    chips, row_count, _ = kept.shape
    rest = D - HEAD
    columns_all = 2 * KV_WIDTH + D + HEAD
    rows = D // shards

    def kernel(kept_ref, hidden_ref, query_w_ref, out_grad_ref, *refs):
        received_refs, refs = refs[:chips], refs[chips:]
        pair_refs, outs = refs[:chips], refs[chips:-1]
        mixed_ref = refs[-1]
        total = jnp.zeros((2 * KV_WIDTH, D), jnp.float32)
        for i in range(chips):
            pairs = (
                kept_ref[i].astype(jnp.float32) + received_refs[i][...].astype(jnp.float32)
            ).astype(jnp.bfloat16)
            if direct:
                for n in range(2 * KV_WIDTH // TILE):
                    pair_refs[i][n * row_count : (n + 1) * row_count, :] = pairs[
                        :, n * TILE : (n + 1) * TILE
                    ]
            else:
                pair_refs[i][...] = pairs
            total += dot_tn(pairs, hidden_ref[i])
        mixed_ref[:, : 2 * KV_WIDTH] = total.T.astype(jnp.bfloat16)
        mixed_ref[:, 2 * KV_WIDTH : 2 * KV_WIDTH + D] = query_w_ref[...]
        mixed_ref[:, 2 * KV_WIDTH + D :] = out_grad_ref[:, rest:]
        if not direct:
            outs[0][...] = mixed_ref[...]
            return
        chip, core = rank()
        for n in range(2 * chips):
            c = (chip ^ (n % chips)) * 2 + (core ^ (n // chips))
            part = mixed_ref[:, pl.ds(pl.multiple_of(c * TILE, TILE), TILE)]
            tile = out_grad_ref[:, pl.ds(pl.multiple_of((c // 2) * TILE, TILE), TILE)]
            unit = jnp.where(c % 2 == 0, tile[:, : TILE // 2], tile[:, TILE // 2 :])
            for z in range(shards):
                outs[n][z, :rows, :] = part[z * rows : (z + 1) * rows]
                middle = z * rows + rows // 2
                outs[n][z, rows:, : TILE // 2] = unit[z * rows : middle]
                outs[n][z, rows:, TILE // 2 :] = unit[middle : (z + 1) * rows]

    tiles = 2 * KV_WIDTH // TILE if direct else 1
    outs = [((row_count * tiles, 2 * KV_WIDTH // tiles), jnp.bfloat16)] * chips
    outs += (
        [((shards, rows + rows // 2, TILE), jnp.bfloat16)] * (2 * chips)
        if direct
        else [((D, columns_all), jnp.bfloat16)]
    )
    result = run_kernel(
        kernel,
        outs,
        [kept, hidden_half, query_w, out_grad, *received],
        scratch=[pltpu.VMEM((D, columns_all), jnp.bfloat16)],
        microseconds=0,
    )
    return result[:chips], result[chips:]


def local(
    layer_input,
    slot_table,
    seq_ids,
    w_query,
    w_key,
    w_value,
    w_out,
    w_gate,
    w_up,
    w_down,
    attn_gain,
    ffn_gain,
    cotangent,
):
    count = lax.axis_size("ctx")
    chips = count // 2
    index = lax.axis_index("ctx")
    chip, core = rank()
    shards = lax.axis_size("fsdp")
    rows, ff = w_gate.shape
    row_count = layer_input.shape[1]
    block_len = row_count // 2
    length = row_count * count
    direct = (
        rows % 16 == 0 and (ff // chips) % TILE == 0 and count * TILE == D + 2 * KV_WIDTH + HEAD
    )

    mixed_shard = jnp.concatenate(
        [w_key, w_value, w_query, w_out[:, D - HEAD :]], axis=1
    )
    piece = first_piece(mixed_shard, index, count)
    unit = first_piece(w_out[:, : D - HEAD], index, count)
    unit = jnp.concatenate([unit[: rows // 2], unit[rows // 2 :]], axis=1)
    gains = jnp.concatenate([attn_gain, ffn_gain])
    gains = jnp.pad(gains, (0, 16 * piece.shape[1] - 2 * rows)).reshape(16, piece.shape[1])
    tokens_low = layer_input[0]
    token_pieces = [tokens_low] + [chip_swap(tokens_low, i) for i in range(1, chips)]
    first_rows = gather_rows(jnp.concatenate([piece, unit, gains], axis=0))
    gains_all = first_rows[:, rows + rows // 2 :].reshape(shards, -1).astype(jnp.float32)
    gain_one = gains_all[:, :rows].reshape(1, D)
    gain_two = gains_all[:, rows : 2 * rows].reshape(1, D)
    hidden_half = normalize(token_pieces, gain_one)
    first_own = gather_same_core(after(first_rows, hidden_half))
    wide_own, wide_received = start_gather_rows(
        wide_piece(w_gate, w_up, chip, core, chips), first_rows
    )
    low_start = start_gather_half(after(w_down, hidden_half))
    first_pieces = first_own + [core_swap(v) for v in first_own]
    if direct:
        first = first_pieces
    else:
        ordered = in_rank_order(first_pieces)
        mixed_all = jnp.concatenate([v[:, :rows].reshape(D, -1) for v in ordered], axis=1)
        units = [
            v[:, rows : rows + rows // 2]
            .reshape(shards, rows // 2, 2, -1)
            .transpose(0, 2, 1, 3)
            .reshape(D, -1)
            for v in ordered
        ]
        first = [mixed_all, jnp.concatenate([*units, mixed_all[:, 2 * KV_WIDTH + D :]], axis=1)]

    docs = seq_ids[0].reshape(2 * count, block_len)
    own_block = lax.dynamic_index_in_dim(slot_table, index, 0, keepdims=False)
    own_blocks = jnp.stack([own_block, 2 * count - 1 - own_block])
    block_pos = own_blocks[:, None] * block_len + jnp.arange(block_len, dtype=jnp.int32)[None, :]
    half_width = after(jnp.arange(HEAD // 2, dtype=jnp.float32), hidden_half)
    frequencies = rope_base ** (-(half_width * 2.0 / HEAD))
    angles = jnp.arange(length, dtype=jnp.int32).astype(jnp.float32)[:, None] * frequencies[None, :]
    cos_all = jnp.tile(jnp.cos(angles), (1, 2 * TILE // HEAD))
    sin_all = jnp.tile(jnp.sin(angles), (1, 2 * TILE // HEAD))
    own_angles = frequencies[:, None] * block_pos.reshape(1, row_count).astype(jnp.float32)
    cos_own, sin_own = jnp.cos(own_angles), jnp.sin(own_angles)

    wide_rows = in_order(wide_own, wide_received, shards // 2)
    query_rot, own_pairs, mixed, out_w_all = project(
        direct, slot_table, after(hidden_half, wide_rows, low_start, cos_own, sin_own), first, cos_all, sin_all
    )
    pair_halves = (own_pairs, core_swap(own_pairs))
    wide_pieces = gather_same_core(wide_rows)
    low_own = finish_gather_half(after(low_start, wide_rows))
    grad_out = cotangent[0]
    attended, log_total = attention_forward(slot_table, docs, query_rot, pair_halves)
    grad_other = core_swap(after(grad_out, attended))
    residual, hidden_two = mix(attended, tokens_low, out_w_all, gain_two)
    if direct:
        wide = wide_pieces
    else:
        whole = [v.reshape(D, -1) for v in by_owner(wide_pieces, chip)]
        wide = [jnp.concatenate(whole[n : n + chips // 2], axis=1) for n in (0, chips // 2)]
    out_kept, grad_kept, sent, *wide_grads = feed_forward(
        direct,
        hidden_two,
        core_swap(hidden_two),
        grad_out,
        grad_other,
        wide,
        low_own,
        ff,
        shards,
    )
    lanes = ff // chips
    slice_rows = w_down.shape[0] // count
    pile = rows // slice_rows
    if not direct:
        gate_grad, up_grad, down_grad = wide_grads
        down_grad = down_grad.reshape(shards // 2, chips, 2, slice_rows, pile, D // pile)
        down_grad = down_grad.transpose(0, 2, 1, 4, 3, 5).reshape(shards, chips, rows, D // pile)
        wide_grads = [
            jnp.concatenate(
                [
                    lax.dynamic_slice_in_dim(
                        jnp.where(c < chips // 2, gate_grad, up_grad),
                        (c % (chips // 2)) * lanes,
                        lanes,
                        1,
                    ).reshape(shards, rows, lanes),
                    lax.dynamic_index_in_dim(down_grad, c, 1, keepdims=False),
                ],
                axis=2,
            )
            for c in (chip ^ i for i in range(chips))
        ]
    output, grad_residual, grad_attended, out_grad = unmix(
        residual,
        out_kept,
        grad_kept,
        core_swap(sent),
        grad_out,
        attended,
        out_w_all,
        gain_two,
    )

    grad_query, query_w, pairs_kept, *pairs_sent = attention_backward(
        slot_table,
        docs,
        query_rot,
        pair_halves,
        log_total,
        attended,
        grad_attended,
        cos_all,
        sin_all,
        cos_own,
        sin_own,
        hidden_half,
    )
    pairs_received = [core_swap(v) for v in pairs_sent]
    pair_sums, mixed_grads = first_gradients(
        direct, pairs_kept, pairs_received, hidden_half, query_w, out_grad, shards
    )
    if not direct:
        targets = [(chip ^ i) * 2 + (core ^ a) for a in range(2) for i in range(chips)]
        units = [
            first_piece(out_grad[:, : D - HEAD], c, count)
            .reshape(shards, 2, rows // 2, -1)
            .transpose(0, 2, 1, 3)
            .reshape(shards, rows // 2, -1)
            for c in targets
        ]
        mixed_grads = [
            jnp.concatenate(
                [first_piece(mixed_grads[0], c, count).reshape(shards, rows, -1), unit], axis=1
            )
            for c, unit in zip(targets, units)
        ]
    mixed_sums = [sum_cores(*pair) for pair in zip(mixed_grads[:chips], mixed_grads[chips:])]
    if direct:
        shape = mixed_sums[0].shape
        split = shape[0] * shape[1]
        both_sum = sum_chips(
            [
                jnp.concatenate([one.reshape(split, TILE), other], axis=0)
                for one, other in zip(mixed_sums, pair_sums)
            ]
        ).astype(jnp.bfloat16)
        first_sum = both_sum[:split].reshape(shape)
        owned = jnp.concatenate(jnp.split(both_sum[split:], 2 * KV_WIDTH // TILE), axis=1)
    else:
        first_sum = sum_chips(mixed_sums).astype(jnp.bfloat16)
        owned = sum_chips(pair_sums).astype(jnp.bfloat16)
    first_part = sum_rows(first_sum).astype(jnp.bfloat16)
    first_mine = gather_same_core(first_part)
    wide_sum = sum_chips(wide_grads, pair_sums[0]).astype(jnp.bfloat16)
    wide_sum = jnp.concatenate(
        [wide_sum[:, :, :lanes], by_core_slices(wide_sum[:, :, lanes:])], axis=2
    )
    wide_part = sum_rows(after(wide_sum, mixed_sums)).astype(jnp.bfloat16)
    wide_all = gather_chips(wide_part)
    grad_hidden_one = dot_nt(
        jnp.concatenate([owned, grad_query], axis=1), mixed[:, : 2 * KV_WIDTH + D]
    )
    tokens = tokens_low.astype(jnp.float32)
    inv_one = inverse_root(tokens)
    grad_input = (
        grad_residual + norm_back(grad_hidden_one, tokens * inv_one, inv_one, gain_one)
    ).astype(jnp.bfloat16)

    gain_rows = [v.astype(jnp.float32).reshape(1, rows) for v in (attn_gain, ffn_gain)]
    if direct:
        gate_grad, up_grad, down_grad, gain_grad_two = finish_wide(
            wide_all, w_gate, w_up, gain_rows[1], pile
        )
        down_grad = down_grad.T
        first_all = first_mine + [core_swap(v) for v in after(tuple(first_mine), gain_grad_two)]
        query_w, key_w, value_w, out_w, gain_grad_one = finish_first(
            first_all, mixed_shard, gain_rows[0]
        )
    else:
        own, other = by_owner(wide_all[:chips], chip), by_owner(wide_all[chips:], chip)
        cores = both_cores(jnp.stack(own), jnp.stack(other), core)
        down_grad = jnp.concatenate(
            [unstack_down(cores[c % 2][c // 2][:, lanes:], pile) for c in range(count)]
        ).astype(jnp.float32)
        gate_grad, up_grad = (
            jnp.concatenate(
                [cores[k][n + q][:, :lanes] for k in range(2) for q in range(chips // 2)], axis=1
            ).astype(jnp.float32)
            for n in (0, chips // 2)
        )
        ordered = in_rank_order(first_mine + [core_swap(v) for v in first_mine])
        first_grad = jnp.concatenate([v[:rows] for v in ordered], axis=1).astype(jnp.float32)
        units = [
            v[rows:].reshape(rows // 2, 2, -1).transpose(1, 0, 2).reshape(rows, -1) for v in ordered
        ]
        key_w, value_w, query_w, last = jnp.split(
            first_grad, [KV_WIDTH, 2 * KV_WIDTH, 2 * KV_WIDTH + D], axis=1
        )
        out_w = jnp.concatenate([*[v.astype(jnp.float32) for v in units], last], axis=1)
        used = 2 * KV_WIDTH + D
        gain_grad_one = (
            jnp.sum(
                first_grad[:, :used] * mixed_shard[:, :used].astype(jnp.float32),
                axis=1,
            )
            / gain_rows[0]
        )
        gain_grad_two = (
            jnp.sum(
                gate_grad * w_gate.astype(jnp.float32) + up_grad * w_up.astype(jnp.float32),
                axis=1,
            )
            / gain_rows[1]
        )
    return (
        output.T[None],
        grad_input[None],
        query_w,
        key_w,
        value_w,
        out_w,
        gate_grad,
        up_grad,
        down_grad,
        gain_grad_one.reshape(rows),
        gain_grad_two.reshape(rows),
    )


def solution(mesh):
    placed = (
        P("fsdp", "ctx", None),
        P(),
        P("fsdp", None),
        P("fsdp", None),
        P("fsdp", None),
        P("fsdp", None),
        P("fsdp", None),
        P("fsdp", None),
        P("fsdp", None),
        P("fsdp", None),
        P("fsdp"),
        P("fsdp"),
        P("fsdp", "ctx", None),
    )
    return jax.shard_map(
        local,
        mesh=mesh,
        in_specs=placed,
        out_specs=(
            P("fsdp", "ctx", None),
            P("fsdp", "ctx", None),
            P("fsdp", None),
            P("fsdp", None),
            P("fsdp", None),
            P("fsdp", None),
            P("fsdp", None),
            P("fsdp", None),
            P("fsdp", None),
            P("fsdp"),
            P("fsdp"),
        ),
        check_vma=False,
    )
```
